256 devices in a mesh: row: 16 (over x, z_lo), col: 16 (over z_hi, y, core).
Axes of the slice: x: 4, y: 4, z: 8 (z_hi: 2, z_lo: 4; z = z_hi * 4 + z_lo), core: 2. Of those that a mesh axis runs over, the one named last changes fastest.
Arguments:
- populations: float32 [19, 64, 256, 256], P(None, 'row', 'col'), may hold values from 0 to 0.5, as said below
- concentrations: float32 [2, 64, 256, 256], P(None, 'row', 'col'), may hold values from 0.5 to 1.5
- solid_mask: int32 [64, 256, 256], P('row', 'col'), may hold values 0 or 1
- charge_sites: int32 [64, 256, 256], P('row', 'col'), may hold values from 0 to 2
Outputs:
- next_populations: float32 [19, 64, 256, 256], P(None, 'row', 'col')
- next_concentrations: float32 [2, 64, 256, 256], P(None, 'row', 'col')
The draws below stay inside these ranges and needn't reach their ends.
Inputs may be any that keep to these rules, and one draw needn't show every extreme that they name: `populations`: each population is its lattice weight w_i times a factor between 0.65 and 1.35.
All inputs are finite; a program needn't handle non-finite values. No bound on the sum of `solid_mask` on one device may be relied on, other than what follows from the above.
Results may differ from the reference program's by a relative error of at most 0.0001.
Values sent between devices are 32-bit elements; how exact they have to be, the bound alone decides.
A program may use at most 64 MiB of HBM per device.

```python
import math
import jax
import jax.numpy as jnp
import numpy as np
from jax import lax

NZ = 256
DEBYE = 32
NX = 64
NY = 256


def draw_populations(key, part):
    key = jax.random.fold_in(key, 11)
    weights = jnp.array([1.0 / 3.0] + [1.0 / 18.0] * 6 + [1.0 / 36.0] * 12, jnp.float32).reshape(19, 1, 1, 1)
    factor = jax.random.uniform(key, (19, NX, NY, NZ), jnp.float32, 0.65, 1.35)
    return factor * weights


def with_ends(values, key, least, top_value):
    longest = values.shape.index(max(values.shape))
    spots = []
    for shift in (0, 1):
        where = [jax.random.randint(jax.random.fold_in(key, axis), (), 0, length) for axis, length in enumerate(values.shape)]
        where[longest] = (where[longest] + shift) % values.shape[longest]
        spots.append(tuple(where))
    return values.at[spots[0]].set(least).at[spots[1]].set(top_value)


def levels(stream_key, shape, split, smallest, high):
    loudness, own = 1.0, jax.random.fold_in(stream_key, 6)
    for axis_at, parts in split:
        draws = jnp.exp(jax.random.uniform(jax.random.fold_in(own, axis_at), (parts,), jnp.float32, smallest / len(split), high / len(split)))
        loudness = loudness * jnp.repeat(draws, shape[axis_at] // parts).reshape([-1 if axis == axis_at else 1 for axis in range(len(shape))])
    return loudness


def setup_inputs(seed: int = 0) -> dict:
    arg_keys = jax.random.split(jax.random.key(seed), 5)
    return {
        "populations": draw_populations(jax.random.fold_in(arg_keys[4], 71), 0),
        "concentrations": jnp.clip(0.5 + 1.0 * jax.random.uniform(arg_keys[1], (2, NX, NY, NZ), jnp.float32) ** levels(arg_keys[1], (2, NX, NY, NZ), ((1, 16), (2, 16)), -0.2, 0.2), 0.5, 1.5),
        "solid_mask": with_ends((jax.random.randint(arg_keys[2], (NX, NY, NZ), 0, 8) < 1).astype(jnp.int32), jax.random.fold_in(arg_keys[2], 1), 0, 1),
        "charge_sites": with_ends(jax.random.randint(arg_keys[3], (NX, NY, NZ), 0, 3), jax.random.fold_in(arg_keys[3], 1), 0, 2).astype(jnp.int32),
    }


lattice_velocity = np.array([[0, 0, 0], [1, 0, 0], [-1, 0, 0], [0, 1, 0], [0, -1, 0], [0, 0, 1], [0, 0, -1], [1, 1, 0], [-1, -1, 0], [1, -1, 0], [-1, 1, 0], [1, 0, 1], [-1, 0, -1], [1, 0, -1], [-1, 0, 1], [0, 1, 1], [0, -1, -1], [0, 1, -1], [0, -1, 1]])
opposite_dir = [0, 2, 1, 4, 3, 6, 5, 8, 7, 10, 9, 12, 11, 14, 13, 16, 15, 18, 17]
lattice_weight = [1.0 / 3.0] + [1.0 / 18.0] * 6 + [1.0 / 36.0] * 12
site_charge = 1.5
valences = (1.0, -1.0)
diffusivities = (0.12, 0.08)
highest = lax.Precision.HIGHEST


def moment_tables():
    table = jnp.asarray(lattice_velocity, jnp.float32)
    vel_x = table[:, 0]
    vel_y = table[:, 1]
    vel_z = table[:, 2]
    speed_square = vel_x * vel_x + vel_y * vel_y + vel_z * vel_z
    polynomials = [jnp.ones((19,), jnp.float32), 19.0 * speed_square - 30.0, (21.0 * speed_square * speed_square - 53.0 * speed_square + 24.0) / 2.0, vel_x, (5.0 * speed_square - 9.0) * vel_x, vel_y, (5.0 * speed_square - 9.0) * vel_y, vel_z, (5.0 * speed_square - 9.0) * vel_z, 3.0 * vel_x * vel_x - speed_square, (3.0 * speed_square - 5.0) * (3.0 * vel_x * vel_x - speed_square), vel_y * vel_y - vel_z * vel_z, (3.0 * speed_square - 5.0) * (vel_y * vel_y - vel_z * vel_z), vel_x * vel_y, vel_y * vel_z, vel_x * vel_z, (vel_y * vel_y - vel_z * vel_z) * vel_x, (vel_z * vel_z - vel_x * vel_x) * vel_y, (vel_x * vel_x - vel_y * vel_y) * vel_z]
    moments = jnp.stack(polynomials)
    norms = jnp.sum(moments * moments, axis=1)
    viscous = 1.25
    relax_rates = jnp.array([0.0, 1.19, 1.4, 0.0, 1.2, 0.0, 1.2, 0.0, 1.2, viscous, 1.4, viscous, 1.4, viscous, viscous, viscous, 1.98, 1.98, 1.98], jnp.float32)
    inverse = jnp.transpose(moments) / norms[None, :]
    relaxation = jnp.dot(inverse * relax_rates[None, :], moments, precision=highest)
    source = jnp.dot(inverse * (1.0 - relax_rates / 2.0)[None, :], moments, precision=highest)
    return relaxation, source


def face_flux(conc_low, conc_high, drift_low, drift_high, pot_low, pot_high):
    valence = jnp.array(valences, jnp.float32).reshape(2, 1, 1, 1)
    spread = jnp.array(diffusivities, jnp.float32).reshape(2, 1, 1, 1)
    summed = conc_low + conc_high
    return 0.25 * (drift_low + drift_high) * summed - spread * ((conc_high - conc_low) + valence * 0.5 * summed * (pot_high - pot_low))


def collide(cell_block, density, momentum, body_force, solid_flag):
    relaxation, source = moment_tables()
    velocity_table = jnp.asarray(lattice_velocity, jnp.float32)
    trailing = (1,) * (cell_block.ndim - 1)
    weights = jnp.asarray(lattice_weight, jnp.float32).reshape((19,) + trailing)
    velocity = (momentum + 0.5 * body_force) / density
    projected = jnp.tensordot(velocity_table, velocity, axes=1, precision=highest)
    speed_square = jnp.sum(velocity * velocity, axis=0)
    equilibrium = weights * density * (1.0 + 3.0 * projected + 4.5 * projected * projected - 1.5 * speed_square)
    pushed = jnp.tensordot(velocity_table, body_force, axes=1, precision=highest)
    aligned = jnp.sum(velocity * body_force, axis=0)
    forcing = weights * (3.0 * (pushed - aligned) + 9.0 * projected * pushed)
    relaxed = jnp.tensordot(relaxation, cell_block - equilibrium, axes=1, precision=highest)
    driven = jnp.tensordot(source, forcing, axes=1, precision=highest)
    collided = cell_block - relaxed + driven
    bounced = jnp.stack([cell_block[member] for member in opposite_dir])
    return jnp.where(solid_flag[None], bounced, collided)


def line_eigen(indices, length):
    angles = indices.astype(jnp.float32) * jnp.float32(2.0 * math.pi / length)
    return 2.0 - 2.0 * jnp.cos(angles)


def take_planes(array_in, offset, planes, axis_dim):
    return lax.dynamic_slice_in_dim(array_in, offset, planes, axis_dim)


def reference(populations, concentrations, solid_mask, charge_sites):
    openness = 1.0 - solid_mask.astype(jnp.float32)
    velocity_table = jnp.asarray(lattice_velocity, jnp.float32)
    density = jnp.sum(populations, axis=0)
    momentum = jnp.tensordot(velocity_table.T, populations, axes=1, precision=highest)
    bare_velocity = momentum / density
    free_charge = (concentrations[0] - concentrations[1]) * openness
    fixed_charge = site_charge * ((charge_sites == 1).astype(jnp.float32) - (charge_sites == 2).astype(jnp.float32))
    charge = free_charge + fixed_charge
    spectrum = jnp.fft.fftn(charge)
    eigenvalues = (line_eigen(jnp.arange(NX, dtype=jnp.int32), NX)[:, None, None]
                   + line_eigen(jnp.arange(NY, dtype=jnp.int32), NY)[None, :, None]
                   + line_eigen(jnp.arange(NZ, dtype=jnp.int32), NZ)[None, None, :]
                   + 1.0 / (DEBYE * DEBYE))
    potential = jnp.real(jnp.fft.ifftn(spectrum / eigenvalues)).astype(jnp.float32)
    flux_x = face_flux(concentrations, jnp.roll(concentrations, -1, 1), bare_velocity[0], jnp.roll(bare_velocity[0], -1, 0), potential, jnp.roll(potential, -1, 0))
    flux_y = face_flux(concentrations, jnp.roll(concentrations, -1, 2), bare_velocity[1], jnp.roll(bare_velocity[1], -1, 1), potential, jnp.roll(potential, -1, 1))
    flux_z = face_flux(concentrations, jnp.roll(concentrations, -1, 3), bare_velocity[2], jnp.roll(bare_velocity[2], -1, 2), potential, jnp.roll(potential, -1, 2))
    change = (flux_x - jnp.roll(flux_x, 1, 1)) + (flux_y - jnp.roll(flux_y, 1, 2)) + (flux_z - jnp.roll(flux_z, 1, 3))
    next_concentrations = openness * (concentrations - change)
    electric = -0.5 * jnp.stack([jnp.roll(potential, -1, 0) - jnp.roll(potential, 1, 0),
                                 jnp.roll(potential, -1, 1) - jnp.roll(potential, 1, 1),
                                 jnp.roll(potential, -1, 2) - jnp.roll(potential, 1, 2)])
    body_force = free_charge[None] * electric
    solid_flag = solid_mask == 1
    planes = math.gcd(NX, 16)

    def collide_block(block_step, buffer):
        offset = (block_step * planes).astype(jnp.int32)
        collided = collide(take_planes(populations, offset, planes, 1), take_planes(density, offset, planes, 0),
                           take_planes(momentum, offset, planes, 1), take_planes(body_force, offset, planes, 1),
                           take_planes(solid_flag, offset, planes, 0))
        return lax.dynamic_update_slice_in_dim(buffer, collided, offset, 1)

    collided_all = lax.fori_loop(0, NX // planes, collide_block, jnp.zeros_like(populations))
    next_populations = jnp.stack([jnp.roll(collided_all[member], (int(lattice_velocity[member, 0]), int(lattice_velocity[member, 1]), int(lattice_velocity[member, 2])), (0, 1, 2)) for member in range(19)])
    return next_populations, next_concentrations
```

```python
import functools
import math

import jax
import jax.numpy as jnp
import numpy as np
from jax import lax
from jax.experimental import pallas as pl
from jax.experimental.pallas import tpu as pltpu
from jax.sharding import PartitionSpec as P

DEBYE = 32
SCREEN = 1.0 / (DEBYE * DEBYE)
MESH = pl.DeviceIdType.MESH
HIGHEST = lax.Precision.HIGHEST
f32 = jnp.float32

VELOCITY = np.array(
    [[0, 0, 0], [1, 0, 0], [-1, 0, 0], [0, 1, 0], [0, -1, 0], [0, 0, 1], [0, 0, -1],
     [1, 1, 0], [-1, -1, 0], [1, -1, 0], [-1, 1, 0], [1, 0, 1], [-1, 0, -1], [1, 0, -1],
     [-1, 0, 1], [0, 1, 1], [0, -1, -1], [0, 1, -1], [0, -1, 1]]
)
OPPOSITE = [0, 2, 1, 4, 3, 6, 5, 8, 7, 10, 9, 12, 11, 14, 13, 16, 15, 18, 17]
WEIGHT = np.array([1.0 / 3.0] + [1.0 / 18.0] * 6 + [1.0 / 36.0] * 12)
SITE_CHARGE = 1.5
DIFFUSIVITY = (0.12, 0.08)
VALENCE = (1.0, -1.0)

MINUS_X = [2, 8, 10, 12, 14]
PLUS_X = [1, 7, 9, 11, 13]
REST = [0, 3, 4, 5, 6, 15, 16, 17, 18]
SLOT = {d: i for i, d in enumerate(MINUS_X)}
SLOT.update({d: 13 + i for i, d in enumerate(PLUS_X)})
SLOT.update({d: 18 + i for i, d in enumerate(REST)})
AUX = 5
N_AUX = 8
N_FIELD = 27
N_SEND = 13
Y_LOW = [7, 10, 3, 15, 17]
Y_HIGH = [9, 8, 4, 16, 18]


def collision_matrices():
    v = VELOCITY.astype(np.float64)
    x, y, z = v[:, 0], v[:, 1], v[:, 2]
    q = x * x + y * y + z * z
    rows = [
        np.ones(19), 19 * q - 30, (21 * q * q - 53 * q + 24) / 2,
        x, (5 * q - 9) * x, y, (5 * q - 9) * y, z, (5 * q - 9) * z,
        3 * x * x - q, (3 * q - 5) * (3 * x * x - q), y * y - z * z, (3 * q - 5) * (y * y - z * z),
        x * y, y * z, x * z, (y * y - z * z) * x, (z * z - x * x) * y, (x * x - y * y) * z,
    ]
    m = np.stack(rows)
    rates = np.array([0, 1.19, 1.4, 0, 1.2, 0, 1.2, 0, 1.2, 1.25, 1.4, 1.25, 1.4, 1.25, 1.25, 1.25, 1.98, 1.98, 1.98])
    inverse = m.T / np.sum(m * m, axis=1)[None, :]
    return (inverse * rates) @ m, (inverse * (1 - rates / 2)) @ m


K, G = collision_matrices()


def even_vector(f0=0.0, axis=(0, 0, 0), plane=(0, 0, 0)):
    out = np.zeros(19)
    out[0] = f0
    for i in range(1, 19):
        c = VELOCITY[i]
        if np.abs(c).sum() == 1:
            out[i] = axis[int(np.argmax(np.abs(c)))]
        else:
            out[i] = plane[int(np.argmin(np.abs(c)))]
    return out


def relax_coefficients():
    left = np.eye(19) - K
    r0 = left @ even_vector(f0=1.0)
    ra = left @ even_vector(axis=(0.5, 0, 0))
    rp = left @ even_vector(plane=(0.25, 0, 0))
    x_axis, y_axis, yz, xy = 1, 3, 15, 7
    even = {
        "rest": (r0[0], ra[0], rp[0]),
        "axis": (r0[x_axis], ra[y_axis], rp[y_axis], ra[x_axis] - ra[y_axis], rp[x_axis] - rp[y_axis]),
        "plane": (r0[xy], ra[xy], rp[xy], ra[yz] - ra[xy], rp[yz] - rp[xy]),
    }
    h = np.zeros(19)
    h[[7, 8]], h[[9, 10]] = 0.25, -0.25
    even["shear"] = (left @ h)[7]
    d = np.zeros(19)
    d[1], d[2] = 0.5, -0.5
    od = left @ d
    e = np.zeros(19)
    e[[7, 9]], e[[8, 10]] = 0.25, -0.25
    oe = left @ e
    odd = {"axis": (od[1], oe[1]), "plane": (od[7], oe[7], oe[11])}
    return even, odd


def force_coefficients():
    c = VELOCITY.astype(np.float64)

    def quad(t):
        return WEIGHT * (4.5 * np.einsum("ia,ab,ib->i", c, t, c) - 1.5 * np.trace(t))

    t = np.zeros((3, 3))
    t[0, 0] = 1.0
    qa, qb = K @ quad(t), G @ quad(t)
    qr = K @ WEIGHT
    s = np.zeros((3, 3))
    s[0, 1] = s[1, 0] = 1.0
    sa, sb = K @ quad(s), G @ quad(s)
    lj = K @ (WEIGHT * 3 * c[:, 0])
    lf = G @ (WEIGHT * 3 * c[:, 0])
    return {
        "rest": (qa[0], qb[0], qr[0]),
        "axis_trace": (qa[3], qb[3], qr[3]),
        "axis": (qa[1] - qa[3], qb[1] - qb[3]),
        "plane_trace": (qa[7], qb[7], qr[7]),
        "plane": (qa[15] - qa[7], qb[15] - qb[7]),
        "shear": (sa[7], sb[7]),
        "odd_axis": (lj[1], lf[1]),
        "odd_plane": (lj[7], lf[7]),
    }


EVEN, ODD = relax_coefficients()
FORCE = force_coefficients()
PLANES = {0: (15, 17, 1, 2), 1: (11, 13, 0, 2), 2: (7, 9, 0, 1)}


def fl(v):
    return np.float32(v)


def moments_of(f):
    pair = {i: f[i] + f[i + 1] for i in range(1, 19, 2)}
    diff = {i: f[i] - f[i + 1] for i in range(1, 19, 2)}
    s = [pair[1], pair[3], pair[5]]
    g = [pair[15] + pair[17], pair[11] + pair[13], pair[7] + pair[9]]
    ts, tg = s[0] + s[1] + s[2], g[0] + g[1] + g[2]
    density = f[0] + ts + tg
    first = {p: diff[PLANES[p][0]] + diff[PLANES[p][1]] for p in range(3)}
    second = {p: diff[PLANES[p][0]] - diff[PLANES[p][1]] for p in range(3)}
    d = [diff[1], diff[3], diff[5]]
    along = [(first[2], first[1]), (second[2], first[0]), (second[1], second[0])]
    momentum = [d[a] + along[a][0] + along[a][1] for a in range(3)]
    return pair, s, g, ts, tg, density, d, along, momentum


def relaxed(f, moments):
    pair, s, g, ts, tg, _, d, along, _ = moments
    e = EVEN
    out = [None] * 19
    out[0] = fl(e["rest"][0]) * f[0] + fl(e["rest"][1]) * ts + fl(e["rest"][2]) * tg
    ca = fl(e["axis"][0]) * f[0] + fl(e["axis"][1]) * ts + fl(e["axis"][2]) * tg
    cp = fl(e["plane"][0]) * f[0] + fl(e["plane"][1]) * ts + fl(e["plane"][2]) * tg
    odd_axis, odd_plane = [], []
    for a in range(3):
        u, w = along[a]
        odd_axis.append(fl(ODD["axis"][0]) * d[a] + fl(ODD["axis"][1]) * (u + w))
        b = fl(ODD["plane"][0]) * d[a]
        odd_plane.append(
            (b + fl(ODD["plane"][1]) * u + fl(ODD["plane"][2]) * w, b + fl(ODD["plane"][1]) * w + fl(ODD["plane"][2]) * u)
        )
    for a in range(3):
        even = ca + fl(e["axis"][3]) * s[a] + fl(e["axis"][4]) * g[a]
        out[1 + 2 * a] = even + odd_axis[a]
        out[2 + 2 * a] = even - odd_axis[a]
    parts = {
        2: (odd_plane[0][0], odd_plane[1][0]),
        1: (odd_plane[0][1], odd_plane[2][0]),
        0: (odd_plane[1][1], odd_plane[2][1]),
    }
    for p in range(3):
        i, j, _, _ = PLANES[p]
        even = cp + fl(e["plane"][3]) * s[p] + fl(e["plane"][4]) * g[p]
        shear = fl(e["shear"]) * (pair[i] - pair[j])
        u, w = parts[p]
        out[i], out[i + 1] = even + shear + (u + w), even + shear - (u + w)
        out[j], out[j + 1] = even - shear + (u - w), even - shear - (u - w)
    return out


def force_part(density, momentum, force, inverse, wanted):
    k = FORCE
    j = [momentum[a] + 0.5 * force[a] for a in range(3)]
    u = [j[a] * inverse for a in range(3)]
    aa = [j[a] * u[a] for a in range(3)]
    bb = [2.0 * (u[a] * force[a]) for a in range(3)]
    ta, tb = aa[0] + aa[1] + aa[2], bb[0] + bb[1] + bb[2]
    out = {}
    if 0 in wanted:
        out[0] = fl(k["rest"][0]) * ta + fl(k["rest"][1]) * tb + fl(k["rest"][2]) * density
    axis_common = fl(k["axis_trace"][0]) * ta + fl(k["axis_trace"][1]) * tb + fl(k["axis_trace"][2]) * density
    plane_common = fl(k["plane_trace"][0]) * ta + fl(k["plane_trace"][1]) * tb + fl(k["plane_trace"][2]) * density
    odd_plane = [fl(k["odd_plane"][0]) * j[a] + fl(k["odd_plane"][1]) * force[a] for a in range(3)]
    for a in range(3):
        ids = (1 + 2 * a, 2 + 2 * a)
        if not any(i in wanted for i in ids):
            continue
        even = axis_common + fl(k["axis"][0]) * aa[a] + fl(k["axis"][1]) * bb[a]
        odd = fl(k["odd_axis"][0]) * j[a] + fl(k["odd_axis"][1]) * force[a]
        if ids[0] in wanted:
            out[ids[0]] = even + odd
        if ids[1] in wanted:
            out[ids[1]] = even - odd
    for p in range(3):
        i1, i2, a, b = PLANES[p]
        if not any(i in wanted for i in (i1, i1 + 1, i2, i2 + 1)):
            continue
        even = plane_common + fl(k["plane"][0]) * aa[p] + fl(k["plane"][1]) * bb[p]
        shear = fl(k["shear"][0]) * (j[a] * u[b]) + fl(k["shear"][1]) * (u[a] * force[b] + u[b] * force[a])
        up, down = even + shear, even - shear
        total, apart = odd_plane[a] + odd_plane[b], odd_plane[a] - odd_plane[b]
        for i, v in ((i1, (up, total)), (i2, (down, apart))):
            if i in wanted:
                out[i] = v[0] + v[1]
            if i + 1 in wanted:
                out[i + 1] = v[0] - v[1]
    return out


def cas(rows, columns, length):
    angle = 2 * np.pi * (np.outer(rows, columns) % length) / length
    return (np.cos(angle) + np.sin(angle)).astype(np.float32)


def eigen(length):
    return 2.0 - 2.0 * np.cos(2 * np.pi * np.arange(length) / length)


def tables(nx, ny, nz):
    r = np.array([x * 4 + zl for zl in range(4) for x in range(4)])
    own_rows = np.concatenate([4 * r + xi for xi in range(4)])
    ext_rows = np.concatenate([4 * r + xx for xx in range(-1, 5)])
    c = np.arange(16)
    low = np.stack([16 * c - 1] * 6 + [16 * c - 2] * 2, axis=1).reshape(-1)
    high = np.stack([16 * c + 16] * 6 + [16 * c + 17] * 2, axis=1).reshape(-1)
    return {
        "hz": cas(np.arange(nz), np.arange(nz), nz),
        "hx": cas(np.arange(nx), own_rows % nx, nx),
        "hx_ext": cas(ext_rows % nx, np.arange(nx), nx),
        "hy_ext": cas(np.arange(ny), np.concatenate([np.arange(ny), low % ny, high % ny]), ny),
        "eig_xy": (eigen(nx)[:, None] + eigen(ny)[None, :] + SCREEN).astype(np.float32),
        "eig_z": np.broadcast_to(eigen(nz).astype(np.float32)[:, None], (nz, 128)).copy(),
    }


def near(d):
    return min(d, 4 - d)


STEPS = sorted(
    [(dx, dy, dk) for dx in range(4) for dy in range(4) for dk in range(2)],
    key=lambda t: -(near(t[0]) + near(t[1])) * 10 - t[2],
)


def dot(a, b, contract=((1,), (0,))):
    return lax.dot_general(a, b, (contract, ((), ())), precision=HIGHEST, preferred_element_type=f32)


def solve_kernel(
    pops_hbm, conc_hbm, solid_hbm, sites_hbm, hz_ref, hx_ref, hxe_ref, hye_ref, exy_ref, ez_ref,
    pot_ref, field, xr, yr,
    pops, conc, solid, sites, sa, ra, rb, grid, sp, rp, ys, sems, in_sems,
):
    row, col = lax.axis_index("row"), lax.axis_index("col")
    x, zl = row // 4, lax.rem(row, 4)
    zh, y, k = col // 8, lax.rem(col // 2, 4), lax.rem(col, 2)
    z = zh * 4 + zl
    plane = y * 4 + x
    depth = z * 2 + k
    mode = plane * 16 + depth

    loads = [
        pltpu.make_async_copy(conc_hbm, conc, in_sems.at[0]),
        pltpu.make_async_copy(solid_hbm, solid, in_sems.at[1]),
        pltpu.make_async_copy(sites_hbm, sites, in_sems.at[2]),
        pltpu.make_async_copy(pops_hbm, pops, in_sems.at[3]),
    ]
    for c in loads:
        c.start()

    barrier = pltpu.get_barrier_semaphore()
    xs = [lax.rem(x + d, 4) for d in range(4)]
    yy = [lax.rem(y + d, 4) for d in range(4)]
    plane_peers = [(dx, dy) for dx in range(4) for dy in range(4) if (dx, dy) != (0, 0)]
    plane_peers.sort(key=lambda t: -(near(t[0]) + near(t[1])))
    depth_peers = [(dz, dk) for dz in (4, 3, 5, 2, 6, 1, 7, 0) for dk in (1, 0) if (dz, dk) != (0, 0)]
    row_up, row_down = lax.rem(row + 1, 16), lax.rem(row + 15, 16)
    col_up, col_down = lax.rem(col + 1, 16), lax.rem(col + 15, 16)

    def plane_id(dx, dy):
        return {"row": xs[dx] * 4 + zl, "col": zh * 8 + yy[dy] * 2 + k}

    def depth_pos(dz, dk):
        return lax.rem(z + dz, 8), (k if dk == 0 else 1 - k)

    def depth_id(dz, dk):
        zz, kk = depth_pos(dz, dk)
        return {"row": x * 4 + lax.rem(zz, 4), "col": (zz // 4) * 8 + y * 2 + kk}

    ids = [plane_id(*t) for t in plane_peers] + [depth_id(*t) for t in depth_peers]
    ids += [{"row": row_up, "col": col}, {"row": row_down, "col": col}, {"row": row, "col": col_up}, {"row": row, "col": col_down}]
    for device in ids:
        pl.semaphore_signal(barrier, inc=1, device_id=device, device_id_type=MESH)

    for c in loads[:3]:
        c.wait()
    open_all = 1.0 - solid[...].astype(f32)
    kinds = sites[...]
    fixed = SITE_CHARGE * ((kinds == 1).astype(f32) - (kinds == 2).astype(f32))
    charge = (conc[0] - conc[1]) * open_all + fixed
    field[AUX + 4] = conc[0]
    field[AUX + 5] = conc[1]
    field[AUX + 6] = open_all
    field[AUX + 7] = charge
    flat = charge.reshape(64, 256)
    spectrum = dot(hz_ref[...], jnp.concatenate([flat, jnp.zeros((64, 256), f32)], axis=0), ((1,), (1,)))
    sa.reshape(256, 128)[...] = spectrum

    pl.semaphore_wait(barrier, len(ids))
    for t in plane_peers:
        other = yy[t[1]] * 4 + xs[t[0]]
        pltpu.make_async_remote_copy(
            sa.at[pl.ds(other * 16, 16)], ra.at[y, x], sems.at[0], sems.at[1], device_id=plane_id(*t), device_id_type=MESH
        ).start()
    keep = pltpu.make_async_copy(sa.at[pl.ds(plane * 16, 16)], ra.at[y, x], in_sems.at[4])
    keep.start()

    loads[3].wait()

    def before(i, carry):
        xx, part = i // 2, pl.multiple_of(lax.rem(i, 2) * 8, 8)
        rows = pl.ds(part, 8)
        f = [pops[d, xx, rows, :] for d in range(19)]
        moments = moments_of(f)
        field[AUX, xx, rows, :] = moments[5]
        for a in range(3):
            field[AUX + 1 + a, xx, rows, :] = moments[8][a]
        wall = solid[xx, rows, :] == 1
        base = relaxed(f, moments)
        for d in range(19):
            field[SLOT[d], xx, rows, :] = jnp.where(wall, f[OPPOSITE[d]], base[d])
        return carry

    lax.fori_loop(0, 8, before, 0)
    to_up = pltpu.make_async_remote_copy(
        field.at[pl.ds(AUX, N_SEND), 3], xr.at[0], sems.at[2], sems.at[3], device_id={"row": row_up, "col": col}, device_id_type=MESH
    )
    to_down = pltpu.make_async_remote_copy(
        field.at[pl.ds(0, N_SEND), 0], xr.at[1], sems.at[4], sems.at[5], device_id={"row": row_down, "col": col}, device_id_type=MESH
    )
    to_up.start()
    to_down.start()

    keep.wait()
    blocks = sa.at[pl.ds(0, 240)]
    pltpu.make_async_copy(blocks, blocks, sems.at[1]).wait()
    for t in depth_peers:
        zz, kk = depth_pos(*t)
        pltpu.make_async_remote_copy(
            ra.at[:, :, zz * 2 + kk], rb.at[zh, :, k, pl.ds(zl * 4, 4)], sems.at[6], sems.at[7],
            device_id=depth_id(*t), device_id_type=MESH,
        ).start()
    keep = pltpu.make_async_copy(ra.at[:, :, depth], rb.at[zh, :, k, pl.ds(zl * 4, 4)], in_sems.at[4])
    keep.start()

    to_up.wait_recv()
    to_down.wait_recv()
    line = lax.broadcasted_iota(jnp.int32, (8, 256), 0)
    for side, (edge, dirs, low_dir, high_dir) in enumerate(((15, Y_LOW, 7, 10), (0, Y_HIGH, 9, 8))):
        for n in range(N_SEND):
            slot = SLOT[dirs[n]] if n < 5 else AUX + n - 5
            value = jnp.zeros((8, 256), f32)
            for xx in range(4):
                value = jnp.where(line == xx + 1, field[slot, xx, edge : edge + 1, :], value)
            if n >= 5 or dirs[n] == low_dir:
                value = jnp.where(line == 0, xr[0, slot - AUX, edge : edge + 1, :], value)
            if n >= 5 or dirs[n] == high_dir:
                value = jnp.where(line == 5, xr[1, slot, edge : edge + 1, :], value)
            ys[side, n] = value
    y_up = pltpu.make_async_remote_copy(
        ys.at[0], yr.at[0], sems.at[8], sems.at[9], device_id={"row": row, "col": col_up}, device_id_type=MESH
    )
    y_down = pltpu.make_async_remote_copy(
        ys.at[1], yr.at[1], sems.at[10], sems.at[11], device_id={"row": row, "col": col_down}, device_id_type=MESH
    )
    y_up.start()
    y_down.start()
    scale = 1.0 / ((exy_ref[...] + jnp.concatenate([ez_ref[pl.ds(mode, 1), :]] * 2, axis=1)) * float(64 * 256 * 256))
    keep.wait()
    pltpu.make_async_copy(blocks, blocks, sems.at[7]).wait()

    lane = lax.broadcasted_iota(jnp.int32, (16, 128), 1)
    sixteenth = lane // 16
    eighth = lane // 8
    in_eighth = lax.rem(lane, 8)
    arrived = rb.reshape(256, 128)
    for half in range(2):
        pieces = [arrived[(8 * half + j) * 16 : (8 * half + j + 1) * 16, :] for j in range(8)]
        for xi in range(4):
            acc = None
            for j in range(8):
                shift = (j - xi) * 16 % 128
                w = pltpu.roll(pieces[j], shift, 1) if shift else pieces[j]
                acc = w if acc is None else jnp.where(sixteenth == j, w, acc)
            grid[xi * 16 : (xi + 1) * 16, half * 128 : (half + 1) * 128] = acc
    g = dot(dot(hx_ref[...], grid[...]), hz_ref[...]) * scale
    out = dot(dot(hxe_ref[...], g), hye_ref[...])
    sides = []
    for base in (256, 384):
        merged = out[0:16, base : base + 128]
        for j in range(1, 8):
            r = {6: 0, 7: 5}.get(j, j)
            merged = jnp.where(in_eighth == j, out[r * 16 : (r + 1) * 16, base : base + 128], merged)
        sides.append(merged)
    send = sp.reshape(256, 128)
    for c in range(16):
        acc = None
        for xx in range(6):
            v = out[xx * 16 : (xx + 1) * 16, (c // 8) * 128 : (c // 8 + 1) * 128]
            shift = (xx - c % 8) * 16 % 128
            w = pltpu.roll(v, shift, 1) if shift else v
            acc = w if acc is None else jnp.where(sixteenth == xx, w, acc)
        for s in range(2):
            shift = (96 + 8 * s - 8 * c) % 128
            w = pltpu.roll(sides[s], shift, 1) if shift else sides[s]
            acc = jnp.where(eighth == 12 + s, w, acc)
        send[c * 16 : (c + 1) * 16, :] = acc

    ks = [k, 1 - k]

    def to_all(i, last):
        dz = 4 + (1 - 2 * lax.rem(i, 2)) * ((i + 1) // 2)
        zz = lax.rem(z + dz, 8)
        zr, zc = lax.rem(zz, 4), (zz // 4) * 8
        for dx, dy, dk in STEPS:
            if last and (dx, dy, dk) == (0, 0, 0):
                continue
            c = zc + yy[dy] * 2 + ks[dk]
            pltpu.make_async_remote_copy(
                sp.at[c * 16 + zr * 4 + xs[dx]], rp.at[mode], sems.at[12], sems.at[13],
                device_id={"row": xs[dx] * 4 + zr, "col": c}, device_id_type=MESH,
            ).start()

    def step(i, carry):
        to_all(i, False)
        return carry

    lax.fori_loop(0, 7, step, 0)
    to_all(7, True)
    keep = pltpu.make_async_copy(sp.at[col * 16 + zl * 4 + x], rp.at[mode], in_sems.at[4])
    keep.start()
    y_up.wait_recv()
    y_down.wait_recv()
    keep.wait()
    most = rp.at[pl.ds(0, 255)]
    pltpu.make_async_copy(most, most, sems.at[13]).wait()
    pot_ref[...] = dot(rp.reshape(256, 128)[...], hz_ref[...], ((0,), (0,)))

    pltpu.make_async_copy(blocks, blocks, sems.at[0]).wait()
    pltpu.make_async_copy(blocks, blocks, sems.at[6]).wait()
    pltpu.make_async_copy(most, most, sems.at[12]).wait()
    for c in (to_up, to_down, y_up, y_down):
        c.wait_send()


def solve(populations, concentrations, solid_mask, charge_sites):
    t = tables(64, 256, 256)
    vmem = pl.BlockSpec(memory_space=pltpu.VMEM)
    hbm = pl.BlockSpec(memory_space=pl.ANY)
    return pl.pallas_call(
        solve_kernel,
        out_shape=(
            jax.ShapeDtypeStruct((128, 256), f32),
            jax.ShapeDtypeStruct((N_FIELD, 4, 16, 256), f32),
            jax.ShapeDtypeStruct((2, N_SEND, 16, 256), f32),
            jax.ShapeDtypeStruct((2, N_SEND, 8, 256), f32),
        ),
        in_specs=[hbm] * 4 + [vmem] * 6,
        out_specs=(vmem,) * 4,
        scratch_shapes=[
            pltpu.VMEM((19, 4, 16, 256), f32),
            pltpu.VMEM((2, 4, 16, 256), f32),
            pltpu.VMEM((4, 16, 256), jnp.int32),
            pltpu.VMEM((4, 16, 256), jnp.int32),
            pltpu.VMEM((256, 1, 128), f32),
            pltpu.VMEM((4, 4, 16, 1, 128), f32),
            pltpu.VMEM((2, 4, 2, 16, 1, 128), f32),
            pltpu.VMEM((64, 256), f32),
            pltpu.VMEM((256, 1, 128), f32),
            pltpu.VMEM((256, 1, 128), f32),
            pltpu.VMEM((2, N_SEND, 8, 256), f32),
            pltpu.SemaphoreType.DMA((14,)),
            pltpu.SemaphoreType.DMA((5,)),
        ],
        compiler_params=pltpu.CompilerParams(collective_id=0, has_side_effects=True, vmem_limit_bytes=VMEM_A),
    )(
        populations, concentrations, solid_mask, charge_sites,
        *[jnp.asarray(t[n]) for n in ("hz", "hx", "hx_ext", "hy_ext", "eig_xy", "eig_z")],
    )


VMEM_A = 32 * 2**20
VMEM_B = 24 * 2**20


def roll_z(v, shift):
    return pltpu.roll(v, shift % 256, 1)


def step_kernel(pot, field, xr, yr, out_hbm, conc_hbm, out, conc_out, sems):
    line16 = lax.broadcasted_iota(jnp.int32, (16, 256), 0)
    line8 = lax.broadcasted_iota(jnp.int32, (8, 256), 0)

    def up_y(v, beyond):
        return jnp.where(line16 == 15, beyond, pltpu.roll(v, 15, 0))

    def down_y(v, beyond):
        return jnp.where(line16 == 0, beyond, pltpu.roll(v, 1, 0))

    def forces(aux, electric):
        rho, mx, my, mz, c0, c1, opening = aux[:7]
        charge = -0.5 * ((c0 - c1) * opening)
        return rho * opening, [mx * opening, my * opening, mz * opening], [charge * e for e in electric], 1.0 / rho

    y_cells = []
    for side, dirs in enumerate((Y_LOW, Y_HIGH)):
        p = pot[96 + 8 * side : 104 + 8 * side, :]
        inner = jnp.zeros((8, 256), f32)
        for n in range(6):
            inner = jnp.where(line8 == n, pot[n * 16 + 15 * side : n * 16 + 15 * side + 1, :], inner)
        aux = [yr[side, 5 + n] for n in range(N_AUX)]
        left, right = pltpu.roll(p, 1, 0), pltpu.roll(p, 7, 0)
        front, back = roll_z(p, -1), roll_z(p, 1)
        rest = (6.0 + SCREEN) * p - aux[7] - inner - front - back
        given = jnp.where(line8 == 0, p[6:7, :], p[7:8, :])
        corner = (line8 == 0) | (line8 == 5)
        outer = jnp.where(corner, given, rest - left - right)
        left_all = jnp.where(line8 == 0, rest - right - outer, left)
        right_all = jnp.where(line8 == 5, rest - left - outer, right)
        along_y = inner - outer if side == 0 else outer - inner
        rho, m, force, inverse = forces(aux, (right_all - left_all, along_y, front - back))
        part = force_part(rho, m, force, inverse, dirs)
        moved = {d: roll_z(yr[side, n] + part[d], int(VELOCITY[d, 2])) for n, d in enumerate(dirs)}
        speed = aux[2] / aux[0]
        y_cells.append((p, moved, aux[4], aux[5], speed))

    planes = [pot[n * 16 : (n + 1) * 16, :] for n in range(6)]
    p_below = y_cells[0][0]
    p_above = y_cells[1][0]

    def aux_of(s):
        if s == -1:
            return [xr[0, n] for n in range(N_AUX)]
        if s == 4:
            return [xr[1, AUX + n] for n in range(N_AUX)]
        return [field[AUX + n, s] for n in range(N_AUX)]

    def base_of(d, s):
        if s == -1:
            return xr[0, SLOT[d] - AUX]
        if s == 4:
            return xr[1, SLOT[d]]
        return field[SLOT[d], s]

    def face(low, high, n):
        total = low[n] + high[n]
        return 0.25 * (low[2] + high[2]) * total - DIFFUSIVITY[n] * (
            (high[n] - low[n]) + (VALENCE[n] * 0.5) * total * (high[3] - low[3])
        )

    copies = []
    before = None
    for s in range(-1, 5):
        p = planes[s + 1]
        y_up, y_down = up_y(p, p_above[s + 1 : s + 2, :]), down_y(p, p_below[s + 1 : s + 2, :])
        front, back = roll_z(p, -1), roll_z(p, 1)
        aux = aux_of(s)
        if s == -1:
            right = planes[1]
            left = (6.0 + SCREEN) * p - aux[7] - right - y_up - y_down - front - back
            dirs = PLUS_X
        elif s == 4:
            left = planes[4]
            right = (6.0 + SCREEN) * p - aux[7] - left - y_up - y_down - front - back
            dirs = MINUS_X
        else:
            left, right = planes[s], planes[s + 2]
            dirs = [d for d in range(19) if 0 <= s + VELOCITY[d, 0] <= 3]
        rho, m, force, inverse = forces(aux, (right - left, y_up - y_down, front - back))
        part = force_part(rho, m, force, inverse, dirs)
        for d in dirs:
            cx, cy, cz = (int(n) for n in VELOCITY[d])
            v = base_of(d, s) + part[d]
            if cz:
                v = roll_z(v, cz)
            if cy == 1:
                v = down_y(v, y_cells[0][1][d][s + 1 : s + 2, :])
            elif cy == -1:
                v = up_y(v, y_cells[1][1][d][s + 1 : s + 2, :])
            out[d, s + cx] = v
        here_x = (aux[4], aux[5], aux[1] * inverse, p)
        if s >= 0:
            x_flux = [face(before[0], here_x, n) for n in range(2)]
            if s > 0:
                for n in range(2):
                    conc_out[n, s - 1] = before[1] * (before[2][n] - x_flux[n])
            if s < 4:
                uy, uz = aux[2] * inverse, aux[3] * inverse
                row = slice(s + 1, s + 2)
                here_y = (aux[4], aux[5], uy, p)
                below = tuple(down_y(v, y_cells[0][i][row, :]) for v, i in ((aux[4], 2), (aux[5], 3), (uy, 4))) + (y_down,)
                above = tuple(up_y(v, y_cells[1][i][row, :]) for v, i in ((aux[4], 2), (aux[5], 3), (uy, 4))) + (y_up,)
                here_z = (aux[4], aux[5], uz, p)
                ahead = tuple(roll_z(v, -1) for v in here_z[:3]) + (front,)
                rest = []
                for n in range(2):
                    z_flux = face(here_z, ahead, n)
                    change = face(here_y, above, n) - face(below, here_y, n) + (z_flux - roll_z(z_flux, 1))
                    rest.append(aux[4 + n] - change + x_flux[n])
                before = (here_x, aux[6], rest)
        else:
            before = (here_x,)
        if s >= 1:
            copies.append(pltpu.make_async_copy(out.at[:, s - 1], out_hbm.at[:, s - 1], sems.at[s - 1]))
            copies[-1].start()
    copies.append(pltpu.make_async_copy(conc_out, conc_hbm, sems.at[4]))
    copies[-1].start()
    for c in copies:
        c.wait()


def finish(pot, field, xr, yr):
    vmem = pl.BlockSpec(memory_space=pltpu.VMEM)
    hbm = pl.BlockSpec(memory_space=pl.ANY)
    return pl.pallas_call(
        step_kernel,
        out_shape=(jax.ShapeDtypeStruct((19, 4, 16, 256), f32), jax.ShapeDtypeStruct((2, 4, 16, 256), f32)),
        in_specs=[vmem] * 4,
        out_specs=(hbm, hbm),
        scratch_shapes=[
            pltpu.VMEM((19, 4, 16, 256), f32),
            pltpu.VMEM((2, 4, 16, 256), f32),
            pltpu.SemaphoreType.DMA((5,)),
        ],
        compiler_params=pltpu.CompilerParams(vmem_limit_bytes=VMEM_B),
    )(pot, field, xr, yr)


def per_device(populations, concentrations, solid_mask, charge_sites):
    return finish(*solve(populations, concentrations, solid_mask, charge_sites))


def solution(mesh):
    placed = (P(None, "row", "col", None), P(None, "row", "col", None), P("row", "col", None), P("row", "col", None))
    return jax.shard_map(
        per_device, mesh=mesh, in_specs=placed, out_specs=(P(None, "row", "col", None),) * 2, check_vma=False
    )
```

```python
import functools
import math

import jax
import jax.numpy as jnp
import numpy as np
from jax import lax
from jax.experimental import pallas as pl
from jax.experimental.pallas import tpu as pltpu
from jax.sharding import PartitionSpec as P

DEBYE = 32
SCREEN = 1.0 / (DEBYE * DEBYE)
MESH = pl.DeviceIdType.MESH
HIGHEST = lax.Precision.HIGHEST
f32 = jnp.float32

VELOCITY = np.array(
    [[0, 0, 0], [1, 0, 0], [-1, 0, 0], [0, 1, 0], [0, -1, 0], [0, 0, 1], [0, 0, -1],
     [1, 1, 0], [-1, -1, 0], [1, -1, 0], [-1, 1, 0], [1, 0, 1], [-1, 0, -1], [1, 0, -1],
     [-1, 0, 1], [0, 1, 1], [0, -1, -1], [0, 1, -1], [0, -1, 1]]
)
OPPOSITE = [0, 2, 1, 4, 3, 6, 5, 8, 7, 10, 9, 12, 11, 14, 13, 16, 15, 18, 17]
WEIGHT = np.array([1.0 / 3.0] + [1.0 / 18.0] * 6 + [1.0 / 36.0] * 12)
SITE_CHARGE = 1.5
DIFFUSIVITY = (0.12, 0.08)
VALENCE = (1.0, -1.0)

MINUS_X = [2, 8, 10, 12, 14]
PLUS_X = [1, 7, 9, 11, 13]
REST = [0, 3, 4, 5, 6, 15, 16, 17, 18]
SLOT = {d: i for i, d in enumerate(MINUS_X)}
SLOT.update({d: 13 + i for i, d in enumerate(PLUS_X)})
SLOT.update({d: 18 + i for i, d in enumerate(REST)})
AUX = 5
N_AUX = 8
N_FIELD = 27
N_SEND = 13
Y_LOW = [7, 10, 3, 15, 17]
Y_HIGH = [9, 8, 4, 16, 18]


def collision_matrices():
    v = VELOCITY.astype(np.float64)
    x, y, z = v[:, 0], v[:, 1], v[:, 2]
    q = x * x + y * y + z * z
    rows = [
        np.ones(19), 19 * q - 30, (21 * q * q - 53 * q + 24) / 2,
        x, (5 * q - 9) * x, y, (5 * q - 9) * y, z, (5 * q - 9) * z,
        3 * x * x - q, (3 * q - 5) * (3 * x * x - q), y * y - z * z, (3 * q - 5) * (y * y - z * z),
        x * y, y * z, x * z, (y * y - z * z) * x, (z * z - x * x) * y, (x * x - y * y) * z,
    ]
    m = np.stack(rows)
    rates = np.array([0, 1.19, 1.4, 0, 1.2, 0, 1.2, 0, 1.2, 1.25, 1.4, 1.25, 1.4, 1.25, 1.25, 1.25, 1.98, 1.98, 1.98])
    inverse = m.T / np.sum(m * m, axis=1)[None, :]
    return (inverse * rates) @ m, (inverse * (1 - rates / 2)) @ m


K, G = collision_matrices()


def even_vector(f0=0.0, axis=(0, 0, 0), plane=(0, 0, 0)):
    out = np.zeros(19)
    out[0] = f0
    for i in range(1, 19):
        c = VELOCITY[i]
        if np.abs(c).sum() == 1:
            out[i] = axis[int(np.argmax(np.abs(c)))]
        else:
            out[i] = plane[int(np.argmin(np.abs(c)))]
    return out


def relax_coefficients():
    left = np.eye(19) - K
    r0 = left @ even_vector(f0=1.0)
    ra = left @ even_vector(axis=(0.5, 0, 0))
    rp = left @ even_vector(plane=(0.25, 0, 0))
    x_axis, y_axis, yz, xy = 1, 3, 15, 7
    even = {
        "rest": (r0[0], ra[0], rp[0]),
        "axis": (r0[x_axis], ra[y_axis], rp[y_axis], ra[x_axis] - ra[y_axis], rp[x_axis] - rp[y_axis]),
        "plane": (r0[xy], ra[xy], rp[xy], ra[yz] - ra[xy], rp[yz] - rp[xy]),
    }
    h = np.zeros(19)
    h[[7, 8]], h[[9, 10]] = 0.25, -0.25
    even["shear"] = (left @ h)[7]
    d = np.zeros(19)
    d[1], d[2] = 0.5, -0.5
    od = left @ d
    e = np.zeros(19)
    e[[7, 9]], e[[8, 10]] = 0.25, -0.25
    oe = left @ e
    odd = {"axis": (od[1], oe[1]), "plane": (od[7], oe[7], oe[11])}
    return even, odd


def force_coefficients():
    c = VELOCITY.astype(np.float64)

    def quad(t):
        return WEIGHT * (4.5 * np.einsum("ia,ab,ib->i", c, t, c) - 1.5 * np.trace(t))

    t = np.zeros((3, 3))
    t[0, 0] = 1.0
    qa, qb = K @ quad(t), G @ quad(t)
    qr = K @ WEIGHT
    s = np.zeros((3, 3))
    s[0, 1] = s[1, 0] = 1.0
    sa, sb = K @ quad(s), G @ quad(s)
    lj = K @ (WEIGHT * 3 * c[:, 0])
    lf = G @ (WEIGHT * 3 * c[:, 0])
    return {
        "rest": (qa[0], qb[0], qr[0]),
        "axis_trace": (qa[3], qb[3], qr[3]),
        "axis": (qa[1] - qa[3], qb[1] - qb[3]),
        "plane_trace": (qa[7], qb[7], qr[7]),
        "plane": (qa[15] - qa[7], qb[15] - qb[7]),
        "shear": (sa[7], sb[7]),
        "odd_axis": (lj[1], lf[1]),
        "odd_plane": (lj[7], lf[7]),
    }


EVEN, ODD = relax_coefficients()
FORCE = force_coefficients()
PLANES = {0: (15, 17, 1, 2), 1: (11, 13, 0, 2), 2: (7, 9, 0, 1)}


def fl(v):
    return np.float32(v)


def moments_of(f):
    pair = {i: f[i] + f[i + 1] for i in range(1, 19, 2)}
    diff = {i: f[i] - f[i + 1] for i in range(1, 19, 2)}
    s = [pair[1], pair[3], pair[5]]
    g = [pair[15] + pair[17], pair[11] + pair[13], pair[7] + pair[9]]
    ts, tg = s[0] + s[1] + s[2], g[0] + g[1] + g[2]
    density = f[0] + ts + tg
    first = {p: diff[PLANES[p][0]] + diff[PLANES[p][1]] for p in range(3)}
    second = {p: diff[PLANES[p][0]] - diff[PLANES[p][1]] for p in range(3)}
    d = [diff[1], diff[3], diff[5]]
    along = [(first[2], first[1]), (second[2], first[0]), (second[1], second[0])]
    momentum = [d[a] + along[a][0] + along[a][1] for a in range(3)]
    return pair, s, g, ts, tg, density, d, along, momentum


def relaxed(f, moments):
    pair, s, g, ts, tg, _, d, along, _ = moments
    e = EVEN
    out = [None] * 19
    out[0] = fl(e["rest"][0]) * f[0] + fl(e["rest"][1]) * ts + fl(e["rest"][2]) * tg
    ca = fl(e["axis"][0]) * f[0] + fl(e["axis"][1]) * ts + fl(e["axis"][2]) * tg
    cp = fl(e["plane"][0]) * f[0] + fl(e["plane"][1]) * ts + fl(e["plane"][2]) * tg
    odd_axis, odd_plane = [], []
    for a in range(3):
        u, w = along[a]
        odd_axis.append(fl(ODD["axis"][0]) * d[a] + fl(ODD["axis"][1]) * (u + w))
        b = fl(ODD["plane"][0]) * d[a]
        odd_plane.append(
            (b + fl(ODD["plane"][1]) * u + fl(ODD["plane"][2]) * w, b + fl(ODD["plane"][1]) * w + fl(ODD["plane"][2]) * u)
        )
    for a in range(3):
        even = ca + fl(e["axis"][3]) * s[a] + fl(e["axis"][4]) * g[a]
        out[1 + 2 * a] = even + odd_axis[a]
        out[2 + 2 * a] = even - odd_axis[a]
    parts = {
        2: (odd_plane[0][0], odd_plane[1][0]),
        1: (odd_plane[0][1], odd_plane[2][0]),
        0: (odd_plane[1][1], odd_plane[2][1]),
    }
    for p in range(3):
        i, j, _, _ = PLANES[p]
        even = cp + fl(e["plane"][3]) * s[p] + fl(e["plane"][4]) * g[p]
        shear = fl(e["shear"]) * (pair[i] - pair[j])
        u, w = parts[p]
        out[i], out[i + 1] = even + shear + (u + w), even + shear - (u + w)
        out[j], out[j + 1] = even - shear + (u - w), even - shear - (u - w)
    return out


def force_part(density, momentum, force, inverse, wanted):
    k = FORCE
    j = [momentum[a] + 0.5 * force[a] for a in range(3)]
    u = [j[a] * inverse for a in range(3)]
    aa = [j[a] * u[a] for a in range(3)]
    bb = [2.0 * (u[a] * force[a]) for a in range(3)]
    ta, tb = aa[0] + aa[1] + aa[2], bb[0] + bb[1] + bb[2]
    out = {}
    if 0 in wanted:
        out[0] = fl(k["rest"][0]) * ta + fl(k["rest"][1]) * tb + fl(k["rest"][2]) * density
    axis_common = fl(k["axis_trace"][0]) * ta + fl(k["axis_trace"][1]) * tb + fl(k["axis_trace"][2]) * density
    plane_common = fl(k["plane_trace"][0]) * ta + fl(k["plane_trace"][1]) * tb + fl(k["plane_trace"][2]) * density
    odd_plane = [fl(k["odd_plane"][0]) * j[a] + fl(k["odd_plane"][1]) * force[a] for a in range(3)]
    for a in range(3):
        ids = (1 + 2 * a, 2 + 2 * a)
        if not any(i in wanted for i in ids):
            continue
        even = axis_common + fl(k["axis"][0]) * aa[a] + fl(k["axis"][1]) * bb[a]
        odd = fl(k["odd_axis"][0]) * j[a] + fl(k["odd_axis"][1]) * force[a]
        if ids[0] in wanted:
            out[ids[0]] = even + odd
        if ids[1] in wanted:
            out[ids[1]] = even - odd
    for p in range(3):
        i1, i2, a, b = PLANES[p]
        if not any(i in wanted for i in (i1, i1 + 1, i2, i2 + 1)):
            continue
        even = plane_common + fl(k["plane"][0]) * aa[p] + fl(k["plane"][1]) * bb[p]
        shear = fl(k["shear"][0]) * (j[a] * u[b]) + fl(k["shear"][1]) * (u[a] * force[b] + u[b] * force[a])
        up, down = even + shear, even - shear
        total, apart = odd_plane[a] + odd_plane[b], odd_plane[a] - odd_plane[b]
        for i, v in ((i1, (up, total)), (i2, (down, apart))):
            if i in wanted:
                out[i] = v[0] + v[1]
            if i + 1 in wanted:
                out[i + 1] = v[0] - v[1]
    return out


def cas(rows, columns, length):
    angle = 2 * np.pi * (np.outer(rows, columns) % length) / length
    return (np.cos(angle) + np.sin(angle)).astype(np.float32)


def eigen(length):
    return 2.0 - 2.0 * np.cos(2 * np.pi * np.arange(length) / length)


def tables(nx, ny, nz):
    r = np.array([x * 4 + zl for zl in range(4) for x in range(4)])
    own_rows = np.concatenate([4 * r + xi for xi in range(4)])
    ext_rows = np.concatenate([4 * r + xx for xx in range(-1, 5)])
    c = np.arange(16)
    low = np.stack([16 * c - 1] * 6 + [16 * c - 2] * 2, axis=1).reshape(-1)
    high = np.stack([16 * c + 16] * 6 + [16 * c + 17] * 2, axis=1).reshape(-1)
    return {
        "hz": cas(np.arange(nz), np.arange(nz), nz),
        "hx": cas(np.arange(nx), own_rows % nx, nx),
        "hx_ext": cas(ext_rows % nx, np.arange(nx), nx),
        "hy_ext": cas(np.arange(ny), np.concatenate([np.arange(ny), low % ny, high % ny]), ny),
        "eig_xy": (eigen(nx)[:, None] + eigen(ny)[None, :] + SCREEN).astype(np.float32),
        "eig_z": np.broadcast_to(eigen(nz).astype(np.float32)[:, None], (nz, 128)).copy(),
    }


def near(d):
    return min(d, 4 - d)


STEPS = sorted(
    [(dx, dy, dk) for dx in range(4) for dy in range(4) for dk in range(2)],
    key=lambda t: -(near(t[0]) + near(t[1])) * 10 - t[2],
)


def dot(a, b, contract=((1,), (0,))):
    return lax.dot_general(a, b, (contract, ((), ())), precision=HIGHEST, preferred_element_type=f32)


def solve_kernel(
    pops_hbm, conc_hbm, solid_hbm, sites_hbm, hz_hbm, hx_hbm, hxe_hbm, hye_hbm, exy_hbm, ez_hbm,
    pot_ref, field, xr, yr,
    hz_ref, hx_ref, hxe_ref, hye_ref, exy_ref, ez_ref,
    pops, conc, solid, sites, sa, ra, rb, grid, sp, rp, ys, sems, in_sems,
):
    row, col = lax.axis_index("row"), lax.axis_index("col")
    x, zl = row // 4, lax.rem(row, 4)
    zh, y, k = col // 8, lax.rem(col // 2, 4), lax.rem(col, 2)
    z = zh * 4 + zl
    plane = y * 4 + x
    depth = z * 2 + k
    mode = plane * 16 + depth

    loads = [
        pltpu.make_async_copy(conc_hbm, conc, in_sems.at[0]),
        pltpu.make_async_copy(solid_hbm, solid, in_sems.at[1]),
        pltpu.make_async_copy(sites_hbm, sites, in_sems.at[2]),
        pltpu.make_async_copy(hz_hbm, hz_ref, in_sems.at[5]),
        pltpu.make_async_copy(pops_hbm, pops, in_sems.at[3]),
        pltpu.make_async_copy(exy_hbm, exy_ref, in_sems.at[6]),
        pltpu.make_async_copy(ez_hbm, ez_ref, in_sems.at[7]),
        pltpu.make_async_copy(hx_hbm, hx_ref, in_sems.at[8]),
        pltpu.make_async_copy(hxe_hbm, hxe_ref, in_sems.at[9]),
        pltpu.make_async_copy(hye_hbm, hye_ref, in_sems.at[10]),
    ]
    for c in loads:
        c.start()

    barrier = pltpu.get_barrier_semaphore()
    xs = [lax.rem(x + d, 4) for d in range(4)]
    yy = [lax.rem(y + d, 4) for d in range(4)]
    plane_peers = [(dx, dy) for dx in range(4) for dy in range(4) if (dx, dy) != (0, 0)]
    plane_peers.sort(key=lambda t: -(near(t[0]) + near(t[1])))
    depth_peers = [(dz, dk) for dz in (4, 3, 5, 2, 6, 1, 7, 0) for dk in (1, 0) if (dz, dk) != (0, 0)]
    row_up, row_down = lax.rem(row + 1, 16), lax.rem(row + 15, 16)
    col_up, col_down = lax.rem(col + 1, 16), lax.rem(col + 15, 16)

    def plane_id(dx, dy):
        return {"row": xs[dx] * 4 + zl, "col": zh * 8 + yy[dy] * 2 + k}

    def depth_pos(dz, dk):
        return lax.rem(z + dz, 8), (k if dk == 0 else 1 - k)

    def depth_id(dz, dk):
        zz, kk = depth_pos(dz, dk)
        return {"row": x * 4 + lax.rem(zz, 4), "col": (zz // 4) * 8 + y * 2 + kk}

    ids = [plane_id(*t) for t in plane_peers] + [depth_id(*t) for t in depth_peers]
    ids += [{"row": row_up, "col": col}, {"row": row_down, "col": col}, {"row": row, "col": col_up}, {"row": row, "col": col_down}]
    for device in ids:
        pl.semaphore_signal(barrier, inc=1, device_id=device, device_id_type=MESH)

    for c in loads[:4]:
        c.wait()
    open_all = 1.0 - solid[...].astype(f32)
    kinds = sites[...]
    fixed = SITE_CHARGE * ((kinds == 1).astype(f32) - (kinds == 2).astype(f32))
    charge = (conc[0] - conc[1]) * open_all + fixed
    field[AUX + 4] = conc[0]
    field[AUX + 5] = conc[1]
    field[AUX + 6] = open_all
    field[AUX + 7] = charge
    flat = charge.reshape(64, 256)
    spectrum = dot(hz_ref[...], jnp.concatenate([flat, jnp.zeros((64, 256), f32)], axis=0), ((1,), (1,)))
    sa.reshape(256, 128)[...] = spectrum

    pl.semaphore_wait(barrier, len(ids))
    for t in plane_peers:
        other = yy[t[1]] * 4 + xs[t[0]]
        pltpu.make_async_remote_copy(
            sa.at[pl.ds(other * 16, 16)], ra.at[y, x], sems.at[0], sems.at[1], device_id=plane_id(*t), device_id_type=MESH
        ).start()
    keep = pltpu.make_async_copy(sa.at[pl.ds(plane * 16, 16)], ra.at[y, x], in_sems.at[4])
    keep.start()

    for c in loads[4:]:
        c.wait()

    def before(i, carry):
        xx, part = i // 2, pl.multiple_of(lax.rem(i, 2) * 8, 8)
        rows = pl.ds(part, 8)
        f = [pops[d, xx, rows, :] for d in range(19)]
        moments = moments_of(f)
        field[AUX, xx, rows, :] = moments[5]
        for a in range(3):
            field[AUX + 1 + a, xx, rows, :] = moments[8][a]
        wall = solid[xx, rows, :] == 1
        base = relaxed(f, moments)
        for d in range(19):
            field[SLOT[d], xx, rows, :] = jnp.where(wall, f[OPPOSITE[d]], base[d])
        return carry

    lax.fori_loop(0, 8, before, 0)
    to_up = pltpu.make_async_remote_copy(
        field.at[pl.ds(AUX, N_SEND), 3], xr.at[0], sems.at[2], sems.at[3], device_id={"row": row_up, "col": col}, device_id_type=MESH
    )
    to_down = pltpu.make_async_remote_copy(
        field.at[pl.ds(0, N_SEND), 0], xr.at[1], sems.at[4], sems.at[5], device_id={"row": row_down, "col": col}, device_id_type=MESH
    )
    to_up.start()
    to_down.start()

    keep.wait()
    blocks = sa.at[pl.ds(0, 240)]
    pltpu.make_async_copy(blocks, blocks, sems.at[1]).wait()
    for t in depth_peers:
        zz, kk = depth_pos(*t)
        pltpu.make_async_remote_copy(
            ra.at[:, :, zz * 2 + kk], rb.at[zh, :, k, pl.ds(zl * 4, 4)], sems.at[6], sems.at[7],
            device_id=depth_id(*t), device_id_type=MESH,
        ).start()
    keep = pltpu.make_async_copy(ra.at[:, :, depth], rb.at[zh, :, k, pl.ds(zl * 4, 4)], in_sems.at[4])
    keep.start()

    to_up.wait_recv()
    to_down.wait_recv()
    line = lax.broadcasted_iota(jnp.int32, (8, 256), 0)
    for side, (edge, dirs, low_dir, high_dir) in enumerate(((15, Y_LOW, 7, 10), (0, Y_HIGH, 9, 8))):
        for n in range(N_SEND):
            slot = SLOT[dirs[n]] if n < 5 else AUX + n - 5
            value = jnp.zeros((8, 256), f32)
            for xx in range(4):
                value = jnp.where(line == xx + 1, field[slot, xx, edge : edge + 1, :], value)
            if n >= 5 or dirs[n] == low_dir:
                value = jnp.where(line == 0, xr[0, slot - AUX, edge : edge + 1, :], value)
            if n >= 5 or dirs[n] == high_dir:
                value = jnp.where(line == 5, xr[1, slot, edge : edge + 1, :], value)
            ys[side, n] = value
    y_up = pltpu.make_async_remote_copy(
        ys.at[0], yr.at[0], sems.at[8], sems.at[9], device_id={"row": row, "col": col_up}, device_id_type=MESH
    )
    y_down = pltpu.make_async_remote_copy(
        ys.at[1], yr.at[1], sems.at[10], sems.at[11], device_id={"row": row, "col": col_down}, device_id_type=MESH
    )
    y_up.start()
    y_down.start()
    scale = 1.0 / ((exy_ref[...] + jnp.concatenate([ez_ref[pl.ds(mode, 1), :]] * 2, axis=1)) * float(64 * 256 * 256))
    keep.wait()
    pltpu.make_async_copy(blocks, blocks, sems.at[7]).wait()

    lane = lax.broadcasted_iota(jnp.int32, (16, 128), 1)
    sixteenth = lane // 16
    eighth = lane // 8
    in_eighth = lax.rem(lane, 8)
    arrived = rb.reshape(256, 128)
    for half in range(2):
        pieces = [arrived[(8 * half + j) * 16 : (8 * half + j + 1) * 16, :] for j in range(8)]
        for xi in range(4):
            acc = None
            for j in range(8):
                shift = (j - xi) * 16 % 128
                w = pltpu.roll(pieces[j], shift, 1) if shift else pieces[j]
                acc = w if acc is None else jnp.where(sixteenth == j, w, acc)
            grid[xi * 16 : (xi + 1) * 16, half * 128 : (half + 1) * 128] = acc
    g = dot(dot(hx_ref[...], grid[...]), hz_ref[...]) * scale
    out = dot(dot(hxe_ref[...], g), hye_ref[...])
    sides = []
    for base in (256, 384):
        merged = out[0:16, base : base + 128]
        for j in range(1, 8):
            r = {6: 0, 7: 5}.get(j, j)
            merged = jnp.where(in_eighth == j, out[r * 16 : (r + 1) * 16, base : base + 128], merged)
        sides.append(merged)
    send = sp.reshape(256, 128)
    for c in range(16):
        acc = None
        for xx in range(6):
            v = out[xx * 16 : (xx + 1) * 16, (c // 8) * 128 : (c // 8 + 1) * 128]
            shift = (xx - c % 8) * 16 % 128
            w = pltpu.roll(v, shift, 1) if shift else v
            acc = w if acc is None else jnp.where(sixteenth == xx, w, acc)
        for s in range(2):
            shift = (96 + 8 * s - 8 * c) % 128
            w = pltpu.roll(sides[s], shift, 1) if shift else sides[s]
            acc = jnp.where(eighth == 12 + s, w, acc)
        send[c * 16 : (c + 1) * 16, :] = acc

    ks = [k, 1 - k]

    def to_all(i, last):
        dz = 4 + (1 - 2 * lax.rem(i, 2)) * ((i + 1) // 2)
        zz = lax.rem(z + dz, 8)
        zr, zc = lax.rem(zz, 4), (zz // 4) * 8
        for dx, dy, dk in STEPS:
            if last and (dx, dy, dk) == (0, 0, 0):
                continue
            c = zc + yy[dy] * 2 + ks[dk]
            pltpu.make_async_remote_copy(
                sp.at[c * 16 + zr * 4 + xs[dx]], rp.at[mode], sems.at[12], sems.at[13],
                device_id={"row": xs[dx] * 4 + zr, "col": c}, device_id_type=MESH,
            ).start()

    def step(i, carry):
        to_all(i, False)
        return carry

    lax.fori_loop(0, 7, step, 0)
    to_all(7, True)
    keep = pltpu.make_async_copy(sp.at[col * 16 + zl * 4 + x], rp.at[mode], in_sems.at[4])
    keep.start()
    y_up.wait_recv()
    y_down.wait_recv()
    keep.wait()
    most = rp.at[pl.ds(0, 255)]
    pltpu.make_async_copy(most, most, sems.at[13]).wait()
    pot_ref[...] = dot(rp.reshape(256, 128)[...], hz_ref[...], ((0,), (0,)))

    pltpu.make_async_copy(blocks, blocks, sems.at[0]).wait()
    pltpu.make_async_copy(blocks, blocks, sems.at[6]).wait()
    pltpu.make_async_copy(most, most, sems.at[12]).wait()
    for c in (to_up, to_down, y_up, y_down):
        c.wait_send()


def solve(populations, concentrations, solid_mask, charge_sites):
    t = tables(64, 256, 256)
    vmem = pl.BlockSpec(memory_space=pltpu.VMEM)
    hbm = pl.BlockSpec(memory_space=pltpu.HBM)
    return pl.pallas_call(
        solve_kernel,
        out_shape=(
            jax.ShapeDtypeStruct((128, 256), f32),
            jax.ShapeDtypeStruct((N_FIELD, 4, 16, 256), f32),
            jax.ShapeDtypeStruct((2, N_SEND, 16, 256), f32),
            jax.ShapeDtypeStruct((2, N_SEND, 8, 256), f32),
        ),
        in_specs=[hbm] * 10,
        out_specs=(vmem,) * 4,
        scratch_shapes=[
            *[pltpu.VMEM(t[n].shape, f32) for n in TABLES],
            pltpu.VMEM((19, 4, 16, 256), f32),
            pltpu.VMEM((2, 4, 16, 256), f32),
            pltpu.VMEM((4, 16, 256), jnp.int32),
            pltpu.VMEM((4, 16, 256), jnp.int32),
            pltpu.VMEM((256, 1, 128), f32),
            pltpu.VMEM((4, 4, 16, 1, 128), f32),
            pltpu.VMEM((2, 4, 2, 16, 1, 128), f32),
            pltpu.VMEM((64, 256), f32),
            pltpu.VMEM((256, 1, 128), f32),
            pltpu.VMEM((256, 1, 128), f32),
            pltpu.VMEM((2, N_SEND, 8, 256), f32),
            pltpu.SemaphoreType.DMA((14,)),
            pltpu.SemaphoreType.DMA((11,)),
        ],
        compiler_params=pltpu.CompilerParams(collective_id=0, has_side_effects=True, vmem_limit_bytes=VMEM_A),
    )(
        *[
            pltpu.with_memory_space_constraint(v, pltpu.HBM)
            for v in (populations, concentrations, solid_mask, charge_sites, *[jnp.asarray(t[n]) for n in TABLES])
        ],
    )


TABLES = ("hz", "hx", "hx_ext", "hy_ext", "eig_xy", "eig_z")
VMEM_A = 32 * 2**20
VMEM_B = 24 * 2**20


def roll_z(v, shift):
    return pltpu.roll(v, shift % 256, 1)


def step_kernel(pot, field, xr, yr, out_hbm, conc_hbm, out, conc_out, sems):
    line16 = lax.broadcasted_iota(jnp.int32, (16, 256), 0)
    line8 = lax.broadcasted_iota(jnp.int32, (8, 256), 0)

    def up_y(v, beyond):
        return jnp.where(line16 == 15, beyond, pltpu.roll(v, 15, 0))

    def down_y(v, beyond):
        return jnp.where(line16 == 0, beyond, pltpu.roll(v, 1, 0))

    def forces(aux, electric):
        rho, mx, my, mz, c0, c1, opening = aux[:7]
        charge = -0.5 * ((c0 - c1) * opening)
        return rho * opening, [mx * opening, my * opening, mz * opening], [charge * e for e in electric], 1.0 / rho

    y_cells = []
    for side, dirs in enumerate((Y_LOW, Y_HIGH)):
        p = pot[96 + 8 * side : 104 + 8 * side, :]
        inner = jnp.zeros((8, 256), f32)
        for n in range(6):
            inner = jnp.where(line8 == n, pot[n * 16 + 15 * side : n * 16 + 15 * side + 1, :], inner)
        aux = [yr[side, 5 + n] for n in range(N_AUX)]
        left, right = pltpu.roll(p, 1, 0), pltpu.roll(p, 7, 0)
        front, back = roll_z(p, -1), roll_z(p, 1)
        rest = (6.0 + SCREEN) * p - aux[7] - inner - front - back
        given = jnp.where(line8 == 0, p[6:7, :], p[7:8, :])
        corner = (line8 == 0) | (line8 == 5)
        outer = jnp.where(corner, given, rest - left - right)
        left_all = jnp.where(line8 == 0, rest - right - outer, left)
        right_all = jnp.where(line8 == 5, rest - left - outer, right)
        along_y = inner - outer if side == 0 else outer - inner
        rho, m, force, inverse = forces(aux, (right_all - left_all, along_y, front - back))
        part = force_part(rho, m, force, inverse, dirs)
        moved = {d: roll_z(yr[side, n] + part[d], int(VELOCITY[d, 2])) for n, d in enumerate(dirs)}
        speed = aux[2] / aux[0]
        y_cells.append((p, moved, aux[4], aux[5], speed))

    planes = [pot[n * 16 : (n + 1) * 16, :] for n in range(6)]
    p_below = y_cells[0][0]
    p_above = y_cells[1][0]

    def aux_of(s):
        if s == -1:
            return [xr[0, n] for n in range(N_AUX)]
        if s == 4:
            return [xr[1, AUX + n] for n in range(N_AUX)]
        return [field[AUX + n, s] for n in range(N_AUX)]

    def base_of(d, s):
        if s == -1:
            return xr[0, SLOT[d] - AUX]
        if s == 4:
            return xr[1, SLOT[d]]
        return field[SLOT[d], s]

    def face(low, high, n):
        total = low[n] + high[n]
        return 0.25 * (low[2] + high[2]) * total - DIFFUSIVITY[n] * (
            (high[n] - low[n]) + (VALENCE[n] * 0.5) * total * (high[3] - low[3])
        )

    copies = []
    before = None
    for s in range(-1, 5):
        p = planes[s + 1]
        y_up, y_down = up_y(p, p_above[s + 1 : s + 2, :]), down_y(p, p_below[s + 1 : s + 2, :])
        front, back = roll_z(p, -1), roll_z(p, 1)
        aux = aux_of(s)
        if s == -1:
            right = planes[1]
            left = (6.0 + SCREEN) * p - aux[7] - right - y_up - y_down - front - back
            dirs = PLUS_X
        elif s == 4:
            left = planes[4]
            right = (6.0 + SCREEN) * p - aux[7] - left - y_up - y_down - front - back
            dirs = MINUS_X
        else:
            left, right = planes[s], planes[s + 2]
            dirs = [d for d in range(19) if 0 <= s + VELOCITY[d, 0] <= 3]
        rho, m, force, inverse = forces(aux, (right - left, y_up - y_down, front - back))
        part = force_part(rho, m, force, inverse, dirs)
        for d in dirs:
            cx, cy, cz = (int(n) for n in VELOCITY[d])
            v = base_of(d, s) + part[d]
            if cz:
                v = roll_z(v, cz)
            if cy == 1:
                v = down_y(v, y_cells[0][1][d][s + 1 : s + 2, :])
            elif cy == -1:
                v = up_y(v, y_cells[1][1][d][s + 1 : s + 2, :])
            out[d, s + cx] = v
        here_x = (aux[4], aux[5], aux[1] * inverse, p)
        if s >= 0:
            x_flux = [face(before[0], here_x, n) for n in range(2)]
            if s > 0:
                for n in range(2):
                    conc_out[n, s - 1] = before[1] * (before[2][n] - x_flux[n])
            if s < 4:
                uy, uz = aux[2] * inverse, aux[3] * inverse
                row = slice(s + 1, s + 2)
                here_y = (aux[4], aux[5], uy, p)
                below = tuple(down_y(v, y_cells[0][i][row, :]) for v, i in ((aux[4], 2), (aux[5], 3), (uy, 4))) + (y_down,)
                above = tuple(up_y(v, y_cells[1][i][row, :]) for v, i in ((aux[4], 2), (aux[5], 3), (uy, 4))) + (y_up,)
                here_z = (aux[4], aux[5], uz, p)
                ahead = tuple(roll_z(v, -1) for v in here_z[:3]) + (front,)
                rest = []
                for n in range(2):
                    z_flux = face(here_z, ahead, n)
                    change = face(here_y, above, n) - face(below, here_y, n) + (z_flux - roll_z(z_flux, 1))
                    rest.append(aux[4 + n] - change + x_flux[n])
                before = (here_x, aux[6], rest)
        else:
            before = (here_x,)
        if s >= 1:
            copies.append(pltpu.make_async_copy(out.at[:, s - 1], out_hbm.at[:, s - 1], sems.at[s - 1]))
            copies[-1].start()
    copies.append(pltpu.make_async_copy(conc_out, conc_hbm, sems.at[4]))
    copies[-1].start()
    for c in copies:
        c.wait()


def finish(pot, field, xr, yr):
    vmem = pl.BlockSpec(memory_space=pltpu.VMEM)
    hbm = pl.BlockSpec(memory_space=pl.ANY)
    return pl.pallas_call(
        step_kernel,
        out_shape=(jax.ShapeDtypeStruct((19, 4, 16, 256), f32), jax.ShapeDtypeStruct((2, 4, 16, 256), f32)),
        in_specs=[vmem] * 4,
        out_specs=(hbm, hbm),
        scratch_shapes=[
            pltpu.VMEM((19, 4, 16, 256), f32),
            pltpu.VMEM((2, 4, 16, 256), f32),
            pltpu.SemaphoreType.DMA((5,)),
        ],
        compiler_params=pltpu.CompilerParams(vmem_limit_bytes=VMEM_B),
    )(pot, field, xr, yr)


def per_device(populations, concentrations, solid_mask, charge_sites):
    return finish(*solve(populations, concentrations, solid_mask, charge_sites))


def solution(mesh):
    placed = (P(None, "row", "col", None), P(None, "row", "col", None), P("row", "col", None), P("row", "col", None))
    return jax.shard_map(
        per_device, mesh=mesh, in_specs=placed, out_specs=(P(None, "row", "col", None),) * 2, check_vma=False
    )
```

```python
import functools
import math

import jax
import jax.numpy as jnp
import numpy as np
from jax import lax
from jax.experimental import pallas as pl
from jax.experimental.pallas import tpu as pltpu
from jax.sharding import PartitionSpec as P

DEBYE = 32
SCREEN = 1.0 / (DEBYE * DEBYE)
MESH = pl.DeviceIdType.MESH
HIGHEST = lax.Precision.HIGHEST
f32 = jnp.float32

VELOCITY = np.array(
    [[0, 0, 0], [1, 0, 0], [-1, 0, 0], [0, 1, 0], [0, -1, 0], [0, 0, 1], [0, 0, -1],
     [1, 1, 0], [-1, -1, 0], [1, -1, 0], [-1, 1, 0], [1, 0, 1], [-1, 0, -1], [1, 0, -1],
     [-1, 0, 1], [0, 1, 1], [0, -1, -1], [0, 1, -1], [0, -1, 1]]
)
OPPOSITE = [0, 2, 1, 4, 3, 6, 5, 8, 7, 10, 9, 12, 11, 14, 13, 16, 15, 18, 17]
WEIGHT = np.array([1.0 / 3.0] + [1.0 / 18.0] * 6 + [1.0 / 36.0] * 12)
SITE_CHARGE = 1.5
DIFFUSIVITY = (0.12, 0.08)
VALENCE = (1.0, -1.0)

MINUS_X = [2, 8, 10, 12, 14]
PLUS_X = [1, 7, 9, 11, 13]
REST = [0, 3, 4, 5, 6, 15, 16, 17, 18]
SLOT = {d: i for i, d in enumerate(MINUS_X)}
SLOT.update({d: 13 + i for i, d in enumerate(PLUS_X)})
SLOT.update({d: 18 + i for i, d in enumerate(REST)})
AUX = 5
N_AUX = 8
N_FIELD = 27
N_SEND = 13
Y_LOW = [7, 10, 3, 15, 17]
Y_HIGH = [9, 8, 4, 16, 18]


def collision_matrices():
    v = VELOCITY.astype(np.float64)
    x, y, z = v[:, 0], v[:, 1], v[:, 2]
    q = x * x + y * y + z * z
    rows = [
        np.ones(19), 19 * q - 30, (21 * q * q - 53 * q + 24) / 2,
        x, (5 * q - 9) * x, y, (5 * q - 9) * y, z, (5 * q - 9) * z,
        3 * x * x - q, (3 * q - 5) * (3 * x * x - q), y * y - z * z, (3 * q - 5) * (y * y - z * z),
        x * y, y * z, x * z, (y * y - z * z) * x, (z * z - x * x) * y, (x * x - y * y) * z,
    ]
    m = np.stack(rows)
    rates = np.array([0, 1.19, 1.4, 0, 1.2, 0, 1.2, 0, 1.2, 1.25, 1.4, 1.25, 1.4, 1.25, 1.25, 1.25, 1.98, 1.98, 1.98])
    inverse = m.T / np.sum(m * m, axis=1)[None, :]
    return (inverse * rates) @ m, (inverse * (1 - rates / 2)) @ m


K, G = collision_matrices()


def even_vector(f0=0.0, axis=(0, 0, 0), plane=(0, 0, 0)):
    out = np.zeros(19)
    out[0] = f0
    for i in range(1, 19):
        c = VELOCITY[i]
        if np.abs(c).sum() == 1:
            out[i] = axis[int(np.argmax(np.abs(c)))]
        else:
            out[i] = plane[int(np.argmin(np.abs(c)))]
    return out


def relax_coefficients():
    left = np.eye(19) - K
    r0 = left @ even_vector(f0=1.0)
    ra = left @ even_vector(axis=(0.5, 0, 0))
    rp = left @ even_vector(plane=(0.25, 0, 0))
    x_axis, y_axis, yz, xy = 1, 3, 15, 7
    even = {
        "rest": (r0[0], ra[0], rp[0]),
        "axis": (r0[x_axis], ra[y_axis], rp[y_axis], ra[x_axis] - ra[y_axis], rp[x_axis] - rp[y_axis]),
        "plane": (r0[xy], ra[xy], rp[xy], ra[yz] - ra[xy], rp[yz] - rp[xy]),
    }
    h = np.zeros(19)
    h[[7, 8]], h[[9, 10]] = 0.25, -0.25
    even["shear"] = (left @ h)[7]
    d = np.zeros(19)
    d[1], d[2] = 0.5, -0.5
    od = left @ d
    e = np.zeros(19)
    e[[7, 9]], e[[8, 10]] = 0.25, -0.25
    oe = left @ e
    odd = {"axis": (od[1], oe[1]), "plane": (od[7], oe[7], oe[11])}
    return even, odd


def force_coefficients():
    c = VELOCITY.astype(np.float64)

    def quad(t):
        return WEIGHT * (4.5 * np.einsum("ia,ab,ib->i", c, t, c) - 1.5 * np.trace(t))

    t = np.zeros((3, 3))
    t[0, 0] = 1.0
    qa, qb = K @ quad(t), G @ quad(t)
    qr = K @ WEIGHT
    s = np.zeros((3, 3))
    s[0, 1] = s[1, 0] = 1.0
    sa, sb = K @ quad(s), G @ quad(s)
    lj = K @ (WEIGHT * 3 * c[:, 0])
    lf = G @ (WEIGHT * 3 * c[:, 0])
    return {
        "rest": (qa[0], qb[0], qr[0]),
        "axis_trace": (qa[3], qb[3], qr[3]),
        "axis": (qa[1] - qa[3], qb[1] - qb[3]),
        "plane_trace": (qa[7], qb[7], qr[7]),
        "plane": (qa[15] - qa[7], qb[15] - qb[7]),
        "shear": (sa[7], sb[7]),
        "odd_axis": (lj[1], lf[1]),
        "odd_plane": (lj[7], lf[7]),
    }


EVEN, ODD = relax_coefficients()
FORCE = force_coefficients()
PLANES = {0: (15, 17, 1, 2), 1: (11, 13, 0, 2), 2: (7, 9, 0, 1)}


def fl(v):
    return np.float32(v)


def moments_of(f):
    pair = {i: f[i] + f[i + 1] for i in range(1, 19, 2)}
    diff = {i: f[i] - f[i + 1] for i in range(1, 19, 2)}
    s = [pair[1], pair[3], pair[5]]
    g = [pair[15] + pair[17], pair[11] + pair[13], pair[7] + pair[9]]
    ts, tg = s[0] + s[1] + s[2], g[0] + g[1] + g[2]
    density = f[0] + ts + tg
    first = {p: diff[PLANES[p][0]] + diff[PLANES[p][1]] for p in range(3)}
    second = {p: diff[PLANES[p][0]] - diff[PLANES[p][1]] for p in range(3)}
    d = [diff[1], diff[3], diff[5]]
    along = [(first[2], first[1]), (second[2], first[0]), (second[1], second[0])]
    momentum = [d[a] + along[a][0] + along[a][1] for a in range(3)]
    return pair, s, g, ts, tg, density, d, along, momentum


def relaxed(f, moments):
    pair, s, g, ts, tg, _, d, along, _ = moments
    e = EVEN
    out = [None] * 19
    out[0] = fl(e["rest"][0]) * f[0] + fl(e["rest"][1]) * ts + fl(e["rest"][2]) * tg
    ca = fl(e["axis"][0]) * f[0] + fl(e["axis"][1]) * ts + fl(e["axis"][2]) * tg
    cp = fl(e["plane"][0]) * f[0] + fl(e["plane"][1]) * ts + fl(e["plane"][2]) * tg
    odd_axis, odd_plane = [], []
    for a in range(3):
        u, w = along[a]
        odd_axis.append(fl(ODD["axis"][0]) * d[a] + fl(ODD["axis"][1]) * (u + w))
        b = fl(ODD["plane"][0]) * d[a]
        odd_plane.append(
            (b + fl(ODD["plane"][1]) * u + fl(ODD["plane"][2]) * w, b + fl(ODD["plane"][1]) * w + fl(ODD["plane"][2]) * u)
        )
    for a in range(3):
        even = ca + fl(e["axis"][3]) * s[a] + fl(e["axis"][4]) * g[a]
        out[1 + 2 * a] = even + odd_axis[a]
        out[2 + 2 * a] = even - odd_axis[a]
    parts = {
        2: (odd_plane[0][0], odd_plane[1][0]),
        1: (odd_plane[0][1], odd_plane[2][0]),
        0: (odd_plane[1][1], odd_plane[2][1]),
    }
    for p in range(3):
        i, j, _, _ = PLANES[p]
        even = cp + fl(e["plane"][3]) * s[p] + fl(e["plane"][4]) * g[p]
        shear = fl(e["shear"]) * (pair[i] - pair[j])
        u, w = parts[p]
        out[i], out[i + 1] = even + shear + (u + w), even + shear - (u + w)
        out[j], out[j + 1] = even - shear + (u - w), even - shear - (u - w)
    return out


def force_part(density, momentum, force, inverse, wanted):
    k = FORCE
    j = [momentum[a] + 0.5 * force[a] for a in range(3)]
    u = [j[a] * inverse for a in range(3)]
    aa = [j[a] * u[a] for a in range(3)]
    bb = [2.0 * (u[a] * force[a]) for a in range(3)]
    ta, tb = aa[0] + aa[1] + aa[2], bb[0] + bb[1] + bb[2]
    out = {}
    if 0 in wanted:
        out[0] = fl(k["rest"][0]) * ta + fl(k["rest"][1]) * tb + fl(k["rest"][2]) * density
    axis_common = fl(k["axis_trace"][0]) * ta + fl(k["axis_trace"][1]) * tb + fl(k["axis_trace"][2]) * density
    plane_common = fl(k["plane_trace"][0]) * ta + fl(k["plane_trace"][1]) * tb + fl(k["plane_trace"][2]) * density
    odd_plane = [fl(k["odd_plane"][0]) * j[a] + fl(k["odd_plane"][1]) * force[a] for a in range(3)]
    for a in range(3):
        ids = (1 + 2 * a, 2 + 2 * a)
        if not any(i in wanted for i in ids):
            continue
        even = axis_common + fl(k["axis"][0]) * aa[a] + fl(k["axis"][1]) * bb[a]
        odd = fl(k["odd_axis"][0]) * j[a] + fl(k["odd_axis"][1]) * force[a]
        if ids[0] in wanted:
            out[ids[0]] = even + odd
        if ids[1] in wanted:
            out[ids[1]] = even - odd
    for p in range(3):
        i1, i2, a, b = PLANES[p]
        if not any(i in wanted for i in (i1, i1 + 1, i2, i2 + 1)):
            continue
        even = plane_common + fl(k["plane"][0]) * aa[p] + fl(k["plane"][1]) * bb[p]
        shear = fl(k["shear"][0]) * (j[a] * u[b]) + fl(k["shear"][1]) * (u[a] * force[b] + u[b] * force[a])
        up, down = even + shear, even - shear
        total, apart = odd_plane[a] + odd_plane[b], odd_plane[a] - odd_plane[b]
        for i, v in ((i1, (up, total)), (i2, (down, apart))):
            if i in wanted:
                out[i] = v[0] + v[1]
            if i + 1 in wanted:
                out[i + 1] = v[0] - v[1]
    return out


def cas(rows, columns, length):
    angle = 2 * np.pi * (np.outer(rows, columns) % length) / length
    return (np.cos(angle) + np.sin(angle)).astype(np.float32)


def eigen(length):
    return 2.0 - 2.0 * np.cos(2 * np.pi * np.arange(length) / length)


def tables(nx, ny, nz):
    r = np.array([x * 4 + zl for zl in range(4) for x in range(4)])
    own_rows = np.concatenate([4 * r + xi for xi in range(4)])
    ext_rows = np.concatenate([4 * r + xx for xx in range(-1, 5)])
    c = np.arange(16)
    low = np.stack([16 * c - 1] * 6 + [16 * c - 2] * 2, axis=1).reshape(-1)
    high = np.stack([16 * c + 16] * 6 + [16 * c + 17] * 2, axis=1).reshape(-1)
    return {
        "hz": cas(np.arange(nz), np.arange(nz), nz),
        "hx": cas(np.arange(nx), own_rows % nx, nx),
        "hx_ext": cas(ext_rows % nx, np.arange(nx), nx),
        "hy_ext": cas(np.arange(ny), np.concatenate([np.arange(ny), low % ny, high % ny]), ny),
        "eig_xy": (eigen(nx)[:, None] + eigen(ny)[None, :] + SCREEN).astype(np.float32),
        "eig_z": np.broadcast_to(eigen(nz).astype(np.float32)[:, None], (nz, 128)).copy(),
    }


def near(d):
    return min(d, 4 - d)


STEPS = sorted(
    [(dx, dy, dk) for dx in range(4) for dy in range(4) for dk in range(2)],
    key=lambda t: -(near(t[0]) + near(t[1])) * 10 - t[2],
)


def dot(a, b, contract=((1,), (0,))):
    return lax.dot_general(a, b, (contract, ((), ())), precision=HIGHEST, preferred_element_type=f32)


def solve_kernel(
    pops_hbm, conc_hbm, solid_hbm, sites_hbm, hz_hbm, hx_hbm, hxe_hbm, hye_hbm, exy_hbm, ez_hbm,
    pot_ref, field, xr, yr,
    hz_ref, hx_ref, hxe_ref, hye_ref, exy_ref, ez_ref,
    pops, conc, solid, sites, sa, ra, rb, grid, sp, rp, ys, yin, cs, cin, sems, side_sems, in_sems,
):
    row, col = lax.axis_index("row"), lax.axis_index("col")
    x, zl = row // 4, lax.rem(row, 4)
    zh, y, k = col // 8, lax.rem(col // 2, 4), lax.rem(col, 2)
    z = zh * 4 + zl
    plane = y * 4 + x
    depth = z * 2 + k
    mode = depth * 16 + plane

    loads = [
        pltpu.make_async_copy(conc_hbm, conc, in_sems.at[0]),
        pltpu.make_async_copy(solid_hbm, solid, in_sems.at[1]),
        pltpu.make_async_copy(sites_hbm, sites, in_sems.at[2]),
        pltpu.make_async_copy(hz_hbm, hz_ref, in_sems.at[5]),
        pltpu.make_async_copy(pops_hbm, pops, in_sems.at[3]),
        pltpu.make_async_copy(exy_hbm, exy_ref, in_sems.at[6]),
        pltpu.make_async_copy(ez_hbm, ez_ref, in_sems.at[7]),
        pltpu.make_async_copy(hx_hbm, hx_ref, in_sems.at[8]),
        pltpu.make_async_copy(hxe_hbm, hxe_ref, in_sems.at[9]),
        pltpu.make_async_copy(hye_hbm, hye_ref, in_sems.at[10]),
    ]
    for c in loads:
        c.start()

    barrier = pltpu.get_barrier_semaphore()
    xs = [lax.rem(x + d, 4) for d in range(4)]
    yy = [lax.rem(y + d, 4) for d in range(4)]
    plane_peers = [(dx, dy) for dx in range(4) for dy in range(4) if (dx, dy) != (0, 0)]
    plane_peers.sort(key=lambda t: -(near(t[0]) + near(t[1])))
    depth_peers = [(dz, dk) for dz in (4, 3, 5, 2, 6, 1, 7, 0) for dk in (1, 0) if (dz, dk) != (0, 0)]
    row_up, row_down = lax.rem(row + 1, 16), lax.rem(row + 15, 16)
    col_up, col_down = lax.rem(col + 1, 16), lax.rem(col + 15, 16)

    def plane_id(dx, dy):
        return {"row": xs[dx] * 4 + zl, "col": zh * 8 + yy[dy] * 2 + k}

    def depth_pos(dz, dk):
        return lax.rem(z + dz, 8), (k if dk == 0 else 1 - k)

    def depth_id(dz, dk):
        zz, kk = depth_pos(dz, dk)
        return {"row": x * 4 + lax.rem(zz, 4), "col": (zz // 4) * 8 + y * 2 + kk}

    ids = [plane_id(*t) for t in plane_peers] + [depth_id(*t) for t in depth_peers]
    ids += [{"row": row_up, "col": col}, {"row": row_down, "col": col}, {"row": row, "col": col_up}, {"row": row, "col": col_down}]
    corner_ids = [{"row": r, "col": c} for c in (col_up, col_down) for r in (row_up, row_down)]
    ids += corner_ids
    for device in ids:
        pl.semaphore_signal(barrier, inc=1, device_id=device, device_id_type=MESH)

    for c in loads[:4]:
        c.wait()
    open_all = 1.0 - solid[...].astype(f32)
    kinds = sites[...]
    fixed = SITE_CHARGE * ((kinds == 1).astype(f32) - (kinds == 2).astype(f32))
    charge = (conc[0] - conc[1]) * open_all + fixed
    field[AUX + 4] = conc[0]
    field[AUX + 5] = conc[1]
    field[AUX + 6] = open_all
    field[AUX + 7] = charge
    flat = charge.reshape(64, 256)
    spectrum = dot(hz_ref[...], jnp.concatenate([flat, jnp.zeros((64, 256), f32)], axis=0), ((1,), (1,)))
    sa.reshape(256, 128)[...] = spectrum

    pl.semaphore_wait(barrier, len(ids))
    for t in depth_peers:
        zz, kk = depth_pos(*t)
        pltpu.make_async_remote_copy(
            sa.at[pl.ds((zz * 2 + kk) * 16, 16)], ra.at[zh, k, zl], sems.at[0], sems.at[1], device_id=depth_id(*t), device_id_type=MESH
        ).start()
    keep = pltpu.make_async_copy(sa.at[pl.ds(depth * 16, 16)], ra.at[zh, k, zl], in_sems.at[4])
    keep.start()

    def to_side(n, source, target, device):
        return pltpu.make_async_remote_copy(
            source, target, side_sems.at[2 * n], side_sems.at[2 * n + 1], device_id=device, device_id_type=MESH
        )

    up, down = {"row": row_up, "col": col}, {"row": row_down, "col": col}
    sides = [
        to_side(0, field.at[pl.ds(AUX + 4, 4), 3], xr.at[0, pl.ds(4, 4)], up),
        to_side(1, field.at[pl.ds(AUX + 4, 4), 0], xr.at[1, pl.ds(AUX + 4, 4)], down),
        to_side(2, field.at[pl.ds(AUX, 4), 3], xr.at[0, pl.ds(0, 4)], up),
        to_side(3, field.at[pl.ds(AUX, 4), 0], xr.at[1, pl.ds(AUX, 4)], down),
    ]
    for c in loads[4:]:
        c.wait()

    def before(i, carry):
        xx, part = lax.rem(3 * (i // 2), 4), pl.multiple_of(lax.rem(i, 2) * 8, 8)
        rows = pl.ds(part, 8)
        f = [pops[d, xx, rows, :] for d in range(19)]
        moments = moments_of(f)
        field[AUX, xx, rows, :] = moments[5]
        for a in range(3):
            field[AUX + 1 + a, xx, rows, :] = moments[8][a]
        wall = solid[xx, rows, :] == 1
        base = relaxed(f, moments)
        for d in range(19):
            field[SLOT[d], xx, rows, :] = jnp.where(wall, f[OPPOSITE[d]], base[d])
        return carry

    lax.fori_loop(0, 4, before, 0)
    late = [
        to_side(8, field.at[pl.ds(SLOT[1], 5), 3], xr.at[0, pl.ds(N_AUX, 5)], up),
        to_side(9, field.at[pl.ds(SLOT[2], 5), 0], xr.at[1, pl.ds(0, 5)], down),
    ]
    lax.fori_loop(4, 8, before, 0)
    line4 = lax.broadcasted_iota(jnp.int32, (4, 256), 0)
    for side, (edge, dirs) in enumerate(((15, Y_LOW), (0, Y_HIGH))):
        for n in range(N_SEND):
            slot = SLOT[dirs[n]] if n < 5 else AUX + n - 5
            value = field[slot, 3, edge : edge + 1, :]
            for xx in range(3):
                value = jnp.where(line4 == xx, field[slot, xx, edge : edge + 1, :], value)
            ys[side, n] = value
        for end, (xx, d) in enumerate(((3, dirs[0]), (0, dirs[1]))):
            for n in range(N_AUX):
                cs[2 * side + end, n : n + 1, :] = field[AUX + n, xx, edge : edge + 1, :]
            for n in range(N_AUX, 16):
                cs[2 * side + end, n : n + 1, :] = field[SLOT[d], xx, edge : edge + 1, :]
    sides += [to_side(10, ys.at[0], yin.at[0], {"row": row, "col": col_up}), to_side(11, ys.at[1], yin.at[1], {"row": row, "col": col_down})]
    sides += [to_side(4 + n, cs.at[n], cin.at[n], corner_ids[n]) for n in range(4)]
    for c in sides[4:]:
        c.start()

    keep.wait()
    blocks = sa.at[pl.ds(0, 240)]
    pltpu.make_async_copy(blocks, blocks, sems.at[1]).wait()
    for t in plane_peers:
        other = yy[t[1]] * 4 + xs[t[0]]
        pltpu.make_async_remote_copy(
            ra.at[:, :, :, other], rb.at[:, y, :, :, x], sems.at[6], sems.at[7], device_id=plane_id(*t), device_id_type=MESH
        ).start()
    keep = pltpu.make_async_copy(ra.at[:, :, :, plane], rb.at[:, y, :, :, x], in_sems.at[4])
    keep.start()

    for c in sides[:2]:
        c.start()
    for c in sides[2:4]:
        c.start()
    sides += late
    scale = 1.0 / ((exy_ref[...] + jnp.concatenate([ez_ref[pl.ds(mode, 1), :]] * 2, axis=1)) * float(64 * 256 * 256))
    keep.wait()
    pltpu.make_async_copy(blocks, blocks, sems.at[7]).wait()

    lane = lax.broadcasted_iota(jnp.int32, (16, 128), 1)
    sixteenth = lane // 16
    eighth = lane // 8
    in_eighth = lax.rem(lane, 8)
    arrived = rb.reshape(256, 128)
    for half in range(2):
        pieces = [arrived[(8 * half + j) * 16 : (8 * half + j + 1) * 16, :] for j in range(8)]
        for xi in range(4):
            acc = None
            for j in range(8):
                shift = (j - xi) * 16 % 128
                w = pltpu.roll(pieces[j], shift, 1) if shift else pieces[j]
                acc = w if acc is None else jnp.where(sixteenth == j, w, acc)
            grid[xi * 16 : (xi + 1) * 16, half * 128 : (half + 1) * 128] = acc
    g = dot(dot(hx_ref[...], grid[...]), hz_ref[...]) * scale
    out = dot(dot(hxe_ref[...], g), hye_ref[...])
    rims = []
    for base in (256, 384):
        merged = out[0:16, base : base + 128]
        for j in range(1, 8):
            r = {6: 0, 7: 5}.get(j, j)
            merged = jnp.where(in_eighth == j, out[r * 16 : (r + 1) * 16, base : base + 128], merged)
        rims.append(merged)
    send = sp.reshape(256, 128)
    for c in range(16):
        acc = None
        for xx in range(6):
            v = out[xx * 16 : (xx + 1) * 16, (c // 8) * 128 : (c // 8 + 1) * 128]
            shift = (xx - c % 8) * 16 % 128
            w = pltpu.roll(v, shift, 1) if shift else v
            acc = w if acc is None else jnp.where(sixteenth == xx, w, acc)
        for s in range(2):
            shift = (96 + 8 * s - 8 * c) % 128
            w = pltpu.roll(rims[s], shift, 1) if shift else rims[s]
            acc = jnp.where(eighth == 12 + s, w, acc)
        send[c * 16 : (c + 1) * 16, :] = acc

    ks = [k, 1 - k]

    def to_all(i, last):
        dz = 4 + (1 - 2 * lax.rem(i, 2)) * ((i + 1) // 2)
        zz = lax.rem(z + dz, 8)
        zr, zc = lax.rem(zz, 4), (zz // 4) * 8
        for dx, dy, dk in STEPS:
            if last and (dx, dy, dk) == (0, 0, 0):
                continue
            c = zc + yy[dy] * 2 + ks[dk]
            pltpu.make_async_remote_copy(
                sp.at[c * 16 + zr * 4 + xs[dx]], rp.at[mode], sems.at[12], sems.at[13],
                device_id={"row": xs[dx] * 4 + zr, "col": c}, device_id_type=MESH,
            ).start()

    def step(i, carry):
        to_all(i, False)
        return carry

    lax.fori_loop(0, 7, step, 0)
    to_all(7, True)
    keep = pltpu.make_async_copy(sp.at[col * 16 + zl * 4 + x], rp.at[mode], in_sems.at[4])
    keep.start()
    for c in late:
        c.start()
    for c in sides:
        c.wait_recv()
    line = lax.broadcasted_iota(jnp.int32, (8, 256), 0)
    for side in range(2):
        for n in range(N_SEND):
            value = jnp.zeros((8, 256), f32)
            for xx in range(4):
                value = jnp.where(line == xx + 1, yin[side, n, xx : xx + 1, :], value)
            for end in range(2):
                if n >= 5 or n == end:
                    at = n - 5 if n >= 5 else N_AUX
                    value = jnp.where(line == 5 * end, cin[2 * side + end, at : at + 1, :], value)
            yr[side, n] = value
    keep.wait()
    most = rp.at[pl.ds(0, 255)]
    pltpu.make_async_copy(most, most, sems.at[13]).wait()
    pot_ref[...] = dot(rp.reshape(256, 128)[...], hz_ref[...], ((0,), (0,)))

    pltpu.make_async_copy(blocks, blocks, sems.at[0]).wait()
    pltpu.make_async_copy(blocks, blocks, sems.at[6]).wait()
    pltpu.make_async_copy(most, most, sems.at[12]).wait()
    for c in sides:
        c.wait_send()


def solve(populations, concentrations, solid_mask, charge_sites):
    t = tables(64, 256, 256)
    vmem = pl.BlockSpec(memory_space=pltpu.VMEM)
    hbm = pl.BlockSpec(memory_space=pltpu.HBM)
    return pl.pallas_call(
        solve_kernel,
        out_shape=(
            jax.ShapeDtypeStruct((128, 256), f32),
            jax.ShapeDtypeStruct((N_FIELD, 4, 16, 256), f32),
            jax.ShapeDtypeStruct((2, N_SEND, 16, 256), f32),
            jax.ShapeDtypeStruct((2, N_SEND, 8, 256), f32),
        ),
        in_specs=[hbm] * 10,
        out_specs=(vmem,) * 4,
        scratch_shapes=[
            *[pltpu.VMEM(t[n].shape, f32) for n in TABLES],
            pltpu.VMEM((19, 4, 16, 256), f32),
            pltpu.VMEM((2, 4, 16, 256), f32),
            pltpu.VMEM((4, 16, 256), jnp.int32),
            pltpu.VMEM((4, 16, 256), jnp.int32),
            pltpu.VMEM((256, 1, 128), f32),
            pltpu.VMEM((2, 2, 4, 16, 1, 128), f32),
            pltpu.VMEM((2, 4, 2, 4, 4, 1, 128), f32),
            pltpu.VMEM((64, 256), f32),
            pltpu.VMEM((256, 1, 128), f32),
            pltpu.VMEM((256, 1, 128), f32),
            pltpu.VMEM((2, N_SEND, 4, 256), f32),
            pltpu.VMEM((2, N_SEND, 4, 256), f32),
            pltpu.VMEM((4, 16, 256), f32),
            pltpu.VMEM((4, 16, 256), f32),
            pltpu.SemaphoreType.DMA((14,)),
            pltpu.SemaphoreType.DMA((24,)),
            pltpu.SemaphoreType.DMA((11,)),
        ],
        compiler_params=pltpu.CompilerParams(collective_id=0, has_side_effects=True, vmem_limit_bytes=VMEM_A),
    )(
        *[
            pltpu.with_memory_space_constraint(v, pltpu.HBM)
            for v in (populations, concentrations, solid_mask, charge_sites, *[jnp.asarray(t[n]) for n in TABLES])
        ],
    )


TABLES = ("hz", "hx", "hx_ext", "hy_ext", "eig_xy", "eig_z")
VMEM_A = 32 * 2**20
VMEM_B = 24 * 2**20


def roll_z(v, shift):
    return pltpu.roll(v, shift % 256, 1)


def step_kernel(pot, field, xr, yr, out_hbm, conc_hbm, out, conc_out, sems):
    line16 = lax.broadcasted_iota(jnp.int32, (16, 256), 0)
    line8 = lax.broadcasted_iota(jnp.int32, (8, 256), 0)

    def up_y(v, beyond):
        return jnp.where(line16 == 15, beyond, pltpu.roll(v, 15, 0))

    def down_y(v, beyond):
        return jnp.where(line16 == 0, beyond, pltpu.roll(v, 1, 0))

    def forces(aux, electric):
        rho, mx, my, mz, c0, c1, opening = aux[:7]
        charge = -0.5 * ((c0 - c1) * opening)
        return rho * opening, [mx * opening, my * opening, mz * opening], [charge * e for e in electric], 1.0 / rho

    y_cells = []
    for side, dirs in enumerate((Y_LOW, Y_HIGH)):
        p = pot[96 + 8 * side : 104 + 8 * side, :]
        inner = jnp.zeros((8, 256), f32)
        for n in range(6):
            inner = jnp.where(line8 == n, pot[n * 16 + 15 * side : n * 16 + 15 * side + 1, :], inner)
        aux = [yr[side, 5 + n] for n in range(N_AUX)]
        left, right = pltpu.roll(p, 1, 0), pltpu.roll(p, 7, 0)
        front, back = roll_z(p, -1), roll_z(p, 1)
        rest = (6.0 + SCREEN) * p - aux[7] - inner - front - back
        given = jnp.where(line8 == 0, p[6:7, :], p[7:8, :])
        corner = (line8 == 0) | (line8 == 5)
        outer = jnp.where(corner, given, rest - left - right)
        left_all = jnp.where(line8 == 0, rest - right - outer, left)
        right_all = jnp.where(line8 == 5, rest - left - outer, right)
        along_y = inner - outer if side == 0 else outer - inner
        rho, m, force, inverse = forces(aux, (right_all - left_all, along_y, front - back))
        part = force_part(rho, m, force, inverse, dirs)
        moved = {d: roll_z(yr[side, n] + part[d], int(VELOCITY[d, 2])) for n, d in enumerate(dirs)}
        speed = aux[2] / aux[0]
        y_cells.append((p, moved, aux[4], aux[5], speed))

    planes = [pot[n * 16 : (n + 1) * 16, :] for n in range(6)]
    p_below = y_cells[0][0]
    p_above = y_cells[1][0]

    def aux_of(s):
        if s == -1:
            return [xr[0, n] for n in range(N_AUX)]
        if s == 4:
            return [xr[1, AUX + n] for n in range(N_AUX)]
        return [field[AUX + n, s] for n in range(N_AUX)]

    def base_of(d, s):
        if s == -1:
            return xr[0, SLOT[d] - AUX]
        if s == 4:
            return xr[1, SLOT[d]]
        return field[SLOT[d], s]

    def face(low, high, n):
        total = low[n] + high[n]
        return 0.25 * (low[2] + high[2]) * total - DIFFUSIVITY[n] * (
            (high[n] - low[n]) + (VALENCE[n] * 0.5) * total * (high[3] - low[3])
        )

    copies = []
    before = None
    for s in range(-1, 5):
        p = planes[s + 1]
        y_up, y_down = up_y(p, p_above[s + 1 : s + 2, :]), down_y(p, p_below[s + 1 : s + 2, :])
        front, back = roll_z(p, -1), roll_z(p, 1)
        aux = aux_of(s)
        if s == -1:
            right = planes[1]
            left = (6.0 + SCREEN) * p - aux[7] - right - y_up - y_down - front - back
            dirs = PLUS_X
        elif s == 4:
            left = planes[4]
            right = (6.0 + SCREEN) * p - aux[7] - left - y_up - y_down - front - back
            dirs = MINUS_X
        else:
            left, right = planes[s], planes[s + 2]
            dirs = [d for d in range(19) if 0 <= s + VELOCITY[d, 0] <= 3]
        rho, m, force, inverse = forces(aux, (right - left, y_up - y_down, front - back))
        part = force_part(rho, m, force, inverse, dirs)
        for d in dirs:
            cx, cy, cz = (int(n) for n in VELOCITY[d])
            v = base_of(d, s) + part[d]
            if cz:
                v = roll_z(v, cz)
            if cy == 1:
                v = down_y(v, y_cells[0][1][d][s + 1 : s + 2, :])
            elif cy == -1:
                v = up_y(v, y_cells[1][1][d][s + 1 : s + 2, :])
            out[d, s + cx] = v
        here_x = (aux[4], aux[5], aux[1] * inverse, p)
        if s >= 0:
            x_flux = [face(before[0], here_x, n) for n in range(2)]
            if s > 0:
                for n in range(2):
                    conc_out[n, s - 1] = before[1] * (before[2][n] - x_flux[n])
            if s < 4:
                uy, uz = aux[2] * inverse, aux[3] * inverse
                row = slice(s + 1, s + 2)
                here_y = (aux[4], aux[5], uy, p)
                below = tuple(down_y(v, y_cells[0][i][row, :]) for v, i in ((aux[4], 2), (aux[5], 3), (uy, 4))) + (y_down,)
                above = tuple(up_y(v, y_cells[1][i][row, :]) for v, i in ((aux[4], 2), (aux[5], 3), (uy, 4))) + (y_up,)
                here_z = (aux[4], aux[5], uz, p)
                ahead = tuple(roll_z(v, -1) for v in here_z[:3]) + (front,)
                rest = []
                for n in range(2):
                    z_flux = face(here_z, ahead, n)
                    change = face(here_y, above, n) - face(below, here_y, n) + (z_flux - roll_z(z_flux, 1))
                    rest.append(aux[4 + n] - change + x_flux[n])
                before = (here_x, aux[6], rest)
        else:
            before = (here_x,)
        if s >= 1:
            copies.append(pltpu.make_async_copy(out.at[:, s - 1], out_hbm.at[:, s - 1], sems.at[s - 1]))
            copies[-1].start()
    copies.append(pltpu.make_async_copy(conc_out, conc_hbm, sems.at[4]))
    copies[-1].start()
    for c in copies:
        c.wait()


def finish(pot, field, xr, yr):
    vmem = pl.BlockSpec(memory_space=pltpu.VMEM)
    hbm = pl.BlockSpec(memory_space=pl.ANY)
    return pl.pallas_call(
        step_kernel,
        out_shape=(jax.ShapeDtypeStruct((19, 4, 16, 256), f32), jax.ShapeDtypeStruct((2, 4, 16, 256), f32)),
        in_specs=[vmem] * 4,
        out_specs=(hbm, hbm),
        scratch_shapes=[
            pltpu.VMEM((19, 4, 16, 256), f32),
            pltpu.VMEM((2, 4, 16, 256), f32),
            pltpu.SemaphoreType.DMA((5,)),
        ],
        compiler_params=pltpu.CompilerParams(vmem_limit_bytes=VMEM_B),
    )(pot, field, xr, yr)


def per_device(populations, concentrations, solid_mask, charge_sites):
    return finish(*solve(populations, concentrations, solid_mask, charge_sites))


def solution(mesh):
    placed = (P(None, "row", "col", None), P(None, "row", "col", None), P("row", "col", None), P("row", "col", None))
    return jax.shard_map(
        per_device, mesh=mesh, in_specs=placed, out_specs=(P(None, "row", "col", None),) * 2, check_vma=False
    )
```

```python
import functools
import math

import jax
import jax.numpy as jnp
import numpy as np
from jax import lax
from jax.experimental import pallas as pl
from jax.experimental.pallas import tpu as pltpu
from jax.sharding import PartitionSpec as P

DEBYE = 32
SCREEN = 1.0 / (DEBYE * DEBYE)
MESH = pl.DeviceIdType.MESH
HIGHEST = lax.Precision.HIGHEST
f32 = jnp.float32

VELOCITY = np.array(
    [[0, 0, 0], [1, 0, 0], [-1, 0, 0], [0, 1, 0], [0, -1, 0], [0, 0, 1], [0, 0, -1],
     [1, 1, 0], [-1, -1, 0], [1, -1, 0], [-1, 1, 0], [1, 0, 1], [-1, 0, -1], [1, 0, -1],
     [-1, 0, 1], [0, 1, 1], [0, -1, -1], [0, 1, -1], [0, -1, 1]]
)
OPPOSITE = [0, 2, 1, 4, 3, 6, 5, 8, 7, 10, 9, 12, 11, 14, 13, 16, 15, 18, 17]
WEIGHT = np.array([1.0 / 3.0] + [1.0 / 18.0] * 6 + [1.0 / 36.0] * 12)
SITE_CHARGE = 1.5
DIFFUSIVITY = (0.12, 0.08)
VALENCE = (1.0, -1.0)

MINUS_X = [2, 8, 10, 12, 14]
PLUS_X = [1, 7, 9, 11, 13]
REST = [0, 3, 4, 5, 6, 15, 16, 17, 18]
SLOT = {d: i for i, d in enumerate(MINUS_X)}
SLOT.update({d: 13 + i for i, d in enumerate(PLUS_X)})
SLOT.update({d: 18 + i for i, d in enumerate(REST)})
AUX = 5
N_AUX = 8
N_FIELD = 27
N_SEND = 13
Y_LOW = [7, 10, 3, 15, 17]
Y_HIGH = [9, 8, 4, 16, 18]


def collision_matrices():
    v = VELOCITY.astype(np.float64)
    x, y, z = v[:, 0], v[:, 1], v[:, 2]
    q = x * x + y * y + z * z
    rows = [
        np.ones(19), 19 * q - 30, (21 * q * q - 53 * q + 24) / 2,
        x, (5 * q - 9) * x, y, (5 * q - 9) * y, z, (5 * q - 9) * z,
        3 * x * x - q, (3 * q - 5) * (3 * x * x - q), y * y - z * z, (3 * q - 5) * (y * y - z * z),
        x * y, y * z, x * z, (y * y - z * z) * x, (z * z - x * x) * y, (x * x - y * y) * z,
    ]
    m = np.stack(rows)
    rates = np.array([0, 1.19, 1.4, 0, 1.2, 0, 1.2, 0, 1.2, 1.25, 1.4, 1.25, 1.4, 1.25, 1.25, 1.25, 1.98, 1.98, 1.98])
    inverse = m.T / np.sum(m * m, axis=1)[None, :]
    return (inverse * rates) @ m, (inverse * (1 - rates / 2)) @ m


K, G = collision_matrices()


def even_vector(f0=0.0, axis=(0, 0, 0), plane=(0, 0, 0)):
    out = np.zeros(19)
    out[0] = f0
    for i in range(1, 19):
        c = VELOCITY[i]
        if np.abs(c).sum() == 1:
            out[i] = axis[int(np.argmax(np.abs(c)))]
        else:
            out[i] = plane[int(np.argmin(np.abs(c)))]
    return out


def relax_coefficients():
    left = np.eye(19) - K
    r0 = left @ even_vector(f0=1.0)
    ra = left @ even_vector(axis=(0.5, 0, 0))
    rp = left @ even_vector(plane=(0.25, 0, 0))
    x_axis, y_axis, yz, xy = 1, 3, 15, 7
    even = {
        "rest": (r0[0], ra[0], rp[0]),
        "axis": (r0[x_axis], ra[y_axis], rp[y_axis], ra[x_axis] - ra[y_axis], rp[x_axis] - rp[y_axis]),
        "plane": (r0[xy], ra[xy], rp[xy], ra[yz] - ra[xy], rp[yz] - rp[xy]),
    }
    h = np.zeros(19)
    h[[7, 8]], h[[9, 10]] = 0.25, -0.25
    even["shear"] = (left @ h)[7]
    d = np.zeros(19)
    d[1], d[2] = 0.5, -0.5
    od = left @ d
    e = np.zeros(19)
    e[[7, 9]], e[[8, 10]] = 0.25, -0.25
    oe = left @ e
    odd = {"axis": (od[1], oe[1]), "plane": (od[7], oe[7], oe[11])}
    return even, odd


def force_coefficients():
    c = VELOCITY.astype(np.float64)

    def quad(t):
        return WEIGHT * (4.5 * np.einsum("ia,ab,ib->i", c, t, c) - 1.5 * np.trace(t))

    t = np.zeros((3, 3))
    t[0, 0] = 1.0
    qa, qb = K @ quad(t), G @ quad(t)
    qr = K @ WEIGHT
    s = np.zeros((3, 3))
    s[0, 1] = s[1, 0] = 1.0
    sa, sb = K @ quad(s), G @ quad(s)
    lj = K @ (WEIGHT * 3 * c[:, 0])
    lf = G @ (WEIGHT * 3 * c[:, 0])
    return {
        "rest": (qa[0], qb[0], qr[0]),
        "axis_trace": (qa[3], qb[3], qr[3]),
        "axis": (qa[1] - qa[3], qb[1] - qb[3]),
        "plane_trace": (qa[7], qb[7], qr[7]),
        "plane": (qa[15] - qa[7], qb[15] - qb[7]),
        "shear": (sa[7], sb[7]),
        "odd_axis": (lj[1], lf[1]),
        "odd_plane": (lj[7], lf[7]),
    }


EVEN, ODD = relax_coefficients()
FORCE = force_coefficients()
PLANES = {0: (15, 17, 1, 2), 1: (11, 13, 0, 2), 2: (7, 9, 0, 1)}


def fl(v):
    return np.float32(v)


def moments_of(f):
    pair = {i: f[i] + f[i + 1] for i in range(1, 19, 2)}
    diff = {i: f[i] - f[i + 1] for i in range(1, 19, 2)}
    s = [pair[1], pair[3], pair[5]]
    g = [pair[15] + pair[17], pair[11] + pair[13], pair[7] + pair[9]]
    ts, tg = s[0] + s[1] + s[2], g[0] + g[1] + g[2]
    density = f[0] + ts + tg
    first = {p: diff[PLANES[p][0]] + diff[PLANES[p][1]] for p in range(3)}
    second = {p: diff[PLANES[p][0]] - diff[PLANES[p][1]] for p in range(3)}
    d = [diff[1], diff[3], diff[5]]
    along = [(first[2], first[1]), (second[2], first[0]), (second[1], second[0])]
    momentum = [d[a] + along[a][0] + along[a][1] for a in range(3)]
    return pair, s, g, ts, tg, density, d, along, momentum


def relaxed(f, moments):
    pair, s, g, ts, tg, _, d, along, _ = moments
    e = EVEN
    out = [None] * 19
    out[0] = fl(e["rest"][0]) * f[0] + fl(e["rest"][1]) * ts + fl(e["rest"][2]) * tg
    ca = fl(e["axis"][0]) * f[0] + fl(e["axis"][1]) * ts + fl(e["axis"][2]) * tg
    cp = fl(e["plane"][0]) * f[0] + fl(e["plane"][1]) * ts + fl(e["plane"][2]) * tg
    odd_axis, odd_plane = [], []
    for a in range(3):
        u, w = along[a]
        odd_axis.append(fl(ODD["axis"][0]) * d[a] + fl(ODD["axis"][1]) * (u + w))
        b = fl(ODD["plane"][0]) * d[a]
        odd_plane.append(
            (b + fl(ODD["plane"][1]) * u + fl(ODD["plane"][2]) * w, b + fl(ODD["plane"][1]) * w + fl(ODD["plane"][2]) * u)
        )
    for a in range(3):
        even = ca + fl(e["axis"][3]) * s[a] + fl(e["axis"][4]) * g[a]
        out[1 + 2 * a] = even + odd_axis[a]
        out[2 + 2 * a] = even - odd_axis[a]
    parts = {
        2: (odd_plane[0][0], odd_plane[1][0]),
        1: (odd_plane[0][1], odd_plane[2][0]),
        0: (odd_plane[1][1], odd_plane[2][1]),
    }
    for p in range(3):
        i, j, _, _ = PLANES[p]
        even = cp + fl(e["plane"][3]) * s[p] + fl(e["plane"][4]) * g[p]
        shear = fl(e["shear"]) * (pair[i] - pair[j])
        u, w = parts[p]
        out[i], out[i + 1] = even + shear + (u + w), even + shear - (u + w)
        out[j], out[j + 1] = even - shear + (u - w), even - shear - (u - w)
    return out


def force_part(density, momentum, force, inverse, wanted):
    k = FORCE
    j = [momentum[a] + 0.5 * force[a] for a in range(3)]
    u = [j[a] * inverse for a in range(3)]
    aa = [j[a] * u[a] for a in range(3)]
    bb = [2.0 * (u[a] * force[a]) for a in range(3)]
    ta, tb = aa[0] + aa[1] + aa[2], bb[0] + bb[1] + bb[2]
    out = {}
    if 0 in wanted:
        out[0] = fl(k["rest"][0]) * ta + fl(k["rest"][1]) * tb + fl(k["rest"][2]) * density
    axis_common = fl(k["axis_trace"][0]) * ta + fl(k["axis_trace"][1]) * tb + fl(k["axis_trace"][2]) * density
    plane_common = fl(k["plane_trace"][0]) * ta + fl(k["plane_trace"][1]) * tb + fl(k["plane_trace"][2]) * density
    odd_plane = [fl(k["odd_plane"][0]) * j[a] + fl(k["odd_plane"][1]) * force[a] for a in range(3)]
    for a in range(3):
        ids = (1 + 2 * a, 2 + 2 * a)
        if not any(i in wanted for i in ids):
            continue
        even = axis_common + fl(k["axis"][0]) * aa[a] + fl(k["axis"][1]) * bb[a]
        odd = fl(k["odd_axis"][0]) * j[a] + fl(k["odd_axis"][1]) * force[a]
        if ids[0] in wanted:
            out[ids[0]] = even + odd
        if ids[1] in wanted:
            out[ids[1]] = even - odd
    for p in range(3):
        i1, i2, a, b = PLANES[p]
        if not any(i in wanted for i in (i1, i1 + 1, i2, i2 + 1)):
            continue
        even = plane_common + fl(k["plane"][0]) * aa[p] + fl(k["plane"][1]) * bb[p]
        shear = fl(k["shear"][0]) * (j[a] * u[b]) + fl(k["shear"][1]) * (u[a] * force[b] + u[b] * force[a])
        up, down = even + shear, even - shear
        total, apart = odd_plane[a] + odd_plane[b], odd_plane[a] - odd_plane[b]
        for i, v in ((i1, (up, total)), (i2, (down, apart))):
            if i in wanted:
                out[i] = v[0] + v[1]
            if i + 1 in wanted:
                out[i + 1] = v[0] - v[1]
    return out


def cas(rows, columns, length):
    angle = 2 * np.pi * (np.outer(rows, columns) % length) / length
    return (np.cos(angle) + np.sin(angle)).astype(np.float32)


def eigen(length):
    return 2.0 - 2.0 * np.cos(2 * np.pi * np.arange(length) / length)


def tables(nx, ny, nz):
    r = np.array([x * 4 + zl for zl in range(4) for x in range(4)])
    own_rows = np.concatenate([4 * r + xi for xi in range(4)])
    ext_rows = np.concatenate([4 * r + xx for xx in range(-1, 5)])
    c = np.arange(16)
    low = np.stack([16 * c - 1] * 6 + [16 * c - 2] * 2, axis=1).reshape(-1)
    high = np.stack([16 * c + 16] * 6 + [16 * c + 17] * 2, axis=1).reshape(-1)
    return {
        "hz": cas(np.arange(nz), np.arange(nz), nz),
        "hx": cas(np.arange(nx), own_rows % nx, nx),
        "hx_ext": cas(ext_rows % nx, np.arange(nx), nx),
        "hy_ext": cas(np.arange(ny), np.concatenate([np.arange(ny), low % ny, high % ny]), ny),
        "eig_xy": (eigen(nx)[:, None] + eigen(ny)[None, :] + SCREEN).astype(np.float32),
        "eig_z": np.broadcast_to(eigen(nz).astype(np.float32)[:, None], (nz, 128)).copy(),
    }


def near(d):
    return min(d, 4 - d)


STEPS = sorted(
    [(dx, dy, dk) for dx in range(4) for dy in range(4) for dk in range(2)],
    key=lambda t: -(near(t[0]) + near(t[1])) * 10 - t[2],
)


def dot(a, b, contract=((1,), (0,))):
    return lax.dot_general(a, b, (contract, ((), ())), precision=HIGHEST, preferred_element_type=f32)


def solve_kernel(
    pops_hbm, conc_hbm, solid_hbm, sites_hbm, hz_hbm, hx_hbm, hxe_hbm, hye_hbm, exy_hbm, ez_hbm,
    pot_ref, field, xr, yr,
    hz_ref, hx_ref, hxe_ref, hye_ref, exy_ref, ez_ref,
    pops, conc, solid, sites, sa, ra, rb, grid, sp, rp, ys, yin, cs, cin, sems, side_sems, in_sems,
):
    row, col = lax.axis_index("row"), lax.axis_index("col")
    x, zl = row // 4, lax.rem(row, 4)
    zh, y, k = col // 8, lax.rem(col // 2, 4), lax.rem(col, 2)
    z = zh * 4 + zl
    plane = y * 4 + x
    depth = z * 2 + k
    mode = depth * 16 + plane

    loads = [
        pltpu.make_async_copy(conc_hbm, conc, in_sems.at[0]),
        pltpu.make_async_copy(solid_hbm, solid, in_sems.at[1]),
        pltpu.make_async_copy(sites_hbm, sites, in_sems.at[2]),
        pltpu.make_async_copy(hz_hbm, hz_ref, in_sems.at[5]),
        pltpu.make_async_copy(pops_hbm, pops, in_sems.at[3]),
        pltpu.make_async_copy(exy_hbm, exy_ref, in_sems.at[6]),
        pltpu.make_async_copy(ez_hbm, ez_ref, in_sems.at[7]),
        pltpu.make_async_copy(hx_hbm, hx_ref, in_sems.at[8]),
        pltpu.make_async_copy(hxe_hbm, hxe_ref, in_sems.at[9]),
        pltpu.make_async_copy(hye_hbm, hye_ref, in_sems.at[10]),
    ]

    barrier = pltpu.get_barrier_semaphore()
    xs = [lax.rem(x + d, 4) for d in range(4)]
    yy = [lax.rem(y + d, 4) for d in range(4)]
    plane_peers = [(dx, dy) for dx in range(4) for dy in range(4) if (dx, dy) != (0, 0)]
    plane_peers.sort(key=lambda t: -(near(t[0]) + near(t[1])))
    depth_peers = [(dz, dk) for dz in (4, 3, 5, 2, 6, 1, 7, 0) for dk in (1, 0) if (dz, dk) != (0, 0)]
    row_up, row_down = lax.rem(row + 1, 16), lax.rem(row + 15, 16)
    col_up, col_down = lax.rem(col + 1, 16), lax.rem(col + 15, 16)

    def plane_id(dx, dy):
        return {"row": xs[dx] * 4 + zl, "col": zh * 8 + yy[dy] * 2 + k}

    def depth_pos(dz, dk):
        return lax.rem(z + dz, 8), (k if dk == 0 else 1 - k)

    def depth_id(dz, dk):
        zz, kk = depth_pos(dz, dk)
        return {"row": x * 4 + lax.rem(zz, 4), "col": (zz // 4) * 8 + y * 2 + kk}

    ids = [depth_id(*t) for t in depth_peers] + [plane_id(*t) for t in plane_peers]
    ids += [{"row": row_up, "col": col}, {"row": row_down, "col": col}, {"row": row, "col": col_up}, {"row": row, "col": col_down}]
    corner_ids = [{"row": r, "col": c} for c in (col_up, col_down) for r in (row_up, row_down)]
    ids += corner_ids
    for device in ids:
        pl.semaphore_signal(barrier, inc=1, device_id=device, device_id_type=MESH)
    for c in loads:
        c.start()

    for c in loads[:4]:
        c.wait()
    open_all = 1.0 - solid[...].astype(f32)
    kinds = sites[...]
    fixed = SITE_CHARGE * ((kinds == 1).astype(f32) - (kinds == 2).astype(f32))
    charge = (conc[0] - conc[1]) * open_all + fixed
    field[AUX + 4] = conc[0]
    field[AUX + 5] = conc[1]
    field[AUX + 6] = open_all
    field[AUX + 7] = charge
    flat = charge.reshape(64, 256)
    spectrum = dot(hz_ref[...], jnp.concatenate([flat, jnp.zeros((64, 256), f32)], axis=0), ((1,), (1,)))
    sa.reshape(256, 128)[...] = spectrum

    pl.semaphore_wait(barrier, len(ids))
    for t in depth_peers:
        zz, kk = depth_pos(*t)
        pltpu.make_async_remote_copy(
            sa.at[pl.ds((zz * 2 + kk) * 16, 16)], ra.at[zh, k, zl], sems.at[0], sems.at[1], device_id=depth_id(*t), device_id_type=MESH
        ).start()
    keep = pltpu.make_async_copy(sa.at[pl.ds(depth * 16, 16)], ra.at[zh, k, zl], in_sems.at[4])
    keep.start()

    def to_side(n, source, target, device):
        return pltpu.make_async_remote_copy(
            source, target, side_sems.at[2 * n], side_sems.at[2 * n + 1], device_id=device, device_id_type=MESH
        )

    up, down = {"row": row_up, "col": col}, {"row": row_down, "col": col}
    sides = [
        to_side(0, field.at[pl.ds(AUX + 4, 4), 3], xr.at[0, pl.ds(4, 4)], up),
        to_side(1, field.at[pl.ds(AUX + 4, 4), 0], xr.at[1, pl.ds(AUX + 4, 4)], down),
        to_side(2, field.at[pl.ds(AUX, 4), 3], xr.at[0, pl.ds(0, 4)], up),
        to_side(3, field.at[pl.ds(AUX, 4), 0], xr.at[1, pl.ds(AUX, 4)], down),
    ]
    for c in loads[4:]:
        c.wait()

    def before(i, carry):
        xx, part = lax.rem(3 * (i // 2), 4), pl.multiple_of(lax.rem(i, 2) * 8, 8)
        rows = pl.ds(part, 8)
        f = [pops[d, xx, rows, :] for d in range(19)]
        moments = moments_of(f)
        field[AUX, xx, rows, :] = moments[5]
        for a in range(3):
            field[AUX + 1 + a, xx, rows, :] = moments[8][a]
        wall = solid[xx, rows, :] == 1
        base = relaxed(f, moments)
        for d in range(19):
            field[SLOT[d], xx, rows, :] = jnp.where(wall, f[OPPOSITE[d]], base[d])
        return carry

    lax.fori_loop(0, 4, before, 0)
    late = [
        to_side(8, field.at[pl.ds(SLOT[1], 5), 3], xr.at[0, pl.ds(N_AUX, 5)], up),
        to_side(9, field.at[pl.ds(SLOT[2], 5), 0], xr.at[1, pl.ds(0, 5)], down),
    ]
    lax.fori_loop(4, 8, before, 0)
    line4 = lax.broadcasted_iota(jnp.int32, (4, 256), 0)
    for side, (edge, dirs) in enumerate(((15, Y_LOW), (0, Y_HIGH))):
        for n in range(N_SEND):
            slot = SLOT[dirs[n]] if n < 5 else AUX + n - 5
            value = field[slot, 3, edge : edge + 1, :]
            for xx in range(3):
                value = jnp.where(line4 == xx, field[slot, xx, edge : edge + 1, :], value)
            ys[side, n] = value
        for end, (xx, d) in enumerate(((3, dirs[0]), (0, dirs[1]))):
            for n in range(N_AUX):
                cs[2 * side + end, n : n + 1, :] = field[AUX + n, xx, edge : edge + 1, :]
            for n in range(N_AUX, 16):
                cs[2 * side + end, n : n + 1, :] = field[SLOT[d], xx, edge : edge + 1, :]
    sides += [to_side(10, ys.at[0], yin.at[0], {"row": row, "col": col_up}), to_side(11, ys.at[1], yin.at[1], {"row": row, "col": col_down})]
    sides += [to_side(4 + n, cs.at[n], cin.at[n], corner_ids[n]) for n in range(4)]
    for c in sides[4:]:
        c.start()

    keep.wait()
    blocks = sa.at[pl.ds(0, 240)]
    pltpu.make_async_copy(blocks, blocks, sems.at[1]).wait()
    for t in plane_peers:
        other = yy[t[1]] * 4 + xs[t[0]]
        pltpu.make_async_remote_copy(
            ra.at[:, :, :, other], rb.at[:, y, :, :, x], sems.at[6], sems.at[7], device_id=plane_id(*t), device_id_type=MESH
        ).start()
    keep = pltpu.make_async_copy(ra.at[:, :, :, plane], rb.at[:, y, :, :, x], in_sems.at[4])
    keep.start()

    for c in sides[:2]:
        c.start()
    for c in sides[2:4]:
        c.start()
    sides += late
    scale = 1.0 / ((exy_ref[...] + jnp.concatenate([ez_ref[pl.ds(mode, 1), :]] * 2, axis=1)) * float(64 * 256 * 256))
    keep.wait()
    pltpu.make_async_copy(blocks, blocks, sems.at[7]).wait()

    lane = lax.broadcasted_iota(jnp.int32, (16, 128), 1)
    sixteenth = lane // 16
    eighth = lane // 8
    in_eighth = lax.rem(lane, 8)
    arrived = rb.reshape(256, 128)
    for half in range(2):
        pieces = [arrived[(8 * half + j) * 16 : (8 * half + j + 1) * 16, :] for j in range(8)]
        for xi in range(4):
            acc = None
            for j in range(8):
                shift = (j - xi) * 16 % 128
                w = pltpu.roll(pieces[j], shift, 1) if shift else pieces[j]
                acc = w if acc is None else jnp.where(sixteenth == j, w, acc)
            grid[xi * 16 : (xi + 1) * 16, half * 128 : (half + 1) * 128] = acc
    g = dot(dot(hx_ref[...], grid[...]), hz_ref[...]) * scale
    out = dot(dot(hxe_ref[...], g), hye_ref[...])
    rims = []
    for base in (256, 384):
        merged = out[0:16, base : base + 128]
        for j in range(1, 8):
            r = {6: 0, 7: 5}.get(j, j)
            merged = jnp.where(in_eighth == j, out[r * 16 : (r + 1) * 16, base : base + 128], merged)
        rims.append(merged)
    send = sp.reshape(256, 128)
    for c in range(16):
        acc = None
        for xx in range(6):
            v = out[xx * 16 : (xx + 1) * 16, (c // 8) * 128 : (c // 8 + 1) * 128]
            shift = (xx - c % 8) * 16 % 128
            w = pltpu.roll(v, shift, 1) if shift else v
            acc = w if acc is None else jnp.where(sixteenth == xx, w, acc)
        for s in range(2):
            shift = (96 + 8 * s - 8 * c) % 128
            w = pltpu.roll(rims[s], shift, 1) if shift else rims[s]
            acc = jnp.where(eighth == 12 + s, w, acc)
        send[c * 16 : (c + 1) * 16, :] = acc

    ks = [k, 1 - k]

    def to_all(i, last):
        dz = 4 + (1 - 2 * lax.rem(i, 2)) * ((i + 1) // 2)
        zz = lax.rem(z + dz, 8)
        zr, zc = lax.rem(zz, 4), (zz // 4) * 8
        for dx, dy, dk in STEPS:
            if last and (dx, dy, dk) == (0, 0, 0):
                continue
            c = zc + yy[dy] * 2 + ks[dk]
            pltpu.make_async_remote_copy(
                sp.at[c * 16 + zr * 4 + xs[dx]], rp.at[mode], sems.at[12], sems.at[13],
                device_id={"row": xs[dx] * 4 + zr, "col": c}, device_id_type=MESH,
            ).start()

    def step(i, carry):
        to_all(i, False)
        return carry

    lax.fori_loop(0, 7, step, 0)
    to_all(7, True)
    keep = pltpu.make_async_copy(sp.at[col * 16 + zl * 4 + x], rp.at[mode], in_sems.at[4])
    keep.start()
    for c in late:
        c.start()
    for c in sides[4:10]:
        c.wait_recv()
    line = lax.broadcasted_iota(jnp.int32, (8, 256), 0)
    for side in range(2):
        for n in range(N_SEND):
            value = jnp.zeros((8, 256), f32)
            for xx in range(4):
                value = jnp.where(line == xx + 1, yin[side, n, xx : xx + 1, :], value)
            for end in range(2):
                if n >= 5 or n == end:
                    at = n - 5 if n >= 5 else N_AUX
                    value = jnp.where(line == 5 * end, cin[2 * side + end, at : at + 1, :], value)
            yr[side, n] = value
    keep.wait()
    most = rp.at[pl.ds(0, 255)]
    pltpu.make_async_copy(most, most, sems.at[13]).wait()
    pot_ref[...] = dot(rp.reshape(256, 128)[...], hz_ref[...], ((0,), (0,)))

    for c in sides[:4] + sides[10:]:
        c.wait_recv()
    pltpu.make_async_copy(blocks, blocks, sems.at[0]).wait()
    pltpu.make_async_copy(blocks, blocks, sems.at[6]).wait()
    pltpu.make_async_copy(most, most, sems.at[12]).wait()
    for c in sides:
        c.wait_send()


def solve(populations, concentrations, solid_mask, charge_sites):
    t = tables(64, 256, 256)
    vmem = pl.BlockSpec(memory_space=pltpu.VMEM)
    hbm = pl.BlockSpec(memory_space=pltpu.HBM)
    return pl.pallas_call(
        solve_kernel,
        out_shape=(
            jax.ShapeDtypeStruct((128, 256), f32),
            jax.ShapeDtypeStruct((N_FIELD, 4, 16, 256), f32),
            jax.ShapeDtypeStruct((2, N_SEND, 16, 256), f32),
            jax.ShapeDtypeStruct((2, N_SEND, 8, 256), f32),
        ),
        in_specs=[hbm] * 10,
        out_specs=(vmem,) * 4,
        scratch_shapes=[
            *[pltpu.VMEM(t[n].shape, f32) for n in TABLES],
            pltpu.VMEM((19, 4, 16, 256), f32),
            pltpu.VMEM((2, 4, 16, 256), f32),
            pltpu.VMEM((4, 16, 256), jnp.int32),
            pltpu.VMEM((4, 16, 256), jnp.int32),
            pltpu.VMEM((256, 1, 128), f32),
            pltpu.VMEM((2, 2, 4, 16, 1, 128), f32),
            pltpu.VMEM((2, 4, 2, 4, 4, 1, 128), f32),
            pltpu.VMEM((64, 256), f32),
            pltpu.VMEM((256, 1, 128), f32),
            pltpu.VMEM((256, 1, 128), f32),
            pltpu.VMEM((2, N_SEND, 4, 256), f32),
            pltpu.VMEM((2, N_SEND, 4, 256), f32),
            pltpu.VMEM((4, 16, 256), f32),
            pltpu.VMEM((4, 16, 256), f32),
            pltpu.SemaphoreType.DMA((14,)),
            pltpu.SemaphoreType.DMA((24,)),
            pltpu.SemaphoreType.DMA((11,)),
        ],
        compiler_params=pltpu.CompilerParams(collective_id=0, has_side_effects=True, vmem_limit_bytes=VMEM_A),
    )(
        *[
            pltpu.with_memory_space_constraint(v, pltpu.HBM)
            for v in (populations, concentrations, solid_mask, charge_sites, *[jnp.asarray(t[n]) for n in TABLES])
        ],
    )


TABLES = ("hz", "hx", "hx_ext", "hy_ext", "eig_xy", "eig_z")
VMEM_A = 32 * 2**20
VMEM_B = 24 * 2**20


def roll_z(v, shift):
    return pltpu.roll(v, shift % 256, 1)


def step_kernel(pot, field, xr, yr, out_hbm, conc_hbm, out, conc_out, sems):
    line16 = lax.broadcasted_iota(jnp.int32, (16, 256), 0)
    line8 = lax.broadcasted_iota(jnp.int32, (8, 256), 0)

    def up_y(v, beyond):
        return jnp.where(line16 == 15, beyond, pltpu.roll(v, 15, 0))

    def down_y(v, beyond):
        return jnp.where(line16 == 0, beyond, pltpu.roll(v, 1, 0))

    def forces(aux, electric):
        rho, mx, my, mz, c0, c1, opening = aux[:7]
        charge = -0.5 * ((c0 - c1) * opening)
        return rho * opening, [mx * opening, my * opening, mz * opening], [charge * e for e in electric], 1.0 / rho

    y_cells = []
    for side, dirs in enumerate((Y_LOW, Y_HIGH)):
        p = pot[96 + 8 * side : 104 + 8 * side, :]
        inner = jnp.zeros((8, 256), f32)
        for n in range(6):
            inner = jnp.where(line8 == n, pot[n * 16 + 15 * side : n * 16 + 15 * side + 1, :], inner)
        aux = [yr[side, 5 + n] for n in range(N_AUX)]
        left, right = pltpu.roll(p, 1, 0), pltpu.roll(p, 7, 0)
        front, back = roll_z(p, -1), roll_z(p, 1)
        rest = (6.0 + SCREEN) * p - aux[7] - inner - front - back
        given = jnp.where(line8 == 0, p[6:7, :], p[7:8, :])
        corner = (line8 == 0) | (line8 == 5)
        outer = jnp.where(corner, given, rest - left - right)
        left_all = jnp.where(line8 == 0, rest - right - outer, left)
        right_all = jnp.where(line8 == 5, rest - left - outer, right)
        along_y = inner - outer if side == 0 else outer - inner
        rho, m, force, inverse = forces(aux, (right_all - left_all, along_y, front - back))
        part = force_part(rho, m, force, inverse, dirs)
        moved = {d: roll_z(yr[side, n] + part[d], int(VELOCITY[d, 2])) for n, d in enumerate(dirs)}
        speed = aux[2] / aux[0]
        y_cells.append((p, moved, aux[4], aux[5], speed))

    planes = [pot[n * 16 : (n + 1) * 16, :] for n in range(6)]
    p_below = y_cells[0][0]
    p_above = y_cells[1][0]

    def aux_of(s):
        if s == -1:
            return [xr[0, n] for n in range(N_AUX)]
        if s == 4:
            return [xr[1, AUX + n] for n in range(N_AUX)]
        return [field[AUX + n, s] for n in range(N_AUX)]

    def base_of(d, s):
        if s == -1:
            return xr[0, SLOT[d] - AUX]
        if s == 4:
            return xr[1, SLOT[d]]
        return field[SLOT[d], s]

    def face(low, high, n):
        total = low[n] + high[n]
        return 0.25 * (low[2] + high[2]) * total - DIFFUSIVITY[n] * (
            (high[n] - low[n]) + (VALENCE[n] * 0.5) * total * (high[3] - low[3])
        )

    copies = []
    before = None
    for s in range(-1, 5):
        p = planes[s + 1]
        y_up, y_down = up_y(p, p_above[s + 1 : s + 2, :]), down_y(p, p_below[s + 1 : s + 2, :])
        front, back = roll_z(p, -1), roll_z(p, 1)
        aux = aux_of(s)
        if s == -1:
            right = planes[1]
            left = (6.0 + SCREEN) * p - aux[7] - right - y_up - y_down - front - back
            dirs = PLUS_X
        elif s == 4:
            left = planes[4]
            right = (6.0 + SCREEN) * p - aux[7] - left - y_up - y_down - front - back
            dirs = MINUS_X
        else:
            left, right = planes[s], planes[s + 2]
            dirs = [d for d in range(19) if 0 <= s + VELOCITY[d, 0] <= 3]
        rho, m, force, inverse = forces(aux, (right - left, y_up - y_down, front - back))
        part = force_part(rho, m, force, inverse, dirs)
        for d in dirs:
            cx, cy, cz = (int(n) for n in VELOCITY[d])
            v = base_of(d, s) + part[d]
            if cz:
                v = roll_z(v, cz)
            if cy == 1:
                v = down_y(v, y_cells[0][1][d][s + 1 : s + 2, :])
            elif cy == -1:
                v = up_y(v, y_cells[1][1][d][s + 1 : s + 2, :])
            out[d, s + cx] = v
        here_x = (aux[4], aux[5], aux[1] * inverse, p)
        if s >= 0:
            x_flux = [face(before[0], here_x, n) for n in range(2)]
            if s > 0:
                for n in range(2):
                    conc_out[n, s - 1] = before[1] * (before[2][n] - x_flux[n])
            if s < 4:
                uy, uz = aux[2] * inverse, aux[3] * inverse
                row = slice(s + 1, s + 2)
                here_y = (aux[4], aux[5], uy, p)
                below = tuple(down_y(v, y_cells[0][i][row, :]) for v, i in ((aux[4], 2), (aux[5], 3), (uy, 4))) + (y_down,)
                above = tuple(up_y(v, y_cells[1][i][row, :]) for v, i in ((aux[4], 2), (aux[5], 3), (uy, 4))) + (y_up,)
                here_z = (aux[4], aux[5], uz, p)
                ahead = tuple(roll_z(v, -1) for v in here_z[:3]) + (front,)
                rest = []
                for n in range(2):
                    z_flux = face(here_z, ahead, n)
                    change = face(here_y, above, n) - face(below, here_y, n) + (z_flux - roll_z(z_flux, 1))
                    rest.append(aux[4 + n] - change + x_flux[n])
                before = (here_x, aux[6], rest)
        else:
            before = (here_x,)
        if s >= 1:
            copies.append(pltpu.make_async_copy(out.at[:, s - 1], out_hbm.at[:, s - 1], sems.at[s - 1]))
            copies[-1].start()
    copies.append(pltpu.make_async_copy(conc_out, conc_hbm, sems.at[4]))
    copies[-1].start()
    for c in copies:
        c.wait()


def finish(pot, field, xr, yr):
    vmem = pl.BlockSpec(memory_space=pltpu.VMEM)
    hbm = pl.BlockSpec(memory_space=pl.ANY)
    return pl.pallas_call(
        step_kernel,
        out_shape=(jax.ShapeDtypeStruct((19, 4, 16, 256), f32), jax.ShapeDtypeStruct((2, 4, 16, 256), f32)),
        in_specs=[vmem] * 4,
        out_specs=(hbm, hbm),
        scratch_shapes=[
            pltpu.VMEM((19, 4, 16, 256), f32),
            pltpu.VMEM((2, 4, 16, 256), f32),
            pltpu.SemaphoreType.DMA((5,)),
        ],
        compiler_params=pltpu.CompilerParams(vmem_limit_bytes=VMEM_B),
    )(pot, field, xr, yr)


def per_device(populations, concentrations, solid_mask, charge_sites):
    return finish(*solve(populations, concentrations, solid_mask, charge_sites))


def solution(mesh):
    placed = (P(None, "row", "col", None), P(None, "row", "col", None), P("row", "col", None), P("row", "col", None))
    return jax.shard_map(
        per_device, mesh=mesh, in_specs=placed, out_specs=(P(None, "row", "col", None),) * 2, check_vma=False
    )
```

```python
import functools
import math

import jax
import jax.numpy as jnp
import numpy as np
from jax import lax
from jax.experimental import pallas as pl
from jax.experimental.pallas import tpu as pltpu
from jax.sharding import PartitionSpec as P

DEBYE = 32
SCREEN = 1.0 / (DEBYE * DEBYE)
MESH = pl.DeviceIdType.MESH
HIGHEST = lax.Precision.HIGHEST
f32 = jnp.float32

VELOCITY = np.array(
    [[0, 0, 0], [1, 0, 0], [-1, 0, 0], [0, 1, 0], [0, -1, 0], [0, 0, 1], [0, 0, -1],
     [1, 1, 0], [-1, -1, 0], [1, -1, 0], [-1, 1, 0], [1, 0, 1], [-1, 0, -1], [1, 0, -1],
     [-1, 0, 1], [0, 1, 1], [0, -1, -1], [0, 1, -1], [0, -1, 1]]
)
OPPOSITE = [0, 2, 1, 4, 3, 6, 5, 8, 7, 10, 9, 12, 11, 14, 13, 16, 15, 18, 17]
WEIGHT = np.array([1.0 / 3.0] + [1.0 / 18.0] * 6 + [1.0 / 36.0] * 12)
SITE_CHARGE = 1.5
DIFFUSIVITY = (0.12, 0.08)
VALENCE = (1.0, -1.0)

MINUS_X = [2, 8, 10, 12, 14]
PLUS_X = [1, 7, 9, 11, 13]
REST = [0, 3, 4, 5, 6, 15, 16, 17, 18]
SLOT = {d: i for i, d in enumerate(MINUS_X)}
SLOT.update({d: 13 + i for i, d in enumerate(PLUS_X)})
SLOT.update({d: 18 + i for i, d in enumerate(REST)})
AUX = 5
N_AUX = 8
N_FIELD = 27
N_SEND = 13
Y_LOW = [7, 10, 3, 15, 17]
Y_HIGH = [9, 8, 4, 16, 18]


def collision_matrices():
    v = VELOCITY.astype(np.float64)
    x, y, z = v[:, 0], v[:, 1], v[:, 2]
    q = x * x + y * y + z * z
    rows = [
        np.ones(19), 19 * q - 30, (21 * q * q - 53 * q + 24) / 2,
        x, (5 * q - 9) * x, y, (5 * q - 9) * y, z, (5 * q - 9) * z,
        3 * x * x - q, (3 * q - 5) * (3 * x * x - q), y * y - z * z, (3 * q - 5) * (y * y - z * z),
        x * y, y * z, x * z, (y * y - z * z) * x, (z * z - x * x) * y, (x * x - y * y) * z,
    ]
    m = np.stack(rows)
    rates = np.array([0, 1.19, 1.4, 0, 1.2, 0, 1.2, 0, 1.2, 1.25, 1.4, 1.25, 1.4, 1.25, 1.25, 1.25, 1.98, 1.98, 1.98])
    inverse = m.T / np.sum(m * m, axis=1)[None, :]
    return (inverse * rates) @ m, (inverse * (1 - rates / 2)) @ m


K, G = collision_matrices()


def even_vector(f0=0.0, axis=(0, 0, 0), plane=(0, 0, 0)):
    out = np.zeros(19)
    out[0] = f0
    for i in range(1, 19):
        c = VELOCITY[i]
        if np.abs(c).sum() == 1:
            out[i] = axis[int(np.argmax(np.abs(c)))]
        else:
            out[i] = plane[int(np.argmin(np.abs(c)))]
    return out


def relax_coefficients():
    left = np.eye(19) - K
    r0 = left @ even_vector(f0=1.0)
    ra = left @ even_vector(axis=(0.5, 0, 0))
    rp = left @ even_vector(plane=(0.25, 0, 0))
    x_axis, y_axis, yz, xy = 1, 3, 15, 7
    even = {
        "rest": (r0[0], ra[0], rp[0]),
        "axis": (r0[x_axis], ra[y_axis], rp[y_axis], ra[x_axis] - ra[y_axis], rp[x_axis] - rp[y_axis]),
        "plane": (r0[xy], ra[xy], rp[xy], ra[yz] - ra[xy], rp[yz] - rp[xy]),
    }
    h = np.zeros(19)
    h[[7, 8]], h[[9, 10]] = 0.25, -0.25
    even["shear"] = (left @ h)[7]
    d = np.zeros(19)
    d[1], d[2] = 0.5, -0.5
    od = left @ d
    e = np.zeros(19)
    e[[7, 9]], e[[8, 10]] = 0.25, -0.25
    oe = left @ e
    odd = {"axis": (od[1], oe[1]), "plane": (od[7], oe[7], oe[11])}
    return even, odd


def force_coefficients():
    c = VELOCITY.astype(np.float64)

    def quad(t):
        return WEIGHT * (4.5 * np.einsum("ia,ab,ib->i", c, t, c) - 1.5 * np.trace(t))

    t = np.zeros((3, 3))
    t[0, 0] = 1.0
    qa, qb = K @ quad(t), G @ quad(t)
    qr = K @ WEIGHT
    s = np.zeros((3, 3))
    s[0, 1] = s[1, 0] = 1.0
    sa, sb = K @ quad(s), G @ quad(s)
    lj = K @ (WEIGHT * 3 * c[:, 0])
    lf = G @ (WEIGHT * 3 * c[:, 0])
    return {
        "rest": (qa[0], qb[0], qr[0]),
        "axis_trace": (qa[3], qb[3], qr[3]),
        "axis": (qa[1] - qa[3], qb[1] - qb[3]),
        "plane_trace": (qa[7], qb[7], qr[7]),
        "plane": (qa[15] - qa[7], qb[15] - qb[7]),
        "shear": (sa[7], sb[7]),
        "odd_axis": (lj[1], lf[1]),
        "odd_plane": (lj[7], lf[7]),
    }


EVEN, ODD = relax_coefficients()
FORCE = force_coefficients()
PLANES = {0: (15, 17, 1, 2), 1: (11, 13, 0, 2), 2: (7, 9, 0, 1)}


def fl(v):
    return np.float32(v)


def moments_of(f):
    pair = {i: f[i] + f[i + 1] for i in range(1, 19, 2)}
    diff = {i: f[i] - f[i + 1] for i in range(1, 19, 2)}
    s = [pair[1], pair[3], pair[5]]
    g = [pair[15] + pair[17], pair[11] + pair[13], pair[7] + pair[9]]
    ts, tg = s[0] + s[1] + s[2], g[0] + g[1] + g[2]
    density = f[0] + ts + tg
    first = {p: diff[PLANES[p][0]] + diff[PLANES[p][1]] for p in range(3)}
    second = {p: diff[PLANES[p][0]] - diff[PLANES[p][1]] for p in range(3)}
    d = [diff[1], diff[3], diff[5]]
    along = [(first[2], first[1]), (second[2], first[0]), (second[1], second[0])]
    momentum = [d[a] + along[a][0] + along[a][1] for a in range(3)]
    return pair, s, g, ts, tg, density, d, along, momentum


def relaxed(f, moments):
    pair, s, g, ts, tg, _, d, along, _ = moments
    e = EVEN
    out = [None] * 19
    out[0] = fl(e["rest"][0]) * f[0] + fl(e["rest"][1]) * ts + fl(e["rest"][2]) * tg
    ca = fl(e["axis"][0]) * f[0] + fl(e["axis"][1]) * ts + fl(e["axis"][2]) * tg
    cp = fl(e["plane"][0]) * f[0] + fl(e["plane"][1]) * ts + fl(e["plane"][2]) * tg
    odd_axis, odd_plane = [], []
    for a in range(3):
        u, w = along[a]
        odd_axis.append(fl(ODD["axis"][0]) * d[a] + fl(ODD["axis"][1]) * (u + w))
        b = fl(ODD["plane"][0]) * d[a]
        odd_plane.append(
            (b + fl(ODD["plane"][1]) * u + fl(ODD["plane"][2]) * w, b + fl(ODD["plane"][1]) * w + fl(ODD["plane"][2]) * u)
        )
    for a in range(3):
        even = ca + fl(e["axis"][3]) * s[a] + fl(e["axis"][4]) * g[a]
        out[1 + 2 * a] = even + odd_axis[a]
        out[2 + 2 * a] = even - odd_axis[a]
    parts = {
        2: (odd_plane[0][0], odd_plane[1][0]),
        1: (odd_plane[0][1], odd_plane[2][0]),
        0: (odd_plane[1][1], odd_plane[2][1]),
    }
    for p in range(3):
        i, j, _, _ = PLANES[p]
        even = cp + fl(e["plane"][3]) * s[p] + fl(e["plane"][4]) * g[p]
        shear = fl(e["shear"]) * (pair[i] - pair[j])
        u, w = parts[p]
        out[i], out[i + 1] = even + shear + (u + w), even + shear - (u + w)
        out[j], out[j + 1] = even - shear + (u - w), even - shear - (u - w)
    return out


def force_part(density, momentum, force, inverse, wanted):
    k = FORCE
    j = [momentum[a] + 0.5 * force[a] for a in range(3)]
    u = [j[a] * inverse for a in range(3)]
    aa = [j[a] * u[a] for a in range(3)]
    bb = [2.0 * (u[a] * force[a]) for a in range(3)]
    ta, tb = aa[0] + aa[1] + aa[2], bb[0] + bb[1] + bb[2]
    out = {}
    if 0 in wanted:
        out[0] = fl(k["rest"][0]) * ta + fl(k["rest"][1]) * tb + fl(k["rest"][2]) * density
    axis_common = fl(k["axis_trace"][0]) * ta + fl(k["axis_trace"][1]) * tb + fl(k["axis_trace"][2]) * density
    plane_common = fl(k["plane_trace"][0]) * ta + fl(k["plane_trace"][1]) * tb + fl(k["plane_trace"][2]) * density
    odd_plane = [fl(k["odd_plane"][0]) * j[a] + fl(k["odd_plane"][1]) * force[a] for a in range(3)]
    for a in range(3):
        ids = (1 + 2 * a, 2 + 2 * a)
        if not any(i in wanted for i in ids):
            continue
        even = axis_common + fl(k["axis"][0]) * aa[a] + fl(k["axis"][1]) * bb[a]
        odd = fl(k["odd_axis"][0]) * j[a] + fl(k["odd_axis"][1]) * force[a]
        if ids[0] in wanted:
            out[ids[0]] = even + odd
        if ids[1] in wanted:
            out[ids[1]] = even - odd
    for p in range(3):
        i1, i2, a, b = PLANES[p]
        if not any(i in wanted for i in (i1, i1 + 1, i2, i2 + 1)):
            continue
        even = plane_common + fl(k["plane"][0]) * aa[p] + fl(k["plane"][1]) * bb[p]
        shear = fl(k["shear"][0]) * (j[a] * u[b]) + fl(k["shear"][1]) * (u[a] * force[b] + u[b] * force[a])
        up, down = even + shear, even - shear
        total, apart = odd_plane[a] + odd_plane[b], odd_plane[a] - odd_plane[b]
        for i, v in ((i1, (up, total)), (i2, (down, apart))):
            if i in wanted:
                out[i] = v[0] + v[1]
            if i + 1 in wanted:
                out[i + 1] = v[0] - v[1]
    return out


def cas(rows, columns, length):
    angle = 2 * np.pi * (np.outer(rows, columns) % length) / length
    return (np.cos(angle) + np.sin(angle)).astype(np.float32)


def eigen(length):
    return 2.0 - 2.0 * np.cos(2 * np.pi * np.arange(length) / length)


def tables(nx, ny, nz):
    r = np.array([x * 4 + zl for zl in range(4) for x in range(4)])
    own_rows = np.concatenate([4 * r + xi for xi in range(4)])
    ext_rows = np.concatenate([4 * r + xx for xx in range(-1, 5)])
    c = np.arange(16)
    low = np.stack([16 * c - 1] * 6 + [16 * c - 2] * 2, axis=1).reshape(-1)
    high = np.stack([16 * c + 16] * 6 + [16 * c + 17] * 2, axis=1).reshape(-1)
    return {
        "hz": cas(np.arange(nz), np.arange(nz), nz),
        "hx": cas(np.arange(nx), own_rows % nx, nx),
        "hx_ext": cas(ext_rows % nx, np.arange(nx), nx),
        "hy_ext": cas(np.arange(ny), np.concatenate([np.arange(ny), low % ny, high % ny]), ny),
        "eig_xy": (eigen(nx)[:, None] + eigen(ny)[None, :] + SCREEN).astype(np.float32),
        "eig_z": np.broadcast_to(eigen(nz).astype(np.float32)[:, None], (nz, 128)).copy(),
    }


def near(d):
    return min(d, 4 - d)


STEPS = sorted(
    [(dx, dy, dk) for dx in range(4) for dy in range(4) for dk in range(2)],
    key=lambda t: -(near(t[0]) + near(t[1])) * 10 - t[2],
)


def dot(a, b, contract=((1,), (0,))):
    return lax.dot_general(a, b, (contract, ((), ())), precision=HIGHEST, preferred_element_type=f32)


def solve_kernel(
    pops_hbm, conc_hbm, solid_hbm, sites_hbm, hz_hbm, hx_hbm, hxe_hbm, hye_hbm, exy_hbm, ez_hbm,
    pot_ref, field, xr, yr,
    hz_ref, hx_ref, hxe_ref, hye_ref, exy_ref, ez_ref,
    pops, conc, solid, sites, sa, ra, rb, grid, sp, rp, ys, yin, cs, cin, sems, side_sems, in_sems,
):
    row, col = lax.axis_index("row"), lax.axis_index("col")
    x, zl = row // 4, lax.rem(row, 4)
    zh, y, k = col // 8, lax.rem(col // 2, 4), lax.rem(col, 2)
    z = zh * 4 + zl
    plane = y * 4 + x
    depth = z * 2 + k
    mode = depth * 16 + plane

    loads = [
        pltpu.make_async_copy(conc_hbm, conc, in_sems.at[0]),
        pltpu.make_async_copy(solid_hbm, solid, in_sems.at[1]),
        pltpu.make_async_copy(sites_hbm, sites, in_sems.at[2]),
        pltpu.make_async_copy(hz_hbm, hz_ref, in_sems.at[5]),
        pltpu.make_async_copy(pops_hbm, pops, in_sems.at[3]),
        pltpu.make_async_copy(exy_hbm, exy_ref, in_sems.at[6]),
        pltpu.make_async_copy(ez_hbm, ez_ref, in_sems.at[7]),
        pltpu.make_async_copy(hx_hbm, hx_ref, in_sems.at[8]),
        pltpu.make_async_copy(hxe_hbm, hxe_ref, in_sems.at[9]),
        pltpu.make_async_copy(hye_hbm, hye_ref, in_sems.at[10]),
    ]

    barrier = pltpu.get_barrier_semaphore()
    xs = [lax.rem(x + d, 4) for d in range(4)]
    yy = [lax.rem(y + d, 4) for d in range(4)]
    plane_peers = [(dx, dy) for dx in range(4) for dy in range(4) if (dx, dy) != (0, 0)]
    plane_peers.sort(key=lambda t: -(near(t[0]) + near(t[1])))
    depth_peers = [(dz, dk) for dz in (4, 3, 5, 2, 6, 1, 7, 0) for dk in (1, 0) if (dz, dk) != (0, 0)]
    row_up, row_down = lax.rem(row + 1, 16), lax.rem(row + 15, 16)
    col_up, col_down = lax.rem(col + 1, 16), lax.rem(col + 15, 16)

    def plane_id(dx, dy):
        return {"row": xs[dx] * 4 + zl, "col": zh * 8 + yy[dy] * 2 + k}

    def depth_pos(dz, dk):
        return lax.rem(z + dz, 8), (k if dk == 0 else 1 - k)

    def depth_id(dz, dk):
        zz, kk = depth_pos(dz, dk)
        return {"row": x * 4 + lax.rem(zz, 4), "col": (zz // 4) * 8 + y * 2 + kk}

    ids = [depth_id(*t) for t in depth_peers] + [plane_id(*t) for t in plane_peers]
    ids += [{"row": row_up, "col": col}, {"row": row_down, "col": col}, {"row": row, "col": col_up}, {"row": row, "col": col_down}]
    corner_ids = [{"row": r, "col": c} for c in (col_up, col_down) for r in (row_up, row_down)]
    ids += corner_ids
    for device in ids:
        pl.semaphore_signal(barrier, inc=1, device_id=device, device_id_type=MESH)
    for c in loads:
        c.start()

    for c in loads[:4]:
        c.wait()
    open_all = 1.0 - solid[...].astype(f32)
    kinds = sites[...]
    fixed = SITE_CHARGE * ((kinds == 1).astype(f32) - (kinds == 2).astype(f32))
    charge = (conc[0] - conc[1]) * open_all + fixed
    field[AUX + 4] = conc[0]
    field[AUX + 5] = conc[1]
    field[AUX + 6] = open_all
    field[AUX + 7] = charge
    flat = charge.reshape(64, 256)
    halves = hz_ref[...].reshape(16, 2, 8, 256)
    empty = jnp.zeros((64, 256), f32)
    spectrum = dot(halves[:, 0].reshape(128, 256), jnp.concatenate([flat, empty], axis=0), ((1,), (1,)))
    spectrum += dot(halves[:, 1].reshape(128, 256), jnp.concatenate([empty, flat], axis=0), ((1,), (1,)))
    sa.reshape(128, 128)[...] = spectrum

    pl.semaphore_wait(barrier, len(ids))
    for t in depth_peers:
        zz, kk = depth_pos(*t)
        pltpu.make_async_remote_copy(
            sa.at[pl.ds((zz * 2 + kk) * 8, 8)], ra.at[zh, k, zl], sems.at[0], sems.at[1], device_id=depth_id(*t), device_id_type=MESH
        ).start()
    keep = pltpu.make_async_copy(sa.at[pl.ds(depth * 8, 8)], ra.at[zh, k, zl], in_sems.at[4])
    keep.start()

    def to_side(n, source, target, device):
        return pltpu.make_async_remote_copy(
            source, target, side_sems.at[2 * n], side_sems.at[2 * n + 1], device_id=device, device_id_type=MESH
        )

    up, down = {"row": row_up, "col": col}, {"row": row_down, "col": col}
    sides = [
        to_side(0, field.at[pl.ds(AUX + 4, 4), 3], xr.at[0, pl.ds(4, 4)], up),
        to_side(1, field.at[pl.ds(AUX + 4, 4), 0], xr.at[1, pl.ds(AUX + 4, 4)], down),
        to_side(2, field.at[pl.ds(AUX, 4), 3], xr.at[0, pl.ds(0, 4)], up),
        to_side(3, field.at[pl.ds(AUX, 4), 0], xr.at[1, pl.ds(AUX, 4)], down),
    ]
    for c in loads[4:]:
        c.wait()

    def before(i, carry):
        xx, part = lax.rem(3 * (i // 2), 4), pl.multiple_of(lax.rem(i, 2) * 8, 8)
        rows = pl.ds(part, 8)
        f = [pops[d, xx, rows, :] for d in range(19)]
        moments = moments_of(f)
        field[AUX, xx, rows, :] = moments[5]
        for a in range(3):
            field[AUX + 1 + a, xx, rows, :] = moments[8][a]
        wall = solid[xx, rows, :] == 1
        base = relaxed(f, moments)
        for d in range(19):
            field[SLOT[d], xx, rows, :] = jnp.where(wall, f[OPPOSITE[d]], base[d])
        return carry

    lax.fori_loop(0, 4, before, 0)
    late = [
        to_side(8, field.at[pl.ds(SLOT[1], 5), 3], xr.at[0, pl.ds(N_AUX, 5)], up),
        to_side(9, field.at[pl.ds(SLOT[2], 5), 0], xr.at[1, pl.ds(0, 5)], down),
    ]
    lax.fori_loop(4, 8, before, 0)
    line4 = lax.broadcasted_iota(jnp.int32, (4, 256), 0)
    for side, (edge, dirs) in enumerate(((15, Y_LOW), (0, Y_HIGH))):
        for n in range(N_SEND):
            slot = SLOT[dirs[n]] if n < 5 else AUX + n - 5
            value = field[slot, 3, edge : edge + 1, :]
            for xx in range(3):
                value = jnp.where(line4 == xx, field[slot, xx, edge : edge + 1, :], value)
            ys[side, n] = value
        for end, (xx, d) in enumerate(((3, dirs[0]), (0, dirs[1]))):
            for n in range(N_AUX):
                cs[2 * side + end, n : n + 1, :] = field[AUX + n, xx, edge : edge + 1, :]
            for n in range(N_AUX, 16):
                cs[2 * side + end, n : n + 1, :] = field[SLOT[d], xx, edge : edge + 1, :]
    sides += [to_side(10, ys.at[0], yin.at[0], {"row": row, "col": col_up}), to_side(11, ys.at[1], yin.at[1], {"row": row, "col": col_down})]
    sides += [to_side(4 + n, cs.at[n], cin.at[n], corner_ids[n]) for n in range(4)]
    for c in sides[4:]:
        c.start()

    keep.wait()
    blocks, packed = sp.at[pl.ds(0, 240)], sa.at[pl.ds(0, 120)]
    pltpu.make_async_copy(packed, packed, sems.at[1]).wait()
    for t in plane_peers:
        other = yy[t[1]] * 4 + xs[t[0]]
        pltpu.make_async_remote_copy(
            ra.at[:, :, :, lax.rem(other, 8)], rb.at[:, y, :, :, x], sems.at[6], sems.at[7], device_id=plane_id(*t), device_id_type=MESH
        ).start()
    keep = pltpu.make_async_copy(ra.at[:, :, :, lax.rem(plane, 8)], rb.at[:, y, :, :, x], in_sems.at[4])
    keep.start()

    for c in sides[:2]:
        c.start()
    for c in sides[2:4]:
        c.start()
    sides += late
    scale = 1.0 / ((exy_ref[...] + jnp.concatenate([ez_ref[pl.ds(mode, 1), :]] * 2, axis=1)) * float(64 * 256 * 256))
    keep.wait()
    pltpu.make_async_copy(blocks, blocks, sems.at[7]).wait()

    lane = lax.broadcasted_iota(jnp.int32, (16, 128), 1)
    sixteenth = lane // 16
    eighth = lane // 8
    in_eighth = lax.rem(lane, 8)
    arrived = rb.reshape(256, 128)
    upper = jnp.broadcast_to(plane, (16, 128)) >= 8
    for half in range(2):
        pieces = [arrived[(8 * half + j) * 16 : (8 * half + j + 1) * 16, :] for j in range(8)]
        pieces = [jnp.where(upper, pltpu.roll(v, 64, 1), v) for v in pieces]
        for xi in range(4):
            acc = None
            for j in range(8):
                shift = (j - xi) * 16 % 128
                w = pltpu.roll(pieces[j], shift, 1) if shift else pieces[j]
                acc = w if acc is None else jnp.where(sixteenth == j, w, acc)
            grid[xi * 16 : (xi + 1) * 16, half * 128 : (half + 1) * 128] = acc
    g = dot(dot(hx_ref[...], grid[...]), hz_ref[...]) * scale
    out = dot(dot(hxe_ref[...], g), hye_ref[...])
    rims = []
    for base in (256, 384):
        merged = out[0:16, base : base + 128]
        for j in range(1, 8):
            r = {6: 0, 7: 5}.get(j, j)
            merged = jnp.where(in_eighth == j, out[r * 16 : (r + 1) * 16, base : base + 128], merged)
        rims.append(merged)
    send = sp.reshape(256, 128)
    for c in range(16):
        acc = None
        for xx in range(6):
            v = out[xx * 16 : (xx + 1) * 16, (c // 8) * 128 : (c // 8 + 1) * 128]
            shift = (xx - c % 8) * 16 % 128
            w = pltpu.roll(v, shift, 1) if shift else v
            acc = w if acc is None else jnp.where(sixteenth == xx, w, acc)
        for s in range(2):
            shift = (96 + 8 * s - 8 * c) % 128
            w = pltpu.roll(rims[s], shift, 1) if shift else rims[s]
            acc = jnp.where(eighth == 12 + s, w, acc)
        send[c * 16 : (c + 1) * 16, :] = acc

    ks = [k, 1 - k]

    def to_all(i, last):
        dz = 4 + (1 - 2 * lax.rem(i, 2)) * ((i + 1) // 2)
        zz = lax.rem(z + dz, 8)
        zr, zc = lax.rem(zz, 4), (zz // 4) * 8
        for dx, dy, dk in STEPS:
            if last and (dx, dy, dk) == (0, 0, 0):
                continue
            c = zc + yy[dy] * 2 + ks[dk]
            pltpu.make_async_remote_copy(
                sp.at[c * 16 + zr * 4 + xs[dx]], rp.at[mode], sems.at[12], sems.at[13],
                device_id={"row": xs[dx] * 4 + zr, "col": c}, device_id_type=MESH,
            ).start()

    def step(i, carry):
        to_all(i, False)
        return carry

    lax.fori_loop(0, 7, step, 0)
    to_all(7, True)
    keep = pltpu.make_async_copy(sp.at[col * 16 + zl * 4 + x], rp.at[mode], in_sems.at[4])
    keep.start()
    for c in late:
        c.start()
    for c in sides[4:10]:
        c.wait_recv()
    line = lax.broadcasted_iota(jnp.int32, (8, 256), 0)
    for side in range(2):
        for n in range(N_SEND):
            value = jnp.zeros((8, 256), f32)
            for xx in range(4):
                value = jnp.where(line == xx + 1, yin[side, n, xx : xx + 1, :], value)
            for end in range(2):
                if n >= 5 or n == end:
                    at = n - 5 if n >= 5 else N_AUX
                    value = jnp.where(line == 5 * end, cin[2 * side + end, at : at + 1, :], value)
            yr[side, n] = value
    keep.wait()
    most = rp.at[pl.ds(0, 255)]
    pltpu.make_async_copy(most, most, sems.at[13]).wait()
    pot_ref[...] = dot(rp.reshape(256, 128)[...], hz_ref[...], ((0,), (0,)))

    for c in sides[:4] + sides[10:]:
        c.wait_recv()
    pltpu.make_async_copy(packed, packed, sems.at[0]).wait()
    pltpu.make_async_copy(blocks, blocks, sems.at[6]).wait()
    pltpu.make_async_copy(most, most, sems.at[12]).wait()
    for c in sides:
        c.wait_send()


def solve(populations, concentrations, solid_mask, charge_sites):
    t = tables(64, 256, 256)
    vmem = pl.BlockSpec(memory_space=pltpu.VMEM)
    hbm = pl.BlockSpec(memory_space=pltpu.HBM)
    return pl.pallas_call(
        solve_kernel,
        out_shape=(
            jax.ShapeDtypeStruct((128, 256), f32),
            jax.ShapeDtypeStruct((N_FIELD, 4, 16, 256), f32),
            jax.ShapeDtypeStruct((2, N_SEND, 16, 256), f32),
            jax.ShapeDtypeStruct((2, N_SEND, 8, 256), f32),
        ),
        in_specs=[hbm] * 10,
        out_specs=(vmem,) * 4,
        scratch_shapes=[
            *[pltpu.VMEM(t[n].shape, f32) for n in TABLES],
            pltpu.VMEM((19, 4, 16, 256), f32),
            pltpu.VMEM((2, 4, 16, 256), f32),
            pltpu.VMEM((4, 16, 256), jnp.int32),
            pltpu.VMEM((4, 16, 256), jnp.int32),
            pltpu.VMEM((128, 1, 128), f32),
            pltpu.VMEM((2, 2, 4, 8, 1, 128), f32),
            pltpu.VMEM((2, 4, 2, 4, 4, 1, 128), f32),
            pltpu.VMEM((64, 256), f32),
            pltpu.VMEM((256, 1, 128), f32),
            pltpu.VMEM((256, 1, 128), f32),
            pltpu.VMEM((2, N_SEND, 4, 256), f32),
            pltpu.VMEM((2, N_SEND, 4, 256), f32),
            pltpu.VMEM((4, 16, 256), f32),
            pltpu.VMEM((4, 16, 256), f32),
            pltpu.SemaphoreType.DMA((14,)),
            pltpu.SemaphoreType.DMA((24,)),
            pltpu.SemaphoreType.DMA((11,)),
        ],
        compiler_params=pltpu.CompilerParams(collective_id=0, has_side_effects=True, vmem_limit_bytes=VMEM_A),
    )(
        *[
            pltpu.with_memory_space_constraint(v, pltpu.HBM)
            for v in (populations, concentrations, solid_mask, charge_sites, *[jnp.asarray(t[n]) for n in TABLES])
        ],
    )


TABLES = ("hz", "hx", "hx_ext", "hy_ext", "eig_xy", "eig_z")
VMEM_A = 32 * 2**20
VMEM_B = 24 * 2**20


def roll_z(v, shift):
    return pltpu.roll(v, shift % 256, 1)


def step_kernel(pot, field, xr, yr, out_hbm, conc_hbm, out, conc_out, sems):
    line16 = lax.broadcasted_iota(jnp.int32, (16, 256), 0)
    line8 = lax.broadcasted_iota(jnp.int32, (8, 256), 0)

    def up_y(v, beyond):
        return jnp.where(line16 == 15, beyond, pltpu.roll(v, 15, 0))

    def down_y(v, beyond):
        return jnp.where(line16 == 0, beyond, pltpu.roll(v, 1, 0))

    def forces(aux, electric):
        rho, mx, my, mz, c0, c1, opening = aux[:7]
        charge = -0.5 * ((c0 - c1) * opening)
        return rho * opening, [mx * opening, my * opening, mz * opening], [charge * e for e in electric], 1.0 / rho

    y_cells = []
    for side, dirs in enumerate((Y_LOW, Y_HIGH)):
        p = pot[96 + 8 * side : 104 + 8 * side, :]
        inner = jnp.zeros((8, 256), f32)
        for n in range(6):
            inner = jnp.where(line8 == n, pot[n * 16 + 15 * side : n * 16 + 15 * side + 1, :], inner)
        aux = [yr[side, 5 + n] for n in range(N_AUX)]
        left, right = pltpu.roll(p, 1, 0), pltpu.roll(p, 7, 0)
        front, back = roll_z(p, -1), roll_z(p, 1)
        rest = (6.0 + SCREEN) * p - aux[7] - inner - front - back
        given = jnp.where(line8 == 0, p[6:7, :], p[7:8, :])
        corner = (line8 == 0) | (line8 == 5)
        outer = jnp.where(corner, given, rest - left - right)
        left_all = jnp.where(line8 == 0, rest - right - outer, left)
        right_all = jnp.where(line8 == 5, rest - left - outer, right)
        along_y = inner - outer if side == 0 else outer - inner
        rho, m, force, inverse = forces(aux, (right_all - left_all, along_y, front - back))
        part = force_part(rho, m, force, inverse, dirs)
        moved = {d: roll_z(yr[side, n] + part[d], int(VELOCITY[d, 2])) for n, d in enumerate(dirs)}
        speed = aux[2] / aux[0]
        y_cells.append((p, moved, aux[4], aux[5], speed))

    planes = [pot[n * 16 : (n + 1) * 16, :] for n in range(6)]
    p_below = y_cells[0][0]
    p_above = y_cells[1][0]

    def aux_of(s):
        if s == -1:
            return [xr[0, n] for n in range(N_AUX)]
        if s == 4:
            return [xr[1, AUX + n] for n in range(N_AUX)]
        return [field[AUX + n, s] for n in range(N_AUX)]

    def base_of(d, s):
        if s == -1:
            return xr[0, SLOT[d] - AUX]
        if s == 4:
            return xr[1, SLOT[d]]
        return field[SLOT[d], s]

    def face(low, high, n):
        total = low[n] + high[n]
        return 0.25 * (low[2] + high[2]) * total - DIFFUSIVITY[n] * (
            (high[n] - low[n]) + (VALENCE[n] * 0.5) * total * (high[3] - low[3])
        )

    copies = []
    before = None
    for s in range(-1, 5):
        p = planes[s + 1]
        y_up, y_down = up_y(p, p_above[s + 1 : s + 2, :]), down_y(p, p_below[s + 1 : s + 2, :])
        front, back = roll_z(p, -1), roll_z(p, 1)
        aux = aux_of(s)
        if s == -1:
            right = planes[1]
            left = (6.0 + SCREEN) * p - aux[7] - right - y_up - y_down - front - back
            dirs = PLUS_X
        elif s == 4:
            left = planes[4]
            right = (6.0 + SCREEN) * p - aux[7] - left - y_up - y_down - front - back
            dirs = MINUS_X
        else:
            left, right = planes[s], planes[s + 2]
            dirs = [d for d in range(19) if 0 <= s + VELOCITY[d, 0] <= 3]
        rho, m, force, inverse = forces(aux, (right - left, y_up - y_down, front - back))
        part = force_part(rho, m, force, inverse, dirs)
        for d in dirs:
            cx, cy, cz = (int(n) for n in VELOCITY[d])
            v = base_of(d, s) + part[d]
            if cz:
                v = roll_z(v, cz)
            if cy == 1:
                v = down_y(v, y_cells[0][1][d][s + 1 : s + 2, :])
            elif cy == -1:
                v = up_y(v, y_cells[1][1][d][s + 1 : s + 2, :])
            out[d, s + cx] = v
        here_x = (aux[4], aux[5], aux[1] * inverse, p)
        if s >= 0:
            x_flux = [face(before[0], here_x, n) for n in range(2)]
            if s > 0:
                for n in range(2):
                    conc_out[n, s - 1] = before[1] * (before[2][n] - x_flux[n])
            if s < 4:
                uy, uz = aux[2] * inverse, aux[3] * inverse
                row = slice(s + 1, s + 2)
                here_y = (aux[4], aux[5], uy, p)
                below = tuple(down_y(v, y_cells[0][i][row, :]) for v, i in ((aux[4], 2), (aux[5], 3), (uy, 4))) + (y_down,)
                above = tuple(up_y(v, y_cells[1][i][row, :]) for v, i in ((aux[4], 2), (aux[5], 3), (uy, 4))) + (y_up,)
                here_z = (aux[4], aux[5], uz, p)
                ahead = tuple(roll_z(v, -1) for v in here_z[:3]) + (front,)
                rest = []
                for n in range(2):
                    z_flux = face(here_z, ahead, n)
                    change = face(here_y, above, n) - face(below, here_y, n) + (z_flux - roll_z(z_flux, 1))
                    rest.append(aux[4 + n] - change + x_flux[n])
                before = (here_x, aux[6], rest)
        else:
            before = (here_x,)
        if s >= 1:
            copies.append(pltpu.make_async_copy(out.at[:, s - 1], out_hbm.at[:, s - 1], sems.at[s - 1]))
            copies[-1].start()
    copies.append(pltpu.make_async_copy(conc_out, conc_hbm, sems.at[4]))
    copies[-1].start()
    for c in copies:
        c.wait()


def finish(pot, field, xr, yr):
    vmem = pl.BlockSpec(memory_space=pltpu.VMEM)
    hbm = pl.BlockSpec(memory_space=pl.ANY)
    return pl.pallas_call(
        step_kernel,
        out_shape=(jax.ShapeDtypeStruct((19, 4, 16, 256), f32), jax.ShapeDtypeStruct((2, 4, 16, 256), f32)),
        in_specs=[vmem] * 4,
        out_specs=(hbm, hbm),
        scratch_shapes=[
            pltpu.VMEM((19, 4, 16, 256), f32),
            pltpu.VMEM((2, 4, 16, 256), f32),
            pltpu.SemaphoreType.DMA((5,)),
        ],
        compiler_params=pltpu.CompilerParams(vmem_limit_bytes=VMEM_B),
    )(pot, field, xr, yr)


def per_device(populations, concentrations, solid_mask, charge_sites):
    return finish(*solve(populations, concentrations, solid_mask, charge_sites))


def solution(mesh):
    placed = (P(None, "row", "col", None), P(None, "row", "col", None), P("row", "col", None), P("row", "col", None))
    return jax.shard_map(
        per_device, mesh=mesh, in_specs=placed, out_specs=(P(None, "row", "col", None),) * 2, check_vma=False
    )
```

```python
import functools
import math

import jax
import jax.numpy as jnp
import numpy as np
from jax import lax
from jax.experimental import pallas as pl
from jax.experimental.pallas import tpu as pltpu
from jax.sharding import PartitionSpec as P

DEBYE = 32
SCREEN = 1.0 / (DEBYE * DEBYE)
MESH = pl.DeviceIdType.MESH
HIGHEST = lax.Precision.HIGHEST
f32 = jnp.float32

VELOCITY = np.array(
    [[0, 0, 0], [1, 0, 0], [-1, 0, 0], [0, 1, 0], [0, -1, 0], [0, 0, 1], [0, 0, -1],
     [1, 1, 0], [-1, -1, 0], [1, -1, 0], [-1, 1, 0], [1, 0, 1], [-1, 0, -1], [1, 0, -1],
     [-1, 0, 1], [0, 1, 1], [0, -1, -1], [0, 1, -1], [0, -1, 1]]
)
OPPOSITE = [0, 2, 1, 4, 3, 6, 5, 8, 7, 10, 9, 12, 11, 14, 13, 16, 15, 18, 17]
WEIGHT = np.array([1.0 / 3.0] + [1.0 / 18.0] * 6 + [1.0 / 36.0] * 12)
SITE_CHARGE = 1.5
DIFFUSIVITY = (0.12, 0.08)
VALENCE = (1.0, -1.0)

MINUS_X = [2, 8, 10, 12, 14]
PLUS_X = [1, 7, 9, 11, 13]
REST = [0, 3, 4, 5, 6, 15, 16, 17, 18]
SLOT = {d: i for i, d in enumerate(MINUS_X)}
SLOT.update({d: 13 + i for i, d in enumerate(PLUS_X)})
SLOT.update({d: 18 + i for i, d in enumerate(REST)})
AUX = 5
N_AUX = 8
N_FIELD = 27
N_SEND = 13
Y_LOW = [7, 10, 3, 15, 17]
Y_HIGH = [9, 8, 4, 16, 18]


def collision_matrices():
    v = VELOCITY.astype(np.float64)
    x, y, z = v[:, 0], v[:, 1], v[:, 2]
    q = x * x + y * y + z * z
    rows = [
        np.ones(19), 19 * q - 30, (21 * q * q - 53 * q + 24) / 2,
        x, (5 * q - 9) * x, y, (5 * q - 9) * y, z, (5 * q - 9) * z,
        3 * x * x - q, (3 * q - 5) * (3 * x * x - q), y * y - z * z, (3 * q - 5) * (y * y - z * z),
        x * y, y * z, x * z, (y * y - z * z) * x, (z * z - x * x) * y, (x * x - y * y) * z,
    ]
    m = np.stack(rows)
    rates = np.array([0, 1.19, 1.4, 0, 1.2, 0, 1.2, 0, 1.2, 1.25, 1.4, 1.25, 1.4, 1.25, 1.25, 1.25, 1.98, 1.98, 1.98])
    inverse = m.T / np.sum(m * m, axis=1)[None, :]
    return (inverse * rates) @ m, (inverse * (1 - rates / 2)) @ m


K, G = collision_matrices()


def even_vector(f0=0.0, axis=(0, 0, 0), plane=(0, 0, 0)):
    out = np.zeros(19)
    out[0] = f0
    for i in range(1, 19):
        c = VELOCITY[i]
        if np.abs(c).sum() == 1:
            out[i] = axis[int(np.argmax(np.abs(c)))]
        else:
            out[i] = plane[int(np.argmin(np.abs(c)))]
    return out


def relax_coefficients():
    left = np.eye(19) - K
    r0 = left @ even_vector(f0=1.0)
    ra = left @ even_vector(axis=(0.5, 0, 0))
    rp = left @ even_vector(plane=(0.25, 0, 0))
    x_axis, y_axis, yz, xy = 1, 3, 15, 7
    even = {
        "rest": (r0[0], ra[0], rp[0]),
        "axis": (r0[x_axis], ra[y_axis], rp[y_axis], ra[x_axis] - ra[y_axis], rp[x_axis] - rp[y_axis]),
        "plane": (r0[xy], ra[xy], rp[xy], ra[yz] - ra[xy], rp[yz] - rp[xy]),
    }
    h = np.zeros(19)
    h[[7, 8]], h[[9, 10]] = 0.25, -0.25
    even["shear"] = (left @ h)[7]
    d = np.zeros(19)
    d[1], d[2] = 0.5, -0.5
    od = left @ d
    e = np.zeros(19)
    e[[7, 9]], e[[8, 10]] = 0.25, -0.25
    oe = left @ e
    odd = {"axis": (od[1], oe[1]), "plane": (od[7], oe[7], oe[11])}
    return even, odd


def force_coefficients():
    c = VELOCITY.astype(np.float64)

    def quad(t):
        return WEIGHT * (4.5 * np.einsum("ia,ab,ib->i", c, t, c) - 1.5 * np.trace(t))

    t = np.zeros((3, 3))
    t[0, 0] = 1.0
    qa, qb = K @ quad(t), G @ quad(t)
    qr = K @ WEIGHT
    s = np.zeros((3, 3))
    s[0, 1] = s[1, 0] = 1.0
    sa, sb = K @ quad(s), G @ quad(s)
    lj = K @ (WEIGHT * 3 * c[:, 0])
    lf = G @ (WEIGHT * 3 * c[:, 0])
    return {
        "rest": (qa[0], qb[0], qr[0]),
        "axis_trace": (qa[3], qb[3], qr[3]),
        "axis": (qa[1] - qa[3], qb[1] - qb[3]),
        "plane_trace": (qa[7], qb[7], qr[7]),
        "plane": (qa[15] - qa[7], qb[15] - qb[7]),
        "shear": (sa[7], sb[7]),
        "odd_axis": (lj[1], lf[1]),
        "odd_plane": (lj[7], lf[7]),
    }


EVEN, ODD = relax_coefficients()
FORCE = force_coefficients()
PLANES = {0: (15, 17, 1, 2), 1: (11, 13, 0, 2), 2: (7, 9, 0, 1)}


def fl(v):
    return np.float32(v)


def moments_of(f):
    pair = {i: f[i] + f[i + 1] for i in range(1, 19, 2)}
    diff = {i: f[i] - f[i + 1] for i in range(1, 19, 2)}
    s = [pair[1], pair[3], pair[5]]
    g = [pair[15] + pair[17], pair[11] + pair[13], pair[7] + pair[9]]
    ts, tg = s[0] + s[1] + s[2], g[0] + g[1] + g[2]
    density = f[0] + ts + tg
    first = {p: diff[PLANES[p][0]] + diff[PLANES[p][1]] for p in range(3)}
    second = {p: diff[PLANES[p][0]] - diff[PLANES[p][1]] for p in range(3)}
    d = [diff[1], diff[3], diff[5]]
    along = [(first[2], first[1]), (second[2], first[0]), (second[1], second[0])]
    momentum = [d[a] + along[a][0] + along[a][1] for a in range(3)]
    return pair, s, g, ts, tg, density, d, along, momentum


def relaxed(f, moments):
    pair, s, g, ts, tg, _, d, along, _ = moments
    e = EVEN
    out = [None] * 19
    out[0] = fl(e["rest"][0]) * f[0] + fl(e["rest"][1]) * ts + fl(e["rest"][2]) * tg
    ca = fl(e["axis"][0]) * f[0] + fl(e["axis"][1]) * ts + fl(e["axis"][2]) * tg
    cp = fl(e["plane"][0]) * f[0] + fl(e["plane"][1]) * ts + fl(e["plane"][2]) * tg
    odd_axis, odd_plane = [], []
    for a in range(3):
        u, w = along[a]
        odd_axis.append(fl(ODD["axis"][0]) * d[a] + fl(ODD["axis"][1]) * (u + w))
        b = fl(ODD["plane"][0]) * d[a]
        odd_plane.append(
            (b + fl(ODD["plane"][1]) * u + fl(ODD["plane"][2]) * w, b + fl(ODD["plane"][1]) * w + fl(ODD["plane"][2]) * u)
        )
    for a in range(3):
        even = ca + fl(e["axis"][3]) * s[a] + fl(e["axis"][4]) * g[a]
        out[1 + 2 * a] = even + odd_axis[a]
        out[2 + 2 * a] = even - odd_axis[a]
    parts = {
        2: (odd_plane[0][0], odd_plane[1][0]),
        1: (odd_plane[0][1], odd_plane[2][0]),
        0: (odd_plane[1][1], odd_plane[2][1]),
    }
    for p in range(3):
        i, j, _, _ = PLANES[p]
        even = cp + fl(e["plane"][3]) * s[p] + fl(e["plane"][4]) * g[p]
        shear = fl(e["shear"]) * (pair[i] - pair[j])
        u, w = parts[p]
        out[i], out[i + 1] = even + shear + (u + w), even + shear - (u + w)
        out[j], out[j + 1] = even - shear + (u - w), even - shear - (u - w)
    return out


def force_part(density, momentum, force, inverse, wanted):
    k = FORCE
    j = [momentum[a] + 0.5 * force[a] for a in range(3)]
    u = [j[a] * inverse for a in range(3)]
    aa = [j[a] * u[a] for a in range(3)]
    bb = [2.0 * (u[a] * force[a]) for a in range(3)]
    ta, tb = aa[0] + aa[1] + aa[2], bb[0] + bb[1] + bb[2]
    out = {}
    if 0 in wanted:
        out[0] = fl(k["rest"][0]) * ta + fl(k["rest"][1]) * tb + fl(k["rest"][2]) * density
    axis_common = fl(k["axis_trace"][0]) * ta + fl(k["axis_trace"][1]) * tb + fl(k["axis_trace"][2]) * density
    plane_common = fl(k["plane_trace"][0]) * ta + fl(k["plane_trace"][1]) * tb + fl(k["plane_trace"][2]) * density
    odd_plane = [fl(k["odd_plane"][0]) * j[a] + fl(k["odd_plane"][1]) * force[a] for a in range(3)]
    for a in range(3):
        ids = (1 + 2 * a, 2 + 2 * a)
        if not any(i in wanted for i in ids):
            continue
        even = axis_common + fl(k["axis"][0]) * aa[a] + fl(k["axis"][1]) * bb[a]
        odd = fl(k["odd_axis"][0]) * j[a] + fl(k["odd_axis"][1]) * force[a]
        if ids[0] in wanted:
            out[ids[0]] = even + odd
        if ids[1] in wanted:
            out[ids[1]] = even - odd
    for p in range(3):
        i1, i2, a, b = PLANES[p]
        if not any(i in wanted for i in (i1, i1 + 1, i2, i2 + 1)):
            continue
        even = plane_common + fl(k["plane"][0]) * aa[p] + fl(k["plane"][1]) * bb[p]
        shear = fl(k["shear"][0]) * (j[a] * u[b]) + fl(k["shear"][1]) * (u[a] * force[b] + u[b] * force[a])
        up, down = even + shear, even - shear
        total, apart = odd_plane[a] + odd_plane[b], odd_plane[a] - odd_plane[b]
        for i, v in ((i1, (up, total)), (i2, (down, apart))):
            if i in wanted:
                out[i] = v[0] + v[1]
            if i + 1 in wanted:
                out[i + 1] = v[0] - v[1]
    return out


def cas(rows, columns, length):
    angle = 2 * np.pi * (np.outer(rows, columns) % length) / length
    return (np.cos(angle) + np.sin(angle)).astype(np.float32)


def eigen(length):
    return 2.0 - 2.0 * np.cos(2 * np.pi * np.arange(length) / length)


def tables(nx, ny, nz):
    r = np.array([x * 4 + zl for zl in range(4) for x in range(4)])
    own_rows = np.concatenate([4 * r + xi for xi in range(4)])
    ext_rows = np.concatenate([4 * r + xx for xx in range(-1, 5)])
    c = np.arange(16)
    low = np.stack([16 * c - 1] * 6 + [16 * c - 2] * 2, axis=1).reshape(-1)
    high = np.stack([16 * c + 16] * 6 + [16 * c + 17] * 2, axis=1).reshape(-1)
    return {
        "hz": cas(np.arange(nz), np.arange(nz), nz),
        "hx": cas(np.arange(nx), own_rows % nx, nx),
        "hx_ext": cas(ext_rows % nx, np.arange(nx), nx),
        "hy_ext": cas(np.arange(ny), np.concatenate([np.arange(ny), low % ny, high % ny]), ny),
        "eig_xy": (eigen(nx)[:, None] + eigen(ny)[None, :] + SCREEN).astype(np.float32),
        "eig_z": np.broadcast_to(eigen(nz).astype(np.float32)[:, None], (nz, 128)).copy(),
    }


def near(d):
    return min(d, 4 - d)


def hops(dx, dy, dz):
    return near(dx) + near(dy) + min(dz, 8 - dz)


STEPS = sorted(
    [(dx, dy, dz, dk) for dz in range(8) for dx in range(4) for dy in range(4) for dk in range(2)][1:],
    key=lambda t: -hops(*t[:3]) * 10 - t[3],
)


def dot(a, b, contract=((1,), (0,))):
    return lax.dot_general(a, b, (contract, ((), ())), precision=HIGHEST, preferred_element_type=f32)


def solve_kernel(
    pops_hbm, conc_hbm, solid_hbm, sites_hbm, hz_hbm, hx_hbm, hxe_hbm, hye_hbm, exy_hbm, ez_hbm,
    pot_ref, field, xr, yr,
    hz_ref, hx_ref, hxe_ref, hye_ref, exy_ref, ez_ref,
    pops, conc, solid, sites, sa, ra, rb, grid, sp, rp, ys, yin, cs, cin, sems, side_sems, in_sems,
):
    row, col = lax.axis_index("row"), lax.axis_index("col")
    x, zl = row // 4, lax.rem(row, 4)
    zh, y, k = col // 8, lax.rem(col // 2, 4), lax.rem(col, 2)
    z = zh * 4 + zl
    plane = y * 4 + x
    depth = z * 2 + k
    mode = depth * 16 + plane

    loads = [
        pltpu.make_async_copy(conc_hbm, conc, in_sems.at[0]),
        pltpu.make_async_copy(solid_hbm, solid, in_sems.at[1]),
        pltpu.make_async_copy(sites_hbm, sites, in_sems.at[2]),
        pltpu.make_async_copy(hz_hbm, hz_ref, in_sems.at[5]),
        pltpu.make_async_copy(pops_hbm, pops, in_sems.at[3]),
        pltpu.make_async_copy(exy_hbm, exy_ref, in_sems.at[6]),
        pltpu.make_async_copy(ez_hbm, ez_ref, in_sems.at[7]),
        pltpu.make_async_copy(hx_hbm, hx_ref, in_sems.at[8]),
        pltpu.make_async_copy(hxe_hbm, hxe_ref, in_sems.at[9]),
        pltpu.make_async_copy(hye_hbm, hye_ref, in_sems.at[10]),
    ]

    barrier = pltpu.get_barrier_semaphore()
    xs = [lax.rem(x + d, 4) for d in range(4)]
    yy = [lax.rem(y + d, 4) for d in range(4)]
    plane_peers = [(dx, dy) for dx in range(4) for dy in range(4) if (dx, dy) != (0, 0)]
    plane_peers.sort(key=lambda t: -(near(t[0]) + near(t[1])))
    depth_peers = [(dz, dk) for dz in (4, 3, 5, 2, 6, 1, 7, 0) for dk in (1, 0) if (dz, dk) != (0, 0)]
    row_up, row_down = lax.rem(row + 1, 16), lax.rem(row + 15, 16)
    col_up, col_down = lax.rem(col + 1, 16), lax.rem(col + 15, 16)

    def plane_id(dx, dy):
        return {"row": xs[dx] * 4 + zl, "col": zh * 8 + yy[dy] * 2 + k}

    def depth_pos(dz, dk):
        return lax.rem(z + dz, 8), (k if dk == 0 else 1 - k)

    def depth_id(dz, dk):
        zz, kk = depth_pos(dz, dk)
        return {"row": x * 4 + lax.rem(zz, 4), "col": (zz // 4) * 8 + y * 2 + kk}

    ids = [depth_id(*t) for t in depth_peers] + [plane_id(*t) for t in plane_peers]
    ids += [{"row": row_up, "col": col}, {"row": row_down, "col": col}, {"row": row, "col": col_up}, {"row": row, "col": col_down}]
    corner_ids = [{"row": r, "col": c} for c in (col_up, col_down) for r in (row_up, row_down)]
    ids += corner_ids
    for device in ids:
        pl.semaphore_signal(barrier, inc=1, device_id=device, device_id_type=MESH)
    for c in loads:
        c.start()

    for c in loads[:4]:
        c.wait()
    open_all = 1.0 - solid[...].astype(f32)
    kinds = sites[...]
    fixed = SITE_CHARGE * ((kinds == 1).astype(f32) - (kinds == 2).astype(f32))
    charge = (conc[0] - conc[1]) * open_all + fixed
    field[AUX + 4] = conc[0]
    field[AUX + 5] = conc[1]
    field[AUX + 6] = open_all
    field[AUX + 7] = charge
    flat = charge.reshape(64, 256)
    halves = hz_ref[...].reshape(16, 2, 8, 256)
    empty = jnp.zeros((64, 256), f32)
    spectrum = dot(halves[:, 0].reshape(128, 256), jnp.concatenate([flat, empty], axis=0), ((1,), (1,)))
    spectrum += dot(halves[:, 1].reshape(128, 256), jnp.concatenate([empty, flat], axis=0), ((1,), (1,)))
    sa.reshape(128, 128)[...] = spectrum

    pl.semaphore_wait(barrier, len(ids))
    for t in depth_peers:
        zz, kk = depth_pos(*t)
        pltpu.make_async_remote_copy(
            sa.at[pl.ds((zz * 2 + kk) * 8, 8)], ra.at[zh, k, zl], sems.at[0], sems.at[1], device_id=depth_id(*t), device_id_type=MESH
        ).start()
    keep = pltpu.make_async_copy(sa.at[pl.ds(depth * 8, 8)], ra.at[zh, k, zl], in_sems.at[4])
    keep.start()

    def to_side(n, source, target, device):
        return pltpu.make_async_remote_copy(
            source, target, side_sems.at[2 * n], side_sems.at[2 * n + 1], device_id=device, device_id_type=MESH
        )

    up, down = {"row": row_up, "col": col}, {"row": row_down, "col": col}
    sides = [
        to_side(0, field.at[pl.ds(AUX + 4, 4), 3], xr.at[0, pl.ds(4, 4)], up),
        to_side(1, field.at[pl.ds(AUX + 4, 4), 0], xr.at[1, pl.ds(AUX + 4, 4)], down),
        to_side(2, field.at[pl.ds(AUX, 4), 3], xr.at[0, pl.ds(0, 4)], up),
        to_side(3, field.at[pl.ds(AUX, 4), 0], xr.at[1, pl.ds(AUX, 4)], down),
    ]
    for c in loads[4:]:
        c.wait()

    def before(i, carry):
        xx, part = lax.rem(3 * (i // 2), 4), pl.multiple_of(lax.rem(i, 2) * 8, 8)
        rows = pl.ds(part, 8)
        f = [pops[d, xx, rows, :] for d in range(19)]
        moments = moments_of(f)
        field[AUX, xx, rows, :] = moments[5]
        for a in range(3):
            field[AUX + 1 + a, xx, rows, :] = moments[8][a]
        wall = solid[xx, rows, :] == 1
        base = relaxed(f, moments)
        for d in range(19):
            field[SLOT[d], xx, rows, :] = jnp.where(wall, f[OPPOSITE[d]], base[d])
        return carry

    lax.fori_loop(0, 4, before, 0)
    late = [
        to_side(8, field.at[pl.ds(SLOT[1], 5), 3], xr.at[0, pl.ds(N_AUX, 5)], up),
        to_side(9, field.at[pl.ds(SLOT[2], 5), 0], xr.at[1, pl.ds(0, 5)], down),
    ]
    lax.fori_loop(4, 8, before, 0)
    line4 = lax.broadcasted_iota(jnp.int32, (4, 256), 0)
    for side, (edge, dirs) in enumerate(((15, Y_LOW), (0, Y_HIGH))):
        for n in range(N_SEND):
            slot = SLOT[dirs[n]] if n < 5 else AUX + n - 5
            value = field[slot, 3, edge : edge + 1, :]
            for xx in range(3):
                value = jnp.where(line4 == xx, field[slot, xx, edge : edge + 1, :], value)
            ys[side, n] = value
        for end, (xx, d) in enumerate(((3, dirs[0]), (0, dirs[1]))):
            for n in range(N_AUX):
                cs[2 * side + end, n : n + 1, :] = field[AUX + n, xx, edge : edge + 1, :]
            for n in range(N_AUX, 16):
                cs[2 * side + end, n : n + 1, :] = field[SLOT[d], xx, edge : edge + 1, :]
    sides += [to_side(10, ys.at[0], yin.at[0], {"row": row, "col": col_up}), to_side(11, ys.at[1], yin.at[1], {"row": row, "col": col_down})]
    sides += [to_side(4 + n, cs.at[n], cin.at[n], corner_ids[n]) for n in range(4)]
    for c in sides[4:]:
        c.start()

    keep.wait()
    blocks, packed = sp.at[pl.ds(0, 240)], sa.at[pl.ds(0, 120)]
    pltpu.make_async_copy(packed, packed, sems.at[1]).wait()
    for t in plane_peers:
        other = yy[t[1]] * 4 + xs[t[0]]
        pltpu.make_async_remote_copy(
            ra.at[:, :, :, lax.rem(other, 8)], rb.at[:, y, :, :, x], sems.at[6], sems.at[7], device_id=plane_id(*t), device_id_type=MESH
        ).start()
    keep = pltpu.make_async_copy(ra.at[:, :, :, lax.rem(plane, 8)], rb.at[:, y, :, :, x], in_sems.at[4])
    keep.start()

    for c in sides[:2]:
        c.start()
    for c in sides[2:4]:
        c.start()
    sides += late
    scale = 1.0 / ((exy_ref[...] + jnp.concatenate([ez_ref[pl.ds(mode, 1), :]] * 2, axis=1)) * float(64 * 256 * 256))
    keep.wait()
    pltpu.make_async_copy(blocks, blocks, sems.at[7]).wait()

    lane = lax.broadcasted_iota(jnp.int32, (16, 128), 1)
    sixteenth = lane // 16
    eighth = lane // 8
    in_eighth = lax.rem(lane, 8)
    arrived = rb.reshape(256, 128)
    upper = jnp.broadcast_to(plane, (16, 128)) >= 8
    for half in range(2):
        pieces = [arrived[(8 * half + j) * 16 : (8 * half + j + 1) * 16, :] for j in range(8)]
        pieces = [jnp.where(upper, pltpu.roll(v, 64, 1), v) for v in pieces]
        for xi in range(4):
            acc = None
            for j in range(8):
                shift = (j - xi) * 16 % 128
                w = pltpu.roll(pieces[j], shift, 1) if shift else pieces[j]
                acc = w if acc is None else jnp.where(sixteenth == j, w, acc)
            grid[xi * 16 : (xi + 1) * 16, half * 128 : (half + 1) * 128] = acc
    g = dot(dot(hx_ref[...], grid[...]), hz_ref[...]) * scale
    out = dot(dot(hxe_ref[...], g), hye_ref[...])
    rims = []
    for base in (256, 384):
        merged = out[0:16, base : base + 128]
        for j in range(1, 8):
            r = {6: 0, 7: 5}.get(j, j)
            merged = jnp.where(in_eighth == j, out[r * 16 : (r + 1) * 16, base : base + 128], merged)
        rims.append(merged)
    send = sp.reshape(256, 128)
    for c in range(16):
        acc = None
        for xx in range(6):
            v = out[xx * 16 : (xx + 1) * 16, (c // 8) * 128 : (c // 8 + 1) * 128]
            shift = (xx - c % 8) * 16 % 128
            w = pltpu.roll(v, shift, 1) if shift else v
            acc = w if acc is None else jnp.where(sixteenth == xx, w, acc)
        for s in range(2):
            shift = (96 + 8 * s - 8 * c) % 128
            w = pltpu.roll(rims[s], shift, 1) if shift else rims[s]
            acc = jnp.where(eighth == 12 + s, w, acc)
        send[c * 16 : (c + 1) * 16, :] = acc

    ks = [k, 1 - k]

    zs = [lax.rem(z + d, 8) for d in range(8)]
    x_row = [v * 4 for v in xs]
    z_row = [lax.rem(v, 4) for v in zs]
    yk_col = [[v * 2 + kk for kk in ks] for v in yy]
    z_col = [(v // 4) * 8 for v in zs]
    for n, (dx, dy, dz, dk) in enumerate(STEPS):
        c = z_col[dz] + yk_col[dy][dk]
        pltpu.make_async_remote_copy(
            sp.at[c * 16 + z_row[dz] * 4 + xs[dx]], rp.at[mode], sems.at[12], sems.at[13],
            device_id={"row": x_row[dx] + z_row[dz], "col": c}, device_id_type=MESH,
        ).start()
    keep = pltpu.make_async_copy(sp.at[col * 16 + zl * 4 + x], rp.at[mode], in_sems.at[4])
    keep.start()
    for c in late:
        c.start()
    for c in sides[4:10]:
        c.wait_recv()
    line = lax.broadcasted_iota(jnp.int32, (8, 256), 0)
    for side in range(2):
        for n in range(N_SEND):
            value = jnp.zeros((8, 256), f32)
            for xx in range(4):
                value = jnp.where(line == xx + 1, yin[side, n, xx : xx + 1, :], value)
            for end in range(2):
                if n >= 5 or n == end:
                    at = n - 5 if n >= 5 else N_AUX
                    value = jnp.where(line == 5 * end, cin[2 * side + end, at : at + 1, :], value)
            yr[side, n] = value
    keep.wait()
    most = rp.at[pl.ds(0, 255)]
    pltpu.make_async_copy(most, most, sems.at[13]).wait()
    pot_ref[...] = dot(rp.reshape(256, 128)[...], hz_ref[...], ((0,), (0,)))

    for c in sides[:4] + sides[10:]:
        c.wait_recv()
    pltpu.make_async_copy(packed, packed, sems.at[0]).wait()
    pltpu.make_async_copy(blocks, blocks, sems.at[6]).wait()
    pltpu.make_async_copy(most, most, sems.at[12]).wait()
    for c in sides:
        c.wait_send()


def solve(populations, concentrations, solid_mask, charge_sites):
    t = tables(64, 256, 256)
    vmem = pl.BlockSpec(memory_space=pltpu.VMEM)
    hbm = pl.BlockSpec(memory_space=pltpu.HBM)
    return pl.pallas_call(
        solve_kernel,
        out_shape=(
            jax.ShapeDtypeStruct((128, 256), f32),
            jax.ShapeDtypeStruct((N_FIELD, 4, 16, 256), f32),
            jax.ShapeDtypeStruct((2, N_SEND, 16, 256), f32),
            jax.ShapeDtypeStruct((2, N_SEND, 8, 256), f32),
        ),
        in_specs=[hbm] * 10,
        out_specs=(vmem,) * 4,
        scratch_shapes=[
            *[pltpu.VMEM(t[n].shape, f32) for n in TABLES],
            pltpu.VMEM((19, 4, 16, 256), f32),
            pltpu.VMEM((2, 4, 16, 256), f32),
            pltpu.VMEM((4, 16, 256), jnp.int32),
            pltpu.VMEM((4, 16, 256), jnp.int32),
            pltpu.VMEM((128, 1, 128), f32),
            pltpu.VMEM((2, 2, 4, 8, 1, 128), f32),
            pltpu.VMEM((2, 4, 2, 4, 4, 1, 128), f32),
            pltpu.VMEM((64, 256), f32),
            pltpu.VMEM((256, 1, 128), f32),
            pltpu.VMEM((256, 1, 128), f32),
            pltpu.VMEM((2, N_SEND, 4, 256), f32),
            pltpu.VMEM((2, N_SEND, 4, 256), f32),
            pltpu.VMEM((4, 16, 256), f32),
            pltpu.VMEM((4, 16, 256), f32),
            pltpu.SemaphoreType.DMA((14,)),
            pltpu.SemaphoreType.DMA((24,)),
            pltpu.SemaphoreType.DMA((11,)),
        ],
        compiler_params=pltpu.CompilerParams(collective_id=0, has_side_effects=True, vmem_limit_bytes=VMEM_A),
    )(
        *[
            pltpu.with_memory_space_constraint(v, pltpu.HBM)
            for v in (populations, concentrations, solid_mask, charge_sites, *[jnp.asarray(t[n]) for n in TABLES])
        ],
    )


TABLES = ("hz", "hx", "hx_ext", "hy_ext", "eig_xy", "eig_z")
VMEM_A = 32 * 2**20
VMEM_B = 24 * 2**20


def roll_z(v, shift):
    return pltpu.roll(v, shift % 256, 1)


def step_kernel(pot, field, xr, yr, out_hbm, conc_hbm, out, conc_out, sems):
    line16 = lax.broadcasted_iota(jnp.int32, (16, 256), 0)
    line8 = lax.broadcasted_iota(jnp.int32, (8, 256), 0)

    def up_y(v, beyond):
        return jnp.where(line16 == 15, beyond, pltpu.roll(v, 15, 0))

    def down_y(v, beyond):
        return jnp.where(line16 == 0, beyond, pltpu.roll(v, 1, 0))

    def forces(aux, electric):
        rho, mx, my, mz, c0, c1, opening = aux[:7]
        charge = -0.5 * ((c0 - c1) * opening)
        return rho * opening, [mx * opening, my * opening, mz * opening], [charge * e for e in electric], 1.0 / rho

    y_cells = []
    for side, dirs in enumerate((Y_LOW, Y_HIGH)):
        p = pot[96 + 8 * side : 104 + 8 * side, :]
        inner = jnp.zeros((8, 256), f32)
        for n in range(6):
            inner = jnp.where(line8 == n, pot[n * 16 + 15 * side : n * 16 + 15 * side + 1, :], inner)
        aux = [yr[side, 5 + n] for n in range(N_AUX)]
        left, right = pltpu.roll(p, 1, 0), pltpu.roll(p, 7, 0)
        front, back = roll_z(p, -1), roll_z(p, 1)
        rest = (6.0 + SCREEN) * p - aux[7] - inner - front - back
        given = jnp.where(line8 == 0, p[6:7, :], p[7:8, :])
        corner = (line8 == 0) | (line8 == 5)
        outer = jnp.where(corner, given, rest - left - right)
        left_all = jnp.where(line8 == 0, rest - right - outer, left)
        right_all = jnp.where(line8 == 5, rest - left - outer, right)
        along_y = inner - outer if side == 0 else outer - inner
        rho, m, force, inverse = forces(aux, (right_all - left_all, along_y, front - back))
        part = force_part(rho, m, force, inverse, dirs)
        moved = {d: roll_z(yr[side, n] + part[d], int(VELOCITY[d, 2])) for n, d in enumerate(dirs)}
        speed = aux[2] / aux[0]
        y_cells.append((p, moved, aux[4], aux[5], speed))

    planes = [pot[n * 16 : (n + 1) * 16, :] for n in range(6)]
    p_below = y_cells[0][0]
    p_above = y_cells[1][0]

    def aux_of(s):
        if s == -1:
            return [xr[0, n] for n in range(N_AUX)]
        if s == 4:
            return [xr[1, AUX + n] for n in range(N_AUX)]
        return [field[AUX + n, s] for n in range(N_AUX)]

    def base_of(d, s):
        if s == -1:
            return xr[0, SLOT[d] - AUX]
        if s == 4:
            return xr[1, SLOT[d]]
        return field[SLOT[d], s]

    def face(low, high, n):
        total = low[n] + high[n]
        return 0.25 * (low[2] + high[2]) * total - DIFFUSIVITY[n] * (
            (high[n] - low[n]) + (VALENCE[n] * 0.5) * total * (high[3] - low[3])
        )

    copies = []
    before = None
    for s in range(-1, 5):
        p = planes[s + 1]
        y_up, y_down = up_y(p, p_above[s + 1 : s + 2, :]), down_y(p, p_below[s + 1 : s + 2, :])
        front, back = roll_z(p, -1), roll_z(p, 1)
        aux = aux_of(s)
        if s == -1:
            right = planes[1]
            left = (6.0 + SCREEN) * p - aux[7] - right - y_up - y_down - front - back
            dirs = PLUS_X
        elif s == 4:
            left = planes[4]
            right = (6.0 + SCREEN) * p - aux[7] - left - y_up - y_down - front - back
            dirs = MINUS_X
        else:
            left, right = planes[s], planes[s + 2]
            dirs = [d for d in range(19) if 0 <= s + VELOCITY[d, 0] <= 3]
        rho, m, force, inverse = forces(aux, (right - left, y_up - y_down, front - back))
        part = force_part(rho, m, force, inverse, dirs)
        for d in dirs:
            cx, cy, cz = (int(n) for n in VELOCITY[d])
            v = base_of(d, s) + part[d]
            if cz:
                v = roll_z(v, cz)
            if cy == 1:
                v = down_y(v, y_cells[0][1][d][s + 1 : s + 2, :])
            elif cy == -1:
                v = up_y(v, y_cells[1][1][d][s + 1 : s + 2, :])
            out[d, s + cx] = v
        here_x = (aux[4], aux[5], aux[1] * inverse, p)
        if s >= 0:
            x_flux = [face(before[0], here_x, n) for n in range(2)]
            if s > 0:
                for n in range(2):
                    conc_out[n, s - 1] = before[1] * (before[2][n] - x_flux[n])
            if s < 4:
                uy, uz = aux[2] * inverse, aux[3] * inverse
                row = slice(s + 1, s + 2)
                here_y = (aux[4], aux[5], uy, p)
                below = tuple(down_y(v, y_cells[0][i][row, :]) for v, i in ((aux[4], 2), (aux[5], 3), (uy, 4))) + (y_down,)
                above = tuple(up_y(v, y_cells[1][i][row, :]) for v, i in ((aux[4], 2), (aux[5], 3), (uy, 4))) + (y_up,)
                here_z = (aux[4], aux[5], uz, p)
                ahead = tuple(roll_z(v, -1) for v in here_z[:3]) + (front,)
                rest = []
                for n in range(2):
                    z_flux = face(here_z, ahead, n)
                    change = face(here_y, above, n) - face(below, here_y, n) + (z_flux - roll_z(z_flux, 1))
                    rest.append(aux[4 + n] - change + x_flux[n])
                before = (here_x, aux[6], rest)
        else:
            before = (here_x,)
        if s >= 1:
            copies.append(pltpu.make_async_copy(out.at[:, s - 1], out_hbm.at[:, s - 1], sems.at[s - 1]))
            copies[-1].start()
    copies.append(pltpu.make_async_copy(conc_out, conc_hbm, sems.at[4]))
    copies[-1].start()
    for c in copies:
        c.wait()


def finish(pot, field, xr, yr):
    vmem = pl.BlockSpec(memory_space=pltpu.VMEM)
    hbm = pl.BlockSpec(memory_space=pl.ANY)
    return pl.pallas_call(
        step_kernel,
        out_shape=(jax.ShapeDtypeStruct((19, 4, 16, 256), f32), jax.ShapeDtypeStruct((2, 4, 16, 256), f32)),
        in_specs=[vmem] * 4,
        out_specs=(hbm, hbm),
        scratch_shapes=[
            pltpu.VMEM((19, 4, 16, 256), f32),
            pltpu.VMEM((2, 4, 16, 256), f32),
            pltpu.SemaphoreType.DMA((5,)),
        ],
        compiler_params=pltpu.CompilerParams(vmem_limit_bytes=VMEM_B),
    )(pot, field, xr, yr)


def per_device(populations, concentrations, solid_mask, charge_sites):
    return finish(*solve(populations, concentrations, solid_mask, charge_sites))


def solution(mesh):
    placed = (P(None, "row", "col", None), P(None, "row", "col", None), P("row", "col", None), P("row", "col", None))
    return jax.shard_map(
        per_device, mesh=mesh, in_specs=placed, out_specs=(P(None, "row", "col", None),) * 2, check_vma=False
    )
```

```python
import functools
import math

import jax
import jax.numpy as jnp
import numpy as np
from jax import lax
from jax.experimental import pallas as pl
from jax.experimental.pallas import tpu as pltpu
from jax.sharding import PartitionSpec as P

DEBYE = 32
SCREEN = 1.0 / (DEBYE * DEBYE)
MESH = pl.DeviceIdType.MESH
HIGHEST = lax.Precision.HIGHEST
f32 = jnp.float32

VELOCITY = np.array(
    [[0, 0, 0], [1, 0, 0], [-1, 0, 0], [0, 1, 0], [0, -1, 0], [0, 0, 1], [0, 0, -1],
     [1, 1, 0], [-1, -1, 0], [1, -1, 0], [-1, 1, 0], [1, 0, 1], [-1, 0, -1], [1, 0, -1],
     [-1, 0, 1], [0, 1, 1], [0, -1, -1], [0, 1, -1], [0, -1, 1]]
)
OPPOSITE = [0, 2, 1, 4, 3, 6, 5, 8, 7, 10, 9, 12, 11, 14, 13, 16, 15, 18, 17]
WEIGHT = np.array([1.0 / 3.0] + [1.0 / 18.0] * 6 + [1.0 / 36.0] * 12)
SITE_CHARGE = 1.5
DIFFUSIVITY = (0.12, 0.08)
VALENCE = (1.0, -1.0)

MINUS_X = [2, 8, 10, 12, 14]
PLUS_X = [1, 7, 9, 11, 13]
REST = [0, 3, 4, 5, 6, 15, 16, 17, 18]
SLOT = {d: i for i, d in enumerate(MINUS_X)}
SLOT.update({d: 13 + i for i, d in enumerate(PLUS_X)})
SLOT.update({d: 18 + i for i, d in enumerate(REST)})
AUX = 5
N_AUX = 8
N_FIELD = 27
N_SEND = 13
Y_LOW = [7, 10, 3, 15, 17]
Y_HIGH = [9, 8, 4, 16, 18]


def collision_matrices():
    v = VELOCITY.astype(np.float64)
    x, y, z = v[:, 0], v[:, 1], v[:, 2]
    q = x * x + y * y + z * z
    rows = [
        np.ones(19), 19 * q - 30, (21 * q * q - 53 * q + 24) / 2,
        x, (5 * q - 9) * x, y, (5 * q - 9) * y, z, (5 * q - 9) * z,
        3 * x * x - q, (3 * q - 5) * (3 * x * x - q), y * y - z * z, (3 * q - 5) * (y * y - z * z),
        x * y, y * z, x * z, (y * y - z * z) * x, (z * z - x * x) * y, (x * x - y * y) * z,
    ]
    m = np.stack(rows)
    rates = np.array([0, 1.19, 1.4, 0, 1.2, 0, 1.2, 0, 1.2, 1.25, 1.4, 1.25, 1.4, 1.25, 1.25, 1.25, 1.98, 1.98, 1.98])
    inverse = m.T / np.sum(m * m, axis=1)[None, :]
    return (inverse * rates) @ m, (inverse * (1 - rates / 2)) @ m


K, G = collision_matrices()


def even_vector(f0=0.0, axis=(0, 0, 0), plane=(0, 0, 0)):
    out = np.zeros(19)
    out[0] = f0
    for i in range(1, 19):
        c = VELOCITY[i]
        if np.abs(c).sum() == 1:
            out[i] = axis[int(np.argmax(np.abs(c)))]
        else:
            out[i] = plane[int(np.argmin(np.abs(c)))]
    return out


def relax_coefficients():
    left = np.eye(19) - K
    r0 = left @ even_vector(f0=1.0)
    ra = left @ even_vector(axis=(0.5, 0, 0))
    rp = left @ even_vector(plane=(0.25, 0, 0))
    x_axis, y_axis, yz, xy = 1, 3, 15, 7
    even = {
        "rest": (r0[0], ra[0], rp[0]),
        "axis": (r0[x_axis], ra[y_axis], rp[y_axis], ra[x_axis] - ra[y_axis], rp[x_axis] - rp[y_axis]),
        "plane": (r0[xy], ra[xy], rp[xy], ra[yz] - ra[xy], rp[yz] - rp[xy]),
    }
    h = np.zeros(19)
    h[[7, 8]], h[[9, 10]] = 0.25, -0.25
    even["shear"] = (left @ h)[7]
    d = np.zeros(19)
    d[1], d[2] = 0.5, -0.5
    od = left @ d
    e = np.zeros(19)
    e[[7, 9]], e[[8, 10]] = 0.25, -0.25
    oe = left @ e
    odd = {"axis": (od[1], oe[1]), "plane": (od[7], oe[7], oe[11])}
    return even, odd


def force_coefficients():
    c = VELOCITY.astype(np.float64)

    def quad(t):
        return WEIGHT * (4.5 * np.einsum("ia,ab,ib->i", c, t, c) - 1.5 * np.trace(t))

    t = np.zeros((3, 3))
    t[0, 0] = 1.0
    qa, qb = K @ quad(t), G @ quad(t)
    qr = K @ WEIGHT
    s = np.zeros((3, 3))
    s[0, 1] = s[1, 0] = 1.0
    sa, sb = K @ quad(s), G @ quad(s)
    lj = K @ (WEIGHT * 3 * c[:, 0])
    lf = G @ (WEIGHT * 3 * c[:, 0])
    return {
        "rest": (qa[0], qb[0], qr[0]),
        "axis_trace": (qa[3], qb[3], qr[3]),
        "axis": (qa[1] - qa[3], qb[1] - qb[3]),
        "plane_trace": (qa[7], qb[7], qr[7]),
        "plane": (qa[15] - qa[7], qb[15] - qb[7]),
        "shear": (sa[7], sb[7]),
        "odd_axis": (lj[1], lf[1]),
        "odd_plane": (lj[7], lf[7]),
    }


EVEN, ODD = relax_coefficients()
FORCE = force_coefficients()
PLANES = {0: (15, 17, 1, 2), 1: (11, 13, 0, 2), 2: (7, 9, 0, 1)}


def fl(v):
    return np.float32(v)


def moments_of(f):
    pair = {i: f[i] + f[i + 1] for i in range(1, 19, 2)}
    diff = {i: f[i] - f[i + 1] for i in range(1, 19, 2)}
    s = [pair[1], pair[3], pair[5]]
    g = [pair[15] + pair[17], pair[11] + pair[13], pair[7] + pair[9]]
    ts, tg = s[0] + s[1] + s[2], g[0] + g[1] + g[2]
    density = f[0] + ts + tg
    first = {p: diff[PLANES[p][0]] + diff[PLANES[p][1]] for p in range(3)}
    second = {p: diff[PLANES[p][0]] - diff[PLANES[p][1]] for p in range(3)}
    d = [diff[1], diff[3], diff[5]]
    along = [(first[2], first[1]), (second[2], first[0]), (second[1], second[0])]
    momentum = [d[a] + along[a][0] + along[a][1] for a in range(3)]
    return pair, s, g, ts, tg, density, d, along, momentum


def relaxed(f, moments):
    pair, s, g, ts, tg, _, d, along, _ = moments
    e = EVEN
    out = [None] * 19
    out[0] = fl(e["rest"][0]) * f[0] + fl(e["rest"][1]) * ts + fl(e["rest"][2]) * tg
    ca = fl(e["axis"][0]) * f[0] + fl(e["axis"][1]) * ts + fl(e["axis"][2]) * tg
    cp = fl(e["plane"][0]) * f[0] + fl(e["plane"][1]) * ts + fl(e["plane"][2]) * tg
    odd_axis, odd_plane = [], []
    for a in range(3):
        u, w = along[a]
        odd_axis.append(fl(ODD["axis"][0]) * d[a] + fl(ODD["axis"][1]) * (u + w))
        b = fl(ODD["plane"][0]) * d[a]
        odd_plane.append(
            (b + fl(ODD["plane"][1]) * u + fl(ODD["plane"][2]) * w, b + fl(ODD["plane"][1]) * w + fl(ODD["plane"][2]) * u)
        )
    for a in range(3):
        even = ca + fl(e["axis"][3]) * s[a] + fl(e["axis"][4]) * g[a]
        out[1 + 2 * a] = even + odd_axis[a]
        out[2 + 2 * a] = even - odd_axis[a]
    parts = {
        2: (odd_plane[0][0], odd_plane[1][0]),
        1: (odd_plane[0][1], odd_plane[2][0]),
        0: (odd_plane[1][1], odd_plane[2][1]),
    }
    for p in range(3):
        i, j, _, _ = PLANES[p]
        even = cp + fl(e["plane"][3]) * s[p] + fl(e["plane"][4]) * g[p]
        shear = fl(e["shear"]) * (pair[i] - pair[j])
        u, w = parts[p]
        out[i], out[i + 1] = even + shear + (u + w), even + shear - (u + w)
        out[j], out[j + 1] = even - shear + (u - w), even - shear - (u - w)
    return out


def force_part(density, momentum, force, inverse, wanted):
    k = FORCE
    j = [momentum[a] + 0.5 * force[a] for a in range(3)]
    u = [j[a] * inverse for a in range(3)]
    aa = [j[a] * u[a] for a in range(3)]
    bb = [2.0 * (u[a] * force[a]) for a in range(3)]
    ta, tb = aa[0] + aa[1] + aa[2], bb[0] + bb[1] + bb[2]
    out = {}
    if 0 in wanted:
        out[0] = fl(k["rest"][0]) * ta + fl(k["rest"][1]) * tb + fl(k["rest"][2]) * density
    axis_common = fl(k["axis_trace"][0]) * ta + fl(k["axis_trace"][1]) * tb + fl(k["axis_trace"][2]) * density
    plane_common = fl(k["plane_trace"][0]) * ta + fl(k["plane_trace"][1]) * tb + fl(k["plane_trace"][2]) * density
    odd_plane = [fl(k["odd_plane"][0]) * j[a] + fl(k["odd_plane"][1]) * force[a] for a in range(3)]
    for a in range(3):
        ids = (1 + 2 * a, 2 + 2 * a)
        if not any(i in wanted for i in ids):
            continue
        even = axis_common + fl(k["axis"][0]) * aa[a] + fl(k["axis"][1]) * bb[a]
        odd = fl(k["odd_axis"][0]) * j[a] + fl(k["odd_axis"][1]) * force[a]
        if ids[0] in wanted:
            out[ids[0]] = even + odd
        if ids[1] in wanted:
            out[ids[1]] = even - odd
    for p in range(3):
        i1, i2, a, b = PLANES[p]
        if not any(i in wanted for i in (i1, i1 + 1, i2, i2 + 1)):
            continue
        even = plane_common + fl(k["plane"][0]) * aa[p] + fl(k["plane"][1]) * bb[p]
        shear = fl(k["shear"][0]) * (j[a] * u[b]) + fl(k["shear"][1]) * (u[a] * force[b] + u[b] * force[a])
        up, down = even + shear, even - shear
        total, apart = odd_plane[a] + odd_plane[b], odd_plane[a] - odd_plane[b]
        for i, v in ((i1, (up, total)), (i2, (down, apart))):
            if i in wanted:
                out[i] = v[0] + v[1]
            if i + 1 in wanted:
                out[i + 1] = v[0] - v[1]
    return out


def cas(rows, columns, length):
    angle = 2 * np.pi * (np.outer(rows, columns) % length) / length
    return (np.cos(angle) + np.sin(angle)).astype(np.float32)


def eigen(length):
    return 2.0 - 2.0 * np.cos(2 * np.pi * np.arange(length) / length)


def tables(nx, ny, nz):
    r = np.array([x * 4 + zl for zl in range(4) for x in range(4)])
    own_rows = np.concatenate([4 * r + xi for xi in range(4)])
    ext_rows = np.concatenate([4 * r + xx for xx in range(-1, 5)])
    c = np.arange(16)
    low = np.stack([16 * c - 1] * 6 + [16 * c - 2] * 2, axis=1).reshape(-1)
    high = np.stack([16 * c + 16] * 6 + [16 * c + 17] * 2, axis=1).reshape(-1)
    return {
        "hz": cas(np.arange(nz), np.arange(nz), nz),
        "hx": cas(np.arange(nx), own_rows % nx, nx),
        "hx_ext": cas(ext_rows % nx, np.arange(nx), nx),
        "hy_ext": cas(np.arange(ny), np.concatenate([np.arange(ny), low % ny, high % ny]), ny),
        "eig_xy": (eigen(nx)[:, None] + eigen(ny)[None, :] + SCREEN).astype(np.float32),
        "eig_z": np.broadcast_to(eigen(nz).astype(np.float32)[:, None], (nz, 128)).copy(),
    }


def near(d):
    return min(d, 4 - d)


STEPS = sorted(
    [(dx, dy, dk) for dx in range(4) for dy in range(4) for dk in range(2)],
    key=lambda t: -(near(t[0]) + near(t[1])) * 10 - t[2],
)


def dot(a, b, contract=((1,), (0,))):
    return lax.dot_general(a, b, (contract, ((), ())), precision=HIGHEST, preferred_element_type=f32)


def solve_kernel(
    pops_hbm, conc_hbm, solid_hbm, sites_hbm, hz_hbm, hx_hbm, hxe_hbm, hye_hbm, exy_hbm, ez_hbm,
    pot_ref, field, xr, yr,
    hz_ref, hx_ref, hxe_ref, hye_ref, exy_ref, ez_ref,
    pops, conc, solid, sites, sa, ra, rb, grid, sp, rp, ys, yin, cs, cin, sems, side_sems, in_sems,
):
    row, col = lax.axis_index("row"), lax.axis_index("col")
    x, zl = row // 4, lax.rem(row, 4)
    zh, y, k = col // 8, lax.rem(col // 2, 4), lax.rem(col, 2)
    z = zh * 4 + zl
    plane = y * 4 + x
    depth = z * 2 + k
    mode = depth * 16 + plane

    loads = [
        pltpu.make_async_copy(conc_hbm, conc, in_sems.at[0]),
        pltpu.make_async_copy(solid_hbm, solid, in_sems.at[1]),
        pltpu.make_async_copy(sites_hbm, sites, in_sems.at[2]),
        pltpu.make_async_copy(hz_hbm, hz_ref, in_sems.at[5]),
        pltpu.make_async_copy(pops_hbm, pops, in_sems.at[3]),
        pltpu.make_async_copy(exy_hbm, exy_ref, in_sems.at[6]),
        pltpu.make_async_copy(ez_hbm, ez_ref, in_sems.at[7]),
        pltpu.make_async_copy(hx_hbm, hx_ref, in_sems.at[8]),
        pltpu.make_async_copy(hxe_hbm, hxe_ref, in_sems.at[9]),
        pltpu.make_async_copy(hye_hbm, hye_ref, in_sems.at[10]),
    ]

    barrier = pltpu.get_barrier_semaphore()
    xs = [lax.rem(x + d, 4) for d in range(4)]
    yy = [lax.rem(y + d, 4) for d in range(4)]
    plane_peers = [(dx, dy) for dx in range(4) for dy in range(4) if (dx, dy) != (0, 0)]
    plane_peers.sort(key=lambda t: -(near(t[0]) + near(t[1])))
    depth_peers = [(dz, dk) for dz in (4, 3, 5, 2, 6, 1, 7, 0) for dk in (1, 0) if (dz, dk) != (0, 0)]
    row_up, row_down = lax.rem(row + 1, 16), lax.rem(row + 15, 16)
    col_up, col_down = lax.rem(col + 1, 16), lax.rem(col + 15, 16)

    def plane_id(dx, dy):
        return {"row": xs[dx] * 4 + zl, "col": zh * 8 + yy[dy] * 2 + k}

    def depth_pos(dz, dk):
        return lax.rem(z + dz, 8), (k if dk == 0 else 1 - k)

    def depth_id(dz, dk):
        zz, kk = depth_pos(dz, dk)
        return {"row": x * 4 + lax.rem(zz, 4), "col": (zz // 4) * 8 + y * 2 + kk}

    ids = [depth_id(*t) for t in depth_peers] + [plane_id(*t) for t in plane_peers]
    ids += [{"row": row_up, "col": col}, {"row": row_down, "col": col}, {"row": row, "col": col_up}, {"row": row, "col": col_down}]
    corner_ids = [{"row": r, "col": c} for c in (col_up, col_down) for r in (row_up, row_down)]
    ids += corner_ids
    for device in ids:
        pl.semaphore_signal(barrier, inc=1, device_id=device, device_id_type=MESH)
    for c in loads:
        c.start()

    for c in loads[:4]:
        c.wait()
    open_all = 1.0 - solid[...].astype(f32)
    kinds = sites[...]
    fixed = SITE_CHARGE * ((kinds == 1).astype(f32) - (kinds == 2).astype(f32))
    charge = (conc[0] - conc[1]) * open_all + fixed
    field[AUX + 4] = conc[0]
    field[AUX + 5] = conc[1]
    field[AUX + 6] = open_all
    field[AUX + 7] = charge
    flat = charge.reshape(64, 256)
    halves = hz_ref[...].reshape(16, 2, 8, 256)
    empty = jnp.zeros((64, 256), f32)
    spectrum = dot(halves[:, 0].reshape(128, 256), jnp.concatenate([flat, empty], axis=0), ((1,), (1,)))
    spectrum += dot(halves[:, 1].reshape(128, 256), jnp.concatenate([empty, flat], axis=0), ((1,), (1,)))
    sa.reshape(128, 128)[...] = spectrum

    pl.semaphore_wait(barrier, len(ids))
    for t in depth_peers:
        zz, kk = depth_pos(*t)
        pltpu.make_async_remote_copy(
            sa.at[pl.ds((zz * 2 + kk) * 8, 8)], ra.at[zh, k, zl], sems.at[0], sems.at[1], device_id=depth_id(*t), device_id_type=MESH
        ).start()
    keep = pltpu.make_async_copy(sa.at[pl.ds(depth * 8, 8)], ra.at[zh, k, zl], in_sems.at[4])
    keep.start()

    def to_side(n, source, target, device):
        return pltpu.make_async_remote_copy(
            source, target, side_sems.at[2 * n], side_sems.at[2 * n + 1], device_id=device, device_id_type=MESH
        )

    up, down = {"row": row_up, "col": col}, {"row": row_down, "col": col}
    sides = [
        to_side(0, field.at[pl.ds(AUX + 4, 4), 3], xr.at[0, pl.ds(4, 4)], up),
        to_side(1, field.at[pl.ds(AUX + 4, 4), 0], xr.at[1, pl.ds(AUX + 4, 4)], down),
        to_side(2, field.at[pl.ds(AUX, 4), 3], xr.at[0, pl.ds(0, 4)], up),
        to_side(3, field.at[pl.ds(AUX, 4), 0], xr.at[1, pl.ds(AUX, 4)], down),
    ]
    for c in loads[4:]:
        c.wait()

    def before(i, carry):
        xx, part = lax.rem(3 * (i // 2), 4), pl.multiple_of(lax.rem(i, 2) * 8, 8)
        rows = pl.ds(part, 8)
        f = [pops[d, xx, rows, :] for d in range(19)]
        moments = moments_of(f)
        field[AUX, xx, rows, :] = moments[5]
        for a in range(3):
            field[AUX + 1 + a, xx, rows, :] = moments[8][a]
        wall = solid[xx, rows, :] == 1
        base = relaxed(f, moments)
        for d in range(19):
            field[SLOT[d], xx, rows, :] = jnp.where(wall, f[OPPOSITE[d]], base[d])
        return carry

    lax.fori_loop(0, 4, before, 0)
    late = [
        to_side(8, field.at[pl.ds(SLOT[1], 5), 3], xr.at[0, pl.ds(N_AUX, 5)], up),
        to_side(9, field.at[pl.ds(SLOT[2], 5), 0], xr.at[1, pl.ds(0, 5)], down),
    ]
    lax.fori_loop(4, 8, before, 0)
    line4 = lax.broadcasted_iota(jnp.int32, (4, 256), 0)
    for side, (edge, dirs) in enumerate(((15, Y_LOW), (0, Y_HIGH))):
        for n in range(N_SEND):
            slot = SLOT[dirs[n]] if n < 5 else AUX + n - 5
            value = field[slot, 3, edge : edge + 1, :]
            for xx in range(3):
                value = jnp.where(line4 == xx, field[slot, xx, edge : edge + 1, :], value)
            ys[side, n] = value
        for end, (xx, d) in enumerate(((3, dirs[0]), (0, dirs[1]))):
            for n in range(N_AUX):
                cs[2 * side + end, n : n + 1, :] = field[AUX + n, xx, edge : edge + 1, :]
            for n in range(N_AUX, 16):
                cs[2 * side + end, n : n + 1, :] = field[SLOT[d], xx, edge : edge + 1, :]
    sides += [to_side(10, ys.at[0], yin.at[0], {"row": row, "col": col_up}), to_side(11, ys.at[1], yin.at[1], {"row": row, "col": col_down})]
    sides += [to_side(4 + n, cs.at[n], cin.at[n], corner_ids[n]) for n in range(4)]
    for c in sides[4:]:
        c.start()

    keep.wait()
    blocks, packed = sp.at[pl.ds(0, 240)], sa.at[pl.ds(0, 120)]
    pltpu.make_async_copy(packed, packed, sems.at[1]).wait()
    for t in plane_peers:
        other = yy[t[1]] * 4 + xs[t[0]]
        pltpu.make_async_remote_copy(
            ra.at[:, :, :, lax.rem(other, 8)], rb.at[:, y, :, :, x], sems.at[6], sems.at[7], device_id=plane_id(*t), device_id_type=MESH
        ).start()
    keep = pltpu.make_async_copy(ra.at[:, :, :, lax.rem(plane, 8)], rb.at[:, y, :, :, x], in_sems.at[4])
    keep.start()

    for c in sides[:2]:
        c.start()
    for c in sides[2:4]:
        c.start()
    sides += late
    scale = 1.0 / ((exy_ref[...] + jnp.concatenate([ez_ref[pl.ds(mode, 1), :]] * 2, axis=1)) * float(64 * 256 * 256))
    keep.wait()
    pltpu.make_async_copy(blocks, blocks, sems.at[7]).wait()

    lane = lax.broadcasted_iota(jnp.int32, (16, 128), 1)
    sixteenth = lane // 16
    eighth = lane // 8
    in_eighth = lax.rem(lane, 8)
    arrived = rb.reshape(256, 128)
    upper = jnp.broadcast_to(plane, (16, 128)) >= 8
    for half in range(2):
        pieces = [arrived[(8 * half + j) * 16 : (8 * half + j + 1) * 16, :] for j in range(8)]
        pieces = [jnp.where(upper, pltpu.roll(v, 64, 1), v) for v in pieces]
        for xi in range(4):
            acc = None
            for j in range(8):
                shift = (j - xi) * 16 % 128
                w = pltpu.roll(pieces[j], shift, 1) if shift else pieces[j]
                acc = w if acc is None else jnp.where(sixteenth == j, w, acc)
            grid[xi * 16 : (xi + 1) * 16, half * 128 : (half + 1) * 128] = acc
    g = dot(dot(hx_ref[...], grid[...]), hz_ref[...]) * scale
    out = dot(dot(hxe_ref[...], g), hye_ref[...])
    rims = []
    for base in (256, 384):
        merged = out[0:16, base : base + 128]
        for j in range(1, 8):
            r = {6: 0, 7: 5}.get(j, j)
            merged = jnp.where(in_eighth == j, out[r * 16 : (r + 1) * 16, base : base + 128], merged)
        rims.append(merged)
    send = sp.reshape(256, 128)
    for c in range(16):
        acc = None
        for xx in range(6):
            v = out[xx * 16 : (xx + 1) * 16, (c // 8) * 128 : (c // 8 + 1) * 128]
            shift = (xx - c % 8) * 16 % 128
            w = pltpu.roll(v, shift, 1) if shift else v
            acc = w if acc is None else jnp.where(sixteenth == xx, w, acc)
        for s in range(2):
            shift = (96 + 8 * s - 8 * c) % 128
            w = pltpu.roll(rims[s], shift, 1) if shift else rims[s]
            acc = jnp.where(eighth == 12 + s, w, acc)
        send[c * 16 : (c + 1) * 16, :] = acc

    ks = [k, 1 - k]

    def to_all(i, last):
        dz = 4 + (1 - 2 * lax.rem(i, 2)) * ((i + 1) // 2)
        zz = lax.rem(z + dz, 8)
        zr, zc = lax.rem(zz, 4), (zz // 4) * 8
        for dx, dy, dk in STEPS:
            if last and (dx, dy, dk) == (0, 0, 0):
                continue
            c = zc + yy[dy] * 2 + ks[dk]
            pltpu.make_async_remote_copy(
                sp.at[c * 16 + zr * 4 + xs[dx]], rp.at[mode], sems.at[12], sems.at[13],
                device_id={"row": xs[dx] * 4 + zr, "col": c}, device_id_type=MESH,
            ).start()

    def step(i, carry):
        to_all(i, False)
        return carry

    keep = pltpu.make_async_copy(sp.at[col * 16 + zl * 4 + x], rp.at[mode], in_sems.at[4])
    keep.start()
    lax.fori_loop(0, 7, step, 0)
    to_all(7, True)
    for c in late:
        c.start()
    for c in sides[4:10]:
        c.wait_recv()
    line = lax.broadcasted_iota(jnp.int32, (8, 256), 0)
    for side in range(2):
        for n in range(N_SEND):
            value = jnp.zeros((8, 256), f32)
            for xx in range(4):
                value = jnp.where(line == xx + 1, yin[side, n, xx : xx + 1, :], value)
            for end in range(2):
                if n >= 5 or n == end:
                    at = n - 5 if n >= 5 else N_AUX
                    value = jnp.where(line == 5 * end, cin[2 * side + end, at : at + 1, :], value)
            yr[side, n] = value
    keep.wait()
    most = rp.at[pl.ds(0, 255)]
    pltpu.make_async_copy(most, most, sems.at[13]).wait()
    pot_ref[...] = dot(rp.reshape(256, 128)[...], hz_ref[...], ((0,), (0,)))

    for c in sides[:4] + sides[10:]:
        c.wait_recv()
    pltpu.make_async_copy(packed, packed, sems.at[0]).wait()
    pltpu.make_async_copy(blocks, blocks, sems.at[6]).wait()
    pltpu.make_async_copy(most, most, sems.at[12]).wait()
    for c in sides:
        c.wait_send()


def solve(populations, concentrations, solid_mask, charge_sites):
    t = tables(64, 256, 256)
    vmem = pl.BlockSpec(memory_space=pltpu.VMEM)
    hbm = pl.BlockSpec(memory_space=pltpu.HBM)
    return pl.pallas_call(
        solve_kernel,
        out_shape=(
            jax.ShapeDtypeStruct((128, 256), f32),
            jax.ShapeDtypeStruct((N_FIELD, 4, 16, 256), f32),
            jax.ShapeDtypeStruct((2, N_SEND, 16, 256), f32),
            jax.ShapeDtypeStruct((2, N_SEND, 8, 256), f32),
        ),
        in_specs=[hbm] * 10,
        out_specs=(vmem,) * 4,
        scratch_shapes=[
            *[pltpu.VMEM(t[n].shape, f32) for n in TABLES],
            pltpu.VMEM((19, 4, 16, 256), f32),
            pltpu.VMEM((2, 4, 16, 256), f32),
            pltpu.VMEM((4, 16, 256), jnp.int32),
            pltpu.VMEM((4, 16, 256), jnp.int32),
            pltpu.VMEM((128, 1, 128), f32),
            pltpu.VMEM((2, 2, 4, 8, 1, 128), f32),
            pltpu.VMEM((2, 4, 2, 4, 4, 1, 128), f32),
            pltpu.VMEM((64, 256), f32),
            pltpu.VMEM((256, 1, 128), f32),
            pltpu.VMEM((256, 1, 128), f32),
            pltpu.VMEM((2, N_SEND, 4, 256), f32),
            pltpu.VMEM((2, N_SEND, 4, 256), f32),
            pltpu.VMEM((4, 16, 256), f32),
            pltpu.VMEM((4, 16, 256), f32),
            pltpu.SemaphoreType.DMA((14,)),
            pltpu.SemaphoreType.DMA((24,)),
            pltpu.SemaphoreType.DMA((11,)),
        ],
        compiler_params=pltpu.CompilerParams(collective_id=0, has_side_effects=True, vmem_limit_bytes=VMEM_A),
    )(
        *[
            pltpu.with_memory_space_constraint(v, pltpu.HBM)
            for v in (populations, concentrations, solid_mask, charge_sites, *[jnp.asarray(t[n]) for n in TABLES])
        ],
    )


TABLES = ("hz", "hx", "hx_ext", "hy_ext", "eig_xy", "eig_z")
VMEM_A = 32 * 2**20
VMEM_B = 24 * 2**20


def roll_z(v, shift):
    return pltpu.roll(v, shift % 256, 1)


def step_kernel(pot, field, xr, yr, out_hbm, conc_hbm, out, conc_out, sems):
    line16 = lax.broadcasted_iota(jnp.int32, (16, 256), 0)
    line8 = lax.broadcasted_iota(jnp.int32, (8, 256), 0)

    def up_y(v, beyond):
        return jnp.where(line16 == 15, beyond, pltpu.roll(v, 15, 0))

    def down_y(v, beyond):
        return jnp.where(line16 == 0, beyond, pltpu.roll(v, 1, 0))

    def forces(aux, electric):
        rho, mx, my, mz, c0, c1, opening = aux[:7]
        charge = -0.5 * ((c0 - c1) * opening)
        return rho * opening, [mx * opening, my * opening, mz * opening], [charge * e for e in electric], 1.0 / rho

    y_cells = []
    for side, dirs in enumerate((Y_LOW, Y_HIGH)):
        p = pot[96 + 8 * side : 104 + 8 * side, :]
        inner = jnp.zeros((8, 256), f32)
        for n in range(6):
            inner = jnp.where(line8 == n, pot[n * 16 + 15 * side : n * 16 + 15 * side + 1, :], inner)
        aux = [yr[side, 5 + n] for n in range(N_AUX)]
        left, right = pltpu.roll(p, 1, 0), pltpu.roll(p, 7, 0)
        front, back = roll_z(p, -1), roll_z(p, 1)
        rest = (6.0 + SCREEN) * p - aux[7] - inner - front - back
        given = jnp.where(line8 == 0, p[6:7, :], p[7:8, :])
        corner = (line8 == 0) | (line8 == 5)
        outer = jnp.where(corner, given, rest - left - right)
        left_all = jnp.where(line8 == 0, rest - right - outer, left)
        right_all = jnp.where(line8 == 5, rest - left - outer, right)
        along_y = inner - outer if side == 0 else outer - inner
        rho, m, force, inverse = forces(aux, (right_all - left_all, along_y, front - back))
        part = force_part(rho, m, force, inverse, dirs)
        moved = {d: roll_z(yr[side, n] + part[d], int(VELOCITY[d, 2])) for n, d in enumerate(dirs)}
        speed = aux[2] / aux[0]
        y_cells.append((p, moved, aux[4], aux[5], speed))

    planes = [pot[n * 16 : (n + 1) * 16, :] for n in range(6)]
    p_below = y_cells[0][0]
    p_above = y_cells[1][0]

    def aux_of(s):
        if s == -1:
            return [xr[0, n] for n in range(N_AUX)]
        if s == 4:
            return [xr[1, AUX + n] for n in range(N_AUX)]
        return [field[AUX + n, s] for n in range(N_AUX)]

    def base_of(d, s):
        if s == -1:
            return xr[0, SLOT[d] - AUX]
        if s == 4:
            return xr[1, SLOT[d]]
        return field[SLOT[d], s]

    def face(low, high, n):
        total = low[n] + high[n]
        return 0.25 * (low[2] + high[2]) * total - DIFFUSIVITY[n] * (
            (high[n] - low[n]) + (VALENCE[n] * 0.5) * total * (high[3] - low[3])
        )

    copies = []
    before = None
    for s in range(-1, 5):
        p = planes[s + 1]
        y_up, y_down = up_y(p, p_above[s + 1 : s + 2, :]), down_y(p, p_below[s + 1 : s + 2, :])
        front, back = roll_z(p, -1), roll_z(p, 1)
        aux = aux_of(s)
        if s == -1:
            right = planes[1]
            left = (6.0 + SCREEN) * p - aux[7] - right - y_up - y_down - front - back
            dirs = PLUS_X
        elif s == 4:
            left = planes[4]
            right = (6.0 + SCREEN) * p - aux[7] - left - y_up - y_down - front - back
            dirs = MINUS_X
        else:
            left, right = planes[s], planes[s + 2]
            dirs = [d for d in range(19) if 0 <= s + VELOCITY[d, 0] <= 3]
        rho, m, force, inverse = forces(aux, (right - left, y_up - y_down, front - back))
        part = force_part(rho, m, force, inverse, dirs)
        for d in dirs:
            cx, cy, cz = (int(n) for n in VELOCITY[d])
            v = base_of(d, s) + part[d]
            if cz:
                v = roll_z(v, cz)
            if cy == 1:
                v = down_y(v, y_cells[0][1][d][s + 1 : s + 2, :])
            elif cy == -1:
                v = up_y(v, y_cells[1][1][d][s + 1 : s + 2, :])
            out[d, s + cx] = v
        here_x = (aux[4], aux[5], aux[1] * inverse, p)
        if s >= 0:
            x_flux = [face(before[0], here_x, n) for n in range(2)]
            if s > 0:
                for n in range(2):
                    conc_out[n, s - 1] = before[1] * (before[2][n] - x_flux[n])
            if s < 4:
                uy, uz = aux[2] * inverse, aux[3] * inverse
                row = slice(s + 1, s + 2)
                here_y = (aux[4], aux[5], uy, p)
                below = tuple(down_y(v, y_cells[0][i][row, :]) for v, i in ((aux[4], 2), (aux[5], 3), (uy, 4))) + (y_down,)
                above = tuple(up_y(v, y_cells[1][i][row, :]) for v, i in ((aux[4], 2), (aux[5], 3), (uy, 4))) + (y_up,)
                here_z = (aux[4], aux[5], uz, p)
                ahead = tuple(roll_z(v, -1) for v in here_z[:3]) + (front,)
                rest = []
                for n in range(2):
                    z_flux = face(here_z, ahead, n)
                    change = face(here_y, above, n) - face(below, here_y, n) + (z_flux - roll_z(z_flux, 1))
                    rest.append(aux[4 + n] - change + x_flux[n])
                before = (here_x, aux[6], rest)
        else:
            before = (here_x,)
        if s >= 1:
            copies.append(pltpu.make_async_copy(out.at[:, s - 1], out_hbm.at[:, s - 1], sems.at[s - 1]))
            copies[-1].start()
    copies.append(pltpu.make_async_copy(conc_out, conc_hbm, sems.at[4]))
    copies[-1].start()
    for c in copies:
        c.wait()


def finish(pot, field, xr, yr):
    vmem = pl.BlockSpec(memory_space=pltpu.VMEM)
    hbm = pl.BlockSpec(memory_space=pl.ANY)
    return pl.pallas_call(
        step_kernel,
        out_shape=(jax.ShapeDtypeStruct((19, 4, 16, 256), f32), jax.ShapeDtypeStruct((2, 4, 16, 256), f32)),
        in_specs=[vmem] * 4,
        out_specs=(hbm, hbm),
        scratch_shapes=[
            pltpu.VMEM((19, 4, 16, 256), f32),
            pltpu.VMEM((2, 4, 16, 256), f32),
            pltpu.SemaphoreType.DMA((5,)),
        ],
        compiler_params=pltpu.CompilerParams(vmem_limit_bytes=VMEM_B),
    )(pot, field, xr, yr)


def per_device(populations, concentrations, solid_mask, charge_sites):
    return finish(*solve(populations, concentrations, solid_mask, charge_sites))


def solution(mesh):
    placed = (P(None, "row", "col", None), P(None, "row", "col", None), P("row", "col", None), P("row", "col", None))
    return jax.shard_map(
        per_device, mesh=mesh, in_specs=placed, out_specs=(P(None, "row", "col", None),) * 2, check_vma=False
    )
```
